128 devices in a mesh: ctx: 32 (over z_lo, x, y), tp: 4 (over z_hi, core).
Axes of the slice: x: 4, y: 4, z: 4 (z_hi: 2, z_lo: 2; z = z_hi * 2 + z_lo), core: 2. Of those that a mesh axis runs over, the one named last changes fastest.
Arguments:
- new_queries: bfloat16 [2048, 8192], P('ctx', 'tp'), may hold values from -24 to 24
- new_keys: bfloat16 [2048, 512], P('ctx', 'tp'), may hold values from -6 to 6
- new_values: bfloat16 [2048, 512], P('ctx', 'tp'), may hold values from -6 to 6
- cache_keys: bfloat16 [32768, 512], P('ctx', 'tp'), may hold values from -24 to 24
- cache_values: bfloat16 [32768, 512], P('ctx', 'tp'), may hold values from -6 to 6
- out_weight: bfloat16 [8192, 16384], P('tp', 'ctx'), may hold values from -0.0625 to 0.0625
- cache_docs: int32 [256], replicated, may hold values from 0 to 3
- new_docs: int32 [16], replicated, may hold values from 0 to 3
- slot_tile: int32 [32], replicated, may hold values from 0 to 31, each once
Outputs:
- projected: bfloat16 [2048, 16384], P('tp', 'ctx')
The draws below stay inside these ranges and needn't reach their ends.
Inputs may be any that keep to these rules, and one draw needn't show every extreme that they name: `slot_tile`: each number once.
All inputs are finite; a program needn't handle non-finite values.
Results may differ from the reference program's by a relative error of at most 0.02.
Values may be sent and summed in bfloat16 or wider, within the bound.
A program may use at most 64 MiB of HBM per device.

```python
import math
import jax
import jax.numpy as jnp
import numpy as np
from jax import lax

D = 16384
QH = 64
KVH = 4
HD = 128
BLK = 128
NDOC = 4
CACHE = 32768
NEW = 2048
N_CTX = 32


def draw_new_queries(key, part):
    key = jax.random.fold_in(key, 1)
    values = jnp.clip(jax.random.normal(key, (NEW, QH, HD), jnp.float32), -6.0, 6.0)
    return values.reshape(NEW, QH * HD).astype(jnp.bfloat16)


def draw_cache_keys(key, part):
    key = jax.random.fold_in(key, 2)
    values = jnp.clip(jax.random.normal(key, (CACHE, KVH, HD), jnp.float32), -6.0, 6.0)
    return values.reshape(CACHE, KVH * HD).astype(jnp.bfloat16)


def set_ends(drawn, own_key, low, high):
    longest = drawn.shape.index(max(drawn.shape))
    spots = []
    for shift in (0, 1):
        where = [jax.random.randint(jax.random.fold_in(own_key, axis), (), 0, length) for axis, length in enumerate(drawn.shape)]
        where[longest] = (where[longest] + shift) % drawn.shape[longest]
        spots.append(tuple(where))
    return drawn.at[spots[0]].set(low).at[spots[1]].set(high)


def levels(own_key, shape, shards, smallest, top_value):
    gain = 1.0
    for axis_at, shards_of in shards:
        steps = jax.random.uniform(jax.random.fold_in(jax.random.fold_in(own_key, 6), axis_at), (shards_of,), jnp.float32, smallest / len(shards), top_value / len(shards))
        gain = gain * jnp.repeat(jnp.exp(steps), shape[axis_at] // shards_of).reshape((-1,) + (1,) * (len(shape) - 1 - axis_at))
    return gain


def cumulative_ranks(amount, lean):
    loads = [(1 << 20) // math.isqrt(rank ** lean) + 1 for rank in range(1, amount + 1)]
    width = 1 + sum(loads) // (1 << 30)
    return np.cumsum(np.array([max(1, weight // width) for weight in loads]))


def skewed_ids(stream_key, extent, number_of, lean):
    grid = cumulative_ranks(number_of, lean)
    ticket = jax.random.randint(jax.random.fold_in(stream_key, 1), extent, 0, int(grid[number_of - 1]))
    standing = jnp.searchsorted(jnp.asarray(grid, jnp.int32), ticket, side="right")
    return jax.random.permutation(jax.random.fold_in(stream_key, 2), number_of)[standing].astype(jnp.int32)


def scatter_about(stream_key, extent, width, limit, shards=(), kind=jnp.bfloat16):
    values = jax.random.normal(stream_key, extent, jnp.float32) * width
    if len(shards) > 0:
        values = levels(stream_key, extent, shards, -0.22, 0.18) * values
    return jnp.clip(values, min=-limit, max=limit).astype(kind)


def setup_inputs(seed: int = 0) -> dict:
    arg_keys = jax.random.split(jax.random.key(seed), 10)
    new_queries = draw_new_queries(jax.random.fold_in(arg_keys[9], 71), 0)
    new_keys = scatter_about(arg_keys[1], (NEW, KVH * HD), 1.0, 6.0, ((0, 32), (1, 4)))
    new_values = scatter_about(arg_keys[2], (NEW, KVH * HD), 1.0, 6.0, ((0, 32), (1, 4)))
    cache_keys = draw_cache_keys(jax.random.fold_in(arg_keys[9], 71), 0)
    cache_values = scatter_about(arg_keys[4], (CACHE, KVH * HD), 1.0, 6.0, ((0, 32), (1, 4)))
    out_weight = scatter_about(arg_keys[5], (QH * HD, D), (QH * HD) ** -0.5, 0.0625, ((0, 4), (1, 32)))
    cache_docs = set_ends(skewed_ids(arg_keys[6], (CACHE // BLK,), NDOC, 2), jax.random.fold_in(arg_keys[6], 3), 0, NDOC - 1).astype(jnp.int32)
    new_docs = set_ends(jax.random.randint(arg_keys[7], (NEW // BLK,), 0, NDOC), jax.random.fold_in(arg_keys[7], 1), 0, NDOC - 1).astype(jnp.int32)
    slot_tile = jax.random.permutation(arg_keys[8], N_CTX).astype(jnp.int32)
    return {"new_queries": new_queries, "new_keys": new_keys, "new_values": new_values, "cache_keys": cache_keys, "cache_values": cache_values, "out_weight": out_weight, "cache_docs": cache_docs, "new_docs": new_docs, "slot_tile": slot_tile}


NEGATIVE = -1.0e30


def reference(new_queries, new_keys, new_values, cache_keys, cache_values, out_weight, cache_docs, new_docs, slot_tile):
    query_rows = NEW // N_CTX
    cache_rows = CACHE // N_CTX
    group_size = QH // KVH
    row_index = jnp.arange(NEW, dtype=jnp.int32)
    query_position = slot_tile[row_index // query_rows] * query_rows + row_index % query_rows
    query_doc = new_docs[query_position // BLK]
    grouped = new_queries.astype(jnp.float32).reshape(NEW, KVH, group_size, HD)

    def visit(running, source):
        largest, normalizer, weighted = running
        cache_index = source * cache_rows + jnp.arange(cache_rows, dtype=jnp.int32)
        new_index = slot_tile[source] * query_rows + jnp.arange(query_rows, dtype=jnp.int32)
        key_position = jnp.concatenate([jnp.full((cache_rows,), -1, jnp.int32), new_index])
        key_doc = jnp.concatenate([cache_docs[cache_index // BLK], new_docs[new_index // BLK]])
        key_rows = jnp.concatenate([
            lax.dynamic_slice_in_dim(cache_keys, (source * cache_rows).astype(jnp.int32), cache_rows, 0),
            lax.dynamic_slice_in_dim(new_keys, (source * query_rows).astype(jnp.int32), query_rows, 0)], 0)
        value_rows = jnp.concatenate([
            lax.dynamic_slice_in_dim(cache_values, (source * cache_rows).astype(jnp.int32), cache_rows, 0),
            lax.dynamic_slice_in_dim(new_values, (source * query_rows).astype(jnp.int32), query_rows, 0)], 0)
        key_rows = key_rows.astype(jnp.float32).reshape(-1, KVH, HD)
        value_rows = value_rows.astype(jnp.float32).reshape(-1, KVH, HD)
        scores = jnp.einsum("rgjd,kgd->gjrk", grouped, key_rows) * (HD ** -0.5)
        allowed = (query_doc[:, None] == key_doc[None, :]) & (key_position[None, :] <= query_position[:, None])
        scores = jnp.where(allowed[None, None], scores, NEGATIVE)
        maxima = jnp.max(scores, axis=3)
        weights = jnp.exp(scores - maxima[..., None])
        totals = jnp.sum(weights, axis=3)
        rounded = lax.optimization_barrier(weights.astype(jnp.bfloat16)).astype(jnp.float32)
        mixture = jnp.einsum("gjrk,kgd->rgjd", rounded, value_rows)
        maxima_rows = jnp.transpose(maxima, (2, 0, 1)).reshape(NEW, QH)
        totals_rows = jnp.transpose(totals, (2, 0, 1)).reshape(NEW, QH)
        partial_value = (mixture / totals_rows.reshape(NEW, KVH, group_size)[..., None]).astype(jnp.bfloat16)
        partial_value = lax.optimization_barrier(partial_value).astype(jnp.float32).reshape(NEW, QH, HD)
        merged = jnp.maximum(largest, maxima_rows)
        rescale = jnp.exp(largest - merged)
        incoming = jnp.exp(maxima_rows - merged) * totals_rows
        weighted = weighted * rescale[..., None] + incoming[..., None] * partial_value
        return (merged, normalizer * rescale + incoming, weighted), None

    start = (jnp.full((NEW, QH), NEGATIVE, jnp.float32), jnp.zeros((NEW, QH), jnp.float32),
             jnp.zeros((NEW, QH, HD), jnp.float32))
    final, unused = lax.scan(visit, start, jnp.arange(N_CTX, dtype=jnp.int32))
    largest, normalizer, weighted = final
    attended = (weighted / normalizer[..., None]).astype(jnp.bfloat16).reshape(NEW, QH * HD)
    return jnp.dot(attended, out_weight, preferred_element_type=jnp.float32).astype(jnp.bfloat16)
```

```python
import functools
import jax, jax.numpy as jnp
from jax import lax
from jax.experimental import pallas as pl
from jax.experimental.pallas import tpu as pltpu
from jax.sharding import PartitionSpec as P

HD=128; BLK=128; NEG=-1e30
SCALE=HD**-0.5
L2E=1.4426950408889634
ROWS=64; HEADS=16; CR=1024; HALF=CR+ROWS; MEM=2*HALF
SUB=1024

def attn_kernel(cdocs, ndocs, tiles, place, q_ref, kv_ref, o_ref, st_ref, q_s, m_s, l_s, acc_s, lst, *, nb):
    g = pl.program_id(0)
    c = place[0]
    y = c % 4
    src = g * 4 + y
    members = [c - y + i for i in range(4)]
    tq = tiles[src]
    qd = ndocs[tq // 2]
    nrow = ROWS*HEADS
    for h in range(HEADS):
        q_s[h*ROWS:(h+1)*ROWS, :] = q_ref[0, :, h*HD:(h+1)*HD]
    m_s[...] = jnp.full_like(m_s, NEG)
    l_s[...] = jnp.zeros_like(l_s)
    acc_s[...] = jnp.zeros_like(acc_s)
    n = jnp.int32(0)
    for mi, c in enumerate(members):
        def add(b, n):
            ok = cdocs[c*8 + b] == qd
            lst[n] = mi*MEM + b*BLK
            return n + ok.astype(jnp.int32)
        n = lax.fori_loop(0, 8, add, n)

    def slow_step(kc, vc, mask_fn):
        for t in range(nrow//SUB):
            r = pl.ds(t*SUB, SUB)
            s = lax.dot_general(q_s[r, :], kc, (((1,),(1,)),((),())), preferred_element_type=jnp.float32)
            if mask_fn is not None:
                s = mask_fn(s)
            w = s.shape[1]//128
            mx = s[:, :128]
            for i in range(1, w):
                mx = jnp.maximum(mx, s[:, i*128:(i+1)*128])
            mx = jnp.max(mx, axis=1, keepdims=True)
            m_old = m_s[r, :]
            m_new = jnp.maximum(m_old, mx)
            alpha = jnp.exp2((m_old - m_new)*(SCALE*L2E))
            p = [jnp.exp2((s[:, i*128:(i+1)*128] - m_new)*(SCALE*L2E)) for i in range(w)]
            ps = p[0]
            for i in range(1, w):
                ps = ps + p[i]
            l_s[r, :] = l_s[r, :]*alpha + ps
            m_s[r, :] = m_new
            pb = jnp.concatenate([x.astype(jnp.bfloat16) for x in p], axis=1)
            acc_s[r, :] = acc_s[r, :]*alpha + jnp.dot(pb, vc, preferred_element_type=jnp.float32)


    def peak(kc, mask_fn):
        for t in range(nrow//SUB):
            r = pl.ds(t*SUB, SUB)
            s = lax.dot_general(q_s[r, :], kc, (((1,),(1,)),((),())), preferred_element_type=jnp.float32)
            if mask_fn is not None:
                s = mask_fn(s)
            w = s.shape[1]//128
            mx = s[:, :128]
            for i in range(1, w):
                mx = jnp.maximum(mx, s[:, i*128:(i+1)*128])
            m_s[r, :] = jnp.broadcast_to(jnp.max(mx, axis=1, keepdims=True), (SUB, 128))

    def step(kc, vc, mask_fn):
        for t in range(nrow//SUB):
            r = pl.ds(t*SUB, SUB)
            s = lax.dot_general(q_s[r, :], kc, (((1,),(1,)),((),())), preferred_element_type=jnp.float32)
            if mask_fn is not None:
                s = mask_fn(s)
            w = s.shape[1]//128
            m = m_s[r, :]
            p = [jnp.exp2((s[:, i*128:(i+1)*128] - m)*(SCALE*L2E)) for i in range(w)]
            ps = p[0]
            for i in range(1, w):
                ps = ps + p[i]
            l_s[r, :] = l_s[r, :] + ps
            pb = jnp.concatenate([x.astype(jnp.bfloat16) for x in p], axis=1)
            acc_s[r, :] = acc_s[r, :] + jnp.dot(pb, vc, preferred_element_type=jnp.float32)

    def at(off, rows=BLK):
        return kv_ref[pl.ds(pl.multiple_of(off, 64), rows), :]

    def chunks(step):
        def chunk(base, size):
            offs = [lst[base + j] for j in range(size)]
            kc = jnp.concatenate([at(o) for o in offs], axis=0)
            vc = jnp.concatenate([at(o + HALF) for o in offs], axis=0)
            step(kc, vc, None)
        def body(i, _):
            chunk(i*nb, nb)
            return 0
        lax.fori_loop(0, n // nb, body, 0)
        size = nb // 2
        while size >= 1:
            @pl.when((n // size) % 2 == 1)
            def _(size=size):
                chunk((n // (2*size))*(2*size), size)
            size //= 2
    kcs = []; vcs = []
    newlims = []
    for mi, c in enumerate(members):
        tk = tiles[c]
        same_doc = ndocs[tk // 2] == qd
        full_ok = same_doc & (tk < tq)
        diag = tk == tq
        newlims.append((jnp.where(full_ok, 1 << 20, jnp.where(diag, 0, -1)), jnp.where(diag, 1, 0)))
        kcs.append(kv_ref[mi*MEM + CR: mi*MEM + HALF, :])
        vcs.append(kv_ref[mi*MEM + HALF + CR: (mi+1)*MEM, :])
    kc = jnp.concatenate(kcs, axis=0); vc = jnp.concatenate(vcs, axis=0)
    any_new = functools.reduce(jnp.logical_or, [lim >= 0 for lim, _ in newlims])
    def mask(s):
        row = lax.broadcasted_iota(jnp.int32, (SUB, 128), 0) % ROWS
        lane = lax.broadcasted_iota(jnp.int32, (SUB, 128), 1)
        out = []
        for a in range(2):
            (b0, d0), (b1, d1) = newlims[2*a], newlims[2*a+1]
            lo = row*d0 + b0
            hi = row*d1 + b1
            ok = lane <= jnp.where(lane < ROWS, lo, hi + ROWS)
            k0 = a*128
            out.append(jnp.where(ok, s[:, k0:k0+128], NEG))
        return jnp.concatenate(out, axis=1)
    @pl.when(n > 0)
    def _():
        peak(at(lst[0]), None)
    @pl.when((n == 0) & any_new)
    def _():
        peak(kc, mask)
    chunks(step)
    @pl.when(any_new)
    def _():
        step(kc, vc, mask)
    @pl.when(jnp.logical_not(jnp.max(l_s[...]) < 1e30))
    def _():
        m_s[...] = jnp.full_like(m_s, NEG)
        l_s[...] = jnp.zeros_like(l_s)
        acc_s[...] = jnp.zeros_like(acc_s)
        chunks(slow_step)
        @pl.when(any_new)
        def _():
            slow_step(kc, vc, mask)
    lane = lax.broadcasted_iota(jnp.int32, (ROWS, 128), 1)
    st = jnp.full((ROWS, 128), NEG, jnp.float32)
    for h in range(HEADS):
        r = pl.ds(h*ROWS, ROWS)
        l = jnp.sum(l_s[r, :], axis=1, keepdims=True)
        l = jnp.maximum(l, 1e-30)
        o_ref[0, :, h*HD:(h+1)*HD] = (acc_s[r, :] / l).astype(jnp.bfloat16)
        lse = m_s[r, :]*SCALE + jnp.log(l)
        st = jnp.where(lane == h, lse, st)
    st_ref[0] = st

def attention(qg, kvg, cdocs, ndocs, tiles, place, nb=4):
    nrow = ROWS*HEADS
    return pl.pallas_call(
        functools.partial(attn_kernel, nb=nb),
        grid_spec=pltpu.PrefetchScalarGridSpec(
            num_scalar_prefetch=4, grid=(8,),
            in_specs=[pl.BlockSpec((1, ROWS, HEADS*HD), lambda g, *_: (g, 0, 0)),
                      pl.BlockSpec((4*MEM, HD), lambda g, *_: (0, 0))],
            out_specs=[pl.BlockSpec((1, ROWS, HEADS*HD), lambda g, *_: (g, 0, 0)),
                       pl.BlockSpec((1, ROWS, 128), lambda g, *_: (g, 0, 0))],
            scratch_shapes=[pltpu.VMEM((nrow, HD), jnp.bfloat16), pltpu.VMEM((nrow, 128), jnp.float32),
                            pltpu.VMEM((nrow, 128), jnp.float32), pltpu.VMEM((nrow, HD), jnp.float32),
                            pltpu.SMEM((40,), jnp.int32)]),
        out_shape=[jax.ShapeDtypeStruct((8, ROWS, HEADS*HD), jnp.bfloat16),
                   jax.ShapeDtypeStruct((8, ROWS, 128), jnp.float32)],
        compiler_params=pltpu.CompilerParams(vmem_limit_bytes=48 << 20),
        name="attention",
    )(cdocs, ndocs, tiles, place, qg, kvg)


MESH = pl.DeviceIdType.MESH


def coords():
    c = lax.axis_index("ctx")
    return c // 16, (c // 4) % 4, c % 4


def ctx_of(z, x, y):
    return z * 16 + x * 4 + y


def send(src, dst, sems, i, device):
    copy = pltpu.make_async_remote_copy(
        src_ref=src, dst_ref=dst, send_sem=sems[0].at[i], recv_sem=sems[1].at[i],
        device_id=device, device_id_type=MESH)
    copy.start()
    return copy


def arrive(ref, sems, i, device):
    pltpu.make_async_remote_copy(
        src_ref=ref, dst_ref=ref, send_sem=sems[0].at[i], recv_sem=sems[1].at[i],
        device_id=device, device_id_type=MESH).wait_recv()


def greet(peers):
    barrier = pltpu.get_barrier_semaphore()
    for device in peers:
        pl.semaphore_signal(barrier, inc=1, device_id=device, device_id_type=MESH)
    pl.semaphore_wait(barrier, len(peers))


def gather_kernel(q, ck, cv, nk, nv, qg, kvg, ssem, rsem, lsem):
    z, x, y = coords()
    sems = (ssem, rsem)
    zp = 1 - z
    xr, xl, yr, yl = (x + 1) % 4, (x + 3) % 4, (y + 1) % 4, (y + 3) % 4
    x2, y2 = (x + 2) % 4, (y + 2) % 4
    dev = lambda z, x, y: {"ctx": ctx_of(z, x, y)}
    to_yr, to_yl, to_xr, to_xl, to_z = dev(z, x, yr), dev(z, x, yl), dev(z, xr, y), dev(z, xl, y), dev(zp, x, y)
    greet([to_yr, to_yl, to_xr, to_xl, to_z])
    slot = lambda z, x: z * 4 + x
    me = slot(z, x)
    out = []
    out.append(send(q, qg.at[me], sems, 0, to_z))
    pieces = [(ck, 0, CR), (nk, CR, ROWS), (cv, HALF, CR), (nv, HALF + CR, ROWS)]
    for i in (0, 1, 2, 3):
        src, off, n = pieces[i]
        out.append(send(src, kvg.at[y, pl.ds(off, n)], sems, 1 + i, to_yr))
    for i in (2, 3, 0, 1):
        src, off, n = pieces[i]
        out.append(send(src, kvg.at[y, pl.ds(off, n)], sems, 5 + i, to_yl))
    out.append(send(q, qg.at[me], sems, 9, to_xr))
    out.append(send(q, qg.at[me], sems, 10, to_xl))
    locs = [pltpu.make_async_copy(q, qg.at[me], lsem.at[0])]
    for i, (src, off, n) in enumerate(pieces):
        locs.append(pltpu.make_async_copy(src, kvg.at[y, pl.ds(off, n)], lsem.at[1 + i]))
    for cp in locs:
        cp.start()
    other = slot(zp, x)
    arrive(qg.at[other], sems, 0, to_z)
    out.append(send(qg.at[other], qg.at[other], sems, 11, to_xr))
    out.append(send(qg.at[other], qg.at[other], sems, 12, to_xl))
    lo, hi = pl.ds(0, 32), pl.ds(32, 32)
    arrive(qg.at[slot(z, xl)], sems, 9, to_xl)
    out.append(send(qg.at[slot(z, xl), lo], qg.at[slot(z, xl), lo], sems, 13, to_xr))
    arrive(qg.at[slot(z, xr)], sems, 10, to_xr)
    out.append(send(qg.at[slot(z, xr), hi], qg.at[slot(z, xr), hi], sems, 14, to_xl))
    arrive(kvg.at[yl, pl.ds(0, CR)], sems, 1, to_yl)
    arrive(kvg.at[yl, pl.ds(CR, ROWS)], sems, 2, to_yl)
    kh, vh = pl.ds(0, HALF), pl.ds(HALF, HALF)
    out.append(send(kvg.at[yl, kh], kvg.at[yl, kh], sems, 17, to_yr))
    arrive(kvg.at[yr, pl.ds(HALF, CR)], sems, 7, to_yr)
    arrive(kvg.at[yr, pl.ds(HALF + CR, ROWS)], sems, 8, to_yr)
    out.append(send(kvg.at[yr, vh], kvg.at[yr, vh], sems, 18, to_yl))
    arrive(qg.at[slot(zp, xl)], sems, 11, to_xl)
    out.append(send(qg.at[slot(zp, xl), lo], qg.at[slot(zp, xl), lo], sems, 15, to_xr))
    arrive(qg.at[slot(zp, xr)], sems, 12, to_xr)
    out.append(send(qg.at[slot(zp, xr), hi], qg.at[slot(zp, xr), hi], sems, 16, to_xl))
    arrive(kvg.at[yl, pl.ds(HALF, CR)], sems, 3, to_yl)
    arrive(kvg.at[yl, pl.ds(HALF + CR, ROWS)], sems, 4, to_yl)
    arrive(kvg.at[yr, pl.ds(0, CR)], sems, 5, to_yr)
    arrive(kvg.at[yr, pl.ds(CR, ROWS)], sems, 6, to_yr)
    arrive(qg.at[slot(z, x2), lo], sems, 13, to_xl)
    arrive(qg.at[slot(z, x2), hi], sems, 14, to_xr)
    arrive(qg.at[slot(zp, x2), lo], sems, 15, to_xl)
    arrive(qg.at[slot(zp, x2), hi], sems, 16, to_xr)
    arrive(kvg.at[y2, kh], sems, 17, to_yl)
    arrive(kvg.at[y2, vh], sems, 18, to_yr)
    for cp in locs:
        cp.wait()
    for cp in out:
        cp.wait_send()


def gather(q, ck, cv, nk, nv):
    anywhere = pl.BlockSpec(memory_space=pl.ANY)
    return pl.pallas_call(
        gather_kernel,
        in_specs=[anywhere] * 5,
        out_specs=[anywhere] * 2,
        out_shape=[jax.ShapeDtypeStruct((8, ROWS, HEADS * HD), jnp.bfloat16),
                   jax.ShapeDtypeStruct((4, MEM, HD), jnp.bfloat16)],
        scratch_shapes=[pltpu.SemaphoreType.DMA((19,)), pltpu.SemaphoreType.DMA((19,)), pltpu.SemaphoreType.DMA((5,))],
        compiler_params=pltpu.CompilerParams(collective_id=0, has_side_effects=True),
        name="gather",
    )(q, ck, cv, nk, nv)


def project_kernel(o, st, w, wp, out, part, stp, attg, w_s, tx, rx, acc, zt, zr,
                   psem, qsem, gs, gr, cs, cr, zs, zrs, lsem):
    z, x, y = coords()
    t = lax.axis_index("tp")
    h, k = t // 2, t % 2
    dev = lambda z, x, y: {"ctx": ctx_of(z, x, y)}
    zdev = lambda b, zh: {"ctx": ctx_of(b, x, y), "tp": zh * 2 + k}
    zp = 1 - z
    xr, xl, yr, yl = (x + 1) % 4, (x + 3) % 4, (y + 1) % 4, (y + 3) % 4
    group = [(dz, dx) for dz in (0, 1) for dx in range(4) if (dz, dx) != (0, 0)]
    there = lambda dz, dx: ((z + dz) % 2, (x + dx) % 4)
    core = {"tp": h * 2 + 1 - k}
    to_yr, to_yl, to_xr, to_xl = dev(z, x, yr), dev(z, x, yl), dev(z, xr, y), dev(z, xl, y)
    greet([dev(*there(dz, dx), y) for dz, dx in group] + [to_yr, to_yl, core, zdev(0, 1 - h), zdev(1, 1 - h)])

    me = z * 4 + x
    outs = []
    order = sorted(group, key=lambda d: -(d[0] + (d[1] != 0) + (d[1] == 2)))
    for dz, dx in order:
        zz, xx = there(dz, dx)
        i = dz * 4 + dx
        outs.append(send(st.at[zz * 4 + xx], stp.at[me], (psem.at[1], qsem.at[1]), i, dev(zz, xx, y)))
        outs.append(send(o.at[zz * 4 + xx], part.at[me], (psem.at[0], qsem.at[0]), i, dev(zz, xx, y)))
    own = [pltpu.make_async_copy(o.at[me], part.at[me], lsem.at[0]),
           pltpu.make_async_copy(st.at[me], stp.at[me], lsem.at[1])]
    weights = [pltpu.make_async_copy(w, w_s.at[z], lsem.at[2]),
               pltpu.make_async_copy(wp, w_s.at[zp], lsem.at[3])]
    for cp in own + weights:
        cp.start()
    for cp in own:
        cp.wait()
    for dz, dx in order:
        zz, xx = (z + 2 - dz) % 2, (x + 4 - dx) % 4
        i = dz * 4 + dx
        arrive(stp.at[zz * 4 + xx], (psem.at[1], qsem.at[1]), i, dev(zz, xx, y))
        arrive(part.at[zz * 4 + xx], (psem.at[0], qsem.at[0]), i, dev(zz, xx, y))

    largest = stp[0]
    for c in range(1, 8):
        largest = jnp.maximum(largest, stp[c])
    e = [jnp.exp(stp[c] - largest) for c in range(8)]
    total = e[0]
    for c in range(1, 8):
        total = total + e[c]
    inverse = 1.0 / total
    e = [a * inverse for a in e]
    mine = x * 4 + y
    for head in range(HEADS):
        cols = pl.ds(head * HD, HD)
        a = jnp.zeros((ROWS, HD), jnp.float32)
        for c in range(8):
            a = a + e[c][:, head:head + 1] * part[c, :, cols].astype(jnp.float32)
        attg[head // 8, mine, :, (head % 8) * HD:(head % 8 + 1) * HD] = a.astype(jnp.bfloat16)

    lo, hi = pl.ds(0, 32), pl.ds(32, 32)
    slot = lambda x, y: x * 4 + y

    def block(hf, a, b):
        if hf == 0:
            return attg.at[0, slot((x + a) % 4, (y + b) % 4)]
        return attg.at[1, slot((x + b) % 4, (y + a) % 4)]

    def ways(hf, stage):
        return (to_xr, to_xl) if (hf == 0) == (stage == 0) else (to_yr, to_yl)

    def both(hf, stage, a, b, i):
        right, left = ways(hf, stage)
        ref = block(hf, a, b)
        outs.append(send(ref, ref, (gs.at[hf], gr.at[hf]), i, right))
        outs.append(send(ref, ref, (gs.at[hf], gr.at[hf]), i + 1, left))

    def relay(hf, stage, a, b, i):
        right, left = ways(hf, stage)
        d = (lambda n: (n, 0)) if stage == 0 else (lambda n: (a, n))
        ref = block(hf, *d(3))
        arrive(ref, (gs.at[hf], gr.at[hf]), i, left)
        outs.append(send(ref.at[lo], ref.at[lo], (gs.at[hf], gr.at[hf]), i + 2, right))
        ref = block(hf, *d(1))
        arrive(ref, (gs.at[hf], gr.at[hf]), i + 1, right)
        outs.append(send(ref.at[hi], ref.at[hi], (gs.at[hf], gr.at[hf]), i + 3, left))

    def last(hf, stage, a, b, i):
        right, left = ways(hf, stage)
        ref = block(hf, 2, 0) if stage == 0 else block(hf, a, 2)
        arrive(ref.at[lo], (gs.at[hf], gr.at[hf]), i + 2, left)
        arrive(ref.at[hi], (gs.at[hf], gr.at[hf]), i + 3, right)

    for hf in (0, 1):
        both(hf, 0, 0, 0, 0)
    for hf in (0, 1):
        both(hf, 1, 0, 0, 4)
    for hf in (0, 1):
        relay(hf, 0, 0, 0, 0)
        both(hf, 1, 3, 0, 8)
        both(hf, 1, 1, 0, 12)
    for hf in (0, 1):
        relay(hf, 1, 0, 0, 4)
    for hf in (0, 1):
        last(hf, 0, 0, 0, 0)
        both(hf, 1, 2, 0, 16)
    for a, i in ((3, 8), (1, 12), (2, 16)):
        for hf in (0, 1):
            relay(hf, 1, a, 0, i)
    for a, i in ((0, 4), (3, 8), (1, 12), (2, 16)):
        for hf in (0, 1):
            last(hf, 1, a, 0, i)
    for cp in weights:
        cp.wait()

    def rows_of(group, b):
        lhs = [jnp.concatenate([attg[hf, group * 4 + i] for i in range(4)], axis=0) for hf in (0, 1)]
        return (jnp.dot(lhs[0], w_s[b, :1024, :], preferred_element_type=jnp.float32)
                + jnp.dot(lhs[1], w_s[b, 1024:, :], preferred_element_type=jnp.float32))

    for i in (0, 1):
        for b in (0, 1):
            tx[i, b] = rows_of(2 * (1 - k) + i, b).astype(jnp.bfloat16)
        outs.append(send(tx.at[i], rx.at[i], (cs, cr), i, core))
    for i in (0, 1):
        for b in (0, 1):
            acc[i, b] = rows_of(2 * k + i, b)
    mine_at = lambda b: (h == z) & (b == z)
    for i in (0, 1):
        arrive(rx.at[i], (cs, cr), i, core)
        for b in (0, 1):
            zt[b, i] = (acc[i, b] + rx[i, b].astype(jnp.float32)).astype(jnp.bfloat16)

            @pl.when(jnp.logical_not(mine_at(b)))
            def _():
                send(zt.at[b, i], zr.at[h, i], (zs, zrs.at[h]), i * 2 + b, zdev(b, z))

            @pl.when(mine_at(b))
            def _():
                zr[h, i] = zt[b, i]
    for i in (0, 1):
        for s in (0, 1):
            @pl.when(jnp.logical_not((s == h) & (z == h)))
            def _():
                pltpu.make_async_remote_copy(
                    src_ref=zr.at[s, i], dst_ref=zr.at[s, i], send_sem=zs.at[0], recv_sem=zrs.at[s, i * 2 + z],
                    device_id=zdev(h, s), device_id_type=MESH).wait_recv()
        out[pl.ds(i * 256, 256), :] = (zr[0, i].astype(jnp.float32) + zr[1, i].astype(jnp.float32)).astype(jnp.bfloat16)
    for i in (0, 1):
        for b in (0, 1):
            @pl.when(jnp.logical_not(mine_at(b)))
            def _():
                pltpu.make_async_remote_copy(
                    src_ref=zt.at[b, i], dst_ref=zt.at[b, i], send_sem=zs.at[i * 2 + b], recv_sem=zrs.at[0, 0],
                    device_id=zdev(b, z), device_id_type=MESH).wait_send()
    for cp in outs:
        cp.wait_send()


def project(o, st, w, wp):
    anywhere = pl.BlockSpec(memory_space=pl.ANY)
    dma = pltpu.SemaphoreType.DMA
    bf = jnp.bfloat16
    return pl.pallas_call(
        project_kernel,
        in_specs=[anywhere] * 4,
        out_specs=pl.BlockSpec(memory_space=pltpu.VMEM),
        out_shape=jax.ShapeDtypeStruct((512, 512), bf),
        scratch_shapes=[
            pltpu.VMEM((8, ROWS, HEADS * HD), bf), pltpu.VMEM((8, ROWS, 128), jnp.float32),
            pltpu.VMEM((2, 16, ROWS, 1024), bf), pltpu.VMEM((2, 2048, 512), bf),
            pltpu.VMEM((2, 2, 256, 512), bf), pltpu.VMEM((2, 2, 256, 512), bf),
            pltpu.VMEM((2, 2, 256, 512), jnp.float32),
            pltpu.VMEM((2, 2, 256, 512), bf), pltpu.VMEM((2, 2, 256, 512), bf),
            dma((2, 8)), dma((2, 8)), dma((2, 20)), dma((2, 20)), dma((2,)), dma((2,)), dma((4,)), dma((2, 4)), dma((4,)),
        ],
        compiler_params=pltpu.CompilerParams(collective_id=1, has_side_effects=True, vmem_limit_bytes=48 << 20),
        name="project",
    )(o, st, w, wp)


def shards(new_queries, new_keys, new_values, cache_keys, cache_values, out_weight, cache_docs, new_docs, slot_tile):
    other = lax.ppermute(out_weight, "ctx", [(i, i ^ 16) for i in range(32)])
    qg, kvg = gather(new_queries, cache_keys, cache_values, new_keys, new_values)
    c = lax.axis_index("ctx")
    place = jnp.reshape(c, (1,)).astype(jnp.int32)
    o, st = attention(qg, kvg.reshape(4 * MEM, HD), cache_docs, new_docs, slot_tile, place)
    return project(o, st, out_weight, other)


def solution(mesh):
    return jax.shard_map(
        shards,
        mesh=mesh,
        in_specs=(
            P("ctx", "tp"),
            P("ctx", "tp"),
            P("ctx", "tp"),
            P("ctx", "tp"),
            P("ctx", "tp"),
            P("tp", "ctx"),
            P(),
            P(),
            P(),
        ),
        out_specs=P("tp", "ctx"),
        check_vma=False,
    )
```

```python
import functools
import jax, jax.numpy as jnp
from jax import lax
from jax.experimental import pallas as pl
from jax.experimental.pallas import tpu as pltpu
from jax.sharding import PartitionSpec as P

HD=128; BLK=128; NEG=-1e30
SCALE=HD**-0.5
L2E=1.4426950408889634
ROWS=64; HEADS=16; CR=1024; HALF=CR+ROWS; MEM=2*HALF
SUB=1024

def attn_kernel(cdocs, ndocs, tiles, place, q_hbm, kv_hbm, o_hbm, st_hbm, q_ref, kv_ref, o_ref, st_ref,
                q_s, m_s, l_s, acc_s, lst, sems, *, nb):
    q_in = lambda g: pltpu.make_async_copy(q_hbm.at[g], q_ref.at[g], sems.at[0, g])
    o_out = lambda g: pltpu.make_async_copy(o_ref.at[g], o_hbm.at[g], sems.at[1, g])
    kv_in = pltpu.make_async_copy(kv_hbm, kv_ref, sems.at[2, 0])
    st_out = pltpu.make_async_copy(st_ref, st_hbm, sems.at[2, 1])
    kv_in.start()
    for g in range(8):
        q_in(g).start()
    kv_in.wait()

    def run(g, _):
        q_in(g).wait()
        attend_run(g, cdocs, ndocs, tiles, place, q_ref, kv_ref, o_ref, st_ref, q_s, m_s, l_s, acc_s, lst, nb)
        o_out(g).start()
        return 0
    lax.fori_loop(0, 8, run, 0)
    st_out.start()
    for g in range(8):
        o_out(g).wait()
    st_out.wait()


def attend_run(g, cdocs, ndocs, tiles, place, q_ref, kv_ref, o_ref, st_ref, q_s, m_s, l_s, acc_s, lst, nb):
    c = place[0]
    y = c % 4
    src = g * 4 + y
    members = [c - y + i for i in range(4)]
    tq = tiles[src]
    qd = ndocs[tq // 2]
    nrow = ROWS*HEADS
    for h in range(HEADS):
        q_s[h*ROWS:(h+1)*ROWS, :] = q_ref[g, :, h*HD:(h+1)*HD]
    m_s[...] = jnp.full_like(m_s, NEG)
    l_s[...] = jnp.zeros_like(l_s)
    acc_s[...] = jnp.zeros_like(acc_s)
    n = jnp.int32(0)
    for mi, c in enumerate(members):
        def add(b, n):
            ok = cdocs[c*8 + b] == qd
            lst[n] = mi*MEM + b*BLK
            return n + ok.astype(jnp.int32)
        n = lax.fori_loop(0, 8, add, n)

    def slow_step(kc, vc, mask_fn):
        for t in range(nrow//SUB):
            r = pl.ds(t*SUB, SUB)
            s = lax.dot_general(q_s[r, :], kc, (((1,),(1,)),((),())), preferred_element_type=jnp.float32)
            if mask_fn is not None:
                s = mask_fn(s)
            w = s.shape[1]//128
            mx = s[:, :128]
            for i in range(1, w):
                mx = jnp.maximum(mx, s[:, i*128:(i+1)*128])
            mx = jnp.max(mx, axis=1, keepdims=True)
            m_old = m_s[r, :]
            m_new = jnp.maximum(m_old, mx)
            alpha = jnp.exp2((m_old - m_new)*(SCALE*L2E))
            p = [jnp.exp2((s[:, i*128:(i+1)*128] - m_new)*(SCALE*L2E)) for i in range(w)]
            ps = p[0]
            for i in range(1, w):
                ps = ps + p[i]
            l_s[r, :] = l_s[r, :]*alpha + ps
            m_s[r, :] = m_new
            pb = jnp.concatenate([x.astype(jnp.bfloat16) for x in p], axis=1)
            acc_s[r, :] = acc_s[r, :]*alpha + jnp.dot(pb, vc, preferred_element_type=jnp.float32)


    def peak(kc, mask_fn):
        for t in range(nrow//SUB):
            r = pl.ds(t*SUB, SUB)
            s = lax.dot_general(q_s[r, :], kc, (((1,),(1,)),((),())), preferred_element_type=jnp.float32)
            if mask_fn is not None:
                s = mask_fn(s)
            w = s.shape[1]//128
            mx = s[:, :128]
            for i in range(1, w):
                mx = jnp.maximum(mx, s[:, i*128:(i+1)*128])
            m_s[r, :] = jnp.broadcast_to(jnp.max(mx, axis=1, keepdims=True), (SUB, 128))

    def step(kc, vc, mask_fn):
        for t in range(nrow//SUB):
            r = pl.ds(t*SUB, SUB)
            s = lax.dot_general(q_s[r, :], kc, (((1,),(1,)),((),())), preferred_element_type=jnp.float32)
            if mask_fn is not None:
                s = mask_fn(s)
            w = s.shape[1]//128
            m = m_s[r, :]
            p = [jnp.exp2((s[:, i*128:(i+1)*128] - m)*(SCALE*L2E)) for i in range(w)]
            ps = p[0]
            for i in range(1, w):
                ps = ps + p[i]
            l_s[r, :] = l_s[r, :] + ps
            pb = jnp.concatenate([x.astype(jnp.bfloat16) for x in p], axis=1)
            acc_s[r, :] = acc_s[r, :] + jnp.dot(pb, vc, preferred_element_type=jnp.float32)

    def at(off, rows=BLK):
        return kv_ref[pl.ds(pl.multiple_of(off, 64), rows), :]

    def chunks(step):
        def chunk(base, size):
            offs = [lst[base + j] for j in range(size)]
            kc = jnp.concatenate([at(o) for o in offs], axis=0)
            vc = jnp.concatenate([at(o + HALF) for o in offs], axis=0)
            step(kc, vc, None)
        def body(i, _):
            chunk(i*nb, nb)
            return 0
        lax.fori_loop(0, n // nb, body, 0)
        size = nb // 2
        while size >= 1:
            @pl.when((n // size) % 2 == 1)
            def _(size=size):
                chunk((n // (2*size))*(2*size), size)
            size //= 2
    kcs = []; vcs = []
    newlims = []
    for mi, c in enumerate(members):
        tk = tiles[c]
        same_doc = ndocs[tk // 2] == qd
        full_ok = same_doc & (tk < tq)
        diag = tk == tq
        newlims.append((jnp.where(full_ok, 1 << 20, jnp.where(diag, 0, -1)), jnp.where(diag, 1, 0)))
        kcs.append(kv_ref[mi*MEM + CR: mi*MEM + HALF, :])
        vcs.append(kv_ref[mi*MEM + HALF + CR: (mi+1)*MEM, :])
    kc = jnp.concatenate(kcs, axis=0); vc = jnp.concatenate(vcs, axis=0)
    any_new = functools.reduce(jnp.logical_or, [lim >= 0 for lim, _ in newlims])
    def mask(s):
        row = lax.broadcasted_iota(jnp.int32, (SUB, 128), 0) % ROWS
        lane = lax.broadcasted_iota(jnp.int32, (SUB, 128), 1)
        out = []
        for a in range(2):
            (b0, d0), (b1, d1) = newlims[2*a], newlims[2*a+1]
            lo = row*d0 + b0
            hi = row*d1 + b1
            ok = lane <= jnp.where(lane < ROWS, lo, hi + ROWS)
            k0 = a*128
            out.append(jnp.where(ok, s[:, k0:k0+128], NEG))
        return jnp.concatenate(out, axis=1)
    @pl.when(n > 0)
    def _():
        peak(at(lst[0]), None)
    @pl.when((n == 0) & any_new)
    def _():
        peak(kc, mask)
    chunks(step)
    @pl.when(any_new)
    def _():
        step(kc, vc, mask)
    @pl.when(jnp.logical_not(jnp.max(l_s[...]) < 1e30))
    def _():
        m_s[...] = jnp.full_like(m_s, NEG)
        l_s[...] = jnp.zeros_like(l_s)
        acc_s[...] = jnp.zeros_like(acc_s)
        chunks(slow_step)
        @pl.when(any_new)
        def _():
            slow_step(kc, vc, mask)
    lane = lax.broadcasted_iota(jnp.int32, (ROWS, 128), 1)
    st = jnp.full((ROWS, 128), NEG, jnp.float32)
    for h in range(HEADS):
        r = pl.ds(h*ROWS, ROWS)
        l = jnp.sum(l_s[r, :], axis=1, keepdims=True)
        l = jnp.maximum(l, 1e-30)
        o_ref[g, :, h*HD:(h+1)*HD] = (acc_s[r, :] / l).astype(jnp.bfloat16)
        lse = m_s[r, :]*SCALE + jnp.log(l)
        st = jnp.where(lane == h, lse, st)
    st_ref[g] = st

def attention(qg, kvg, cdocs, ndocs, tiles, place, nb=4):
    nrow = ROWS*HEADS
    smem, anywhere = pl.BlockSpec(memory_space=pltpu.SMEM), pl.BlockSpec(memory_space=pl.ANY)
    return pl.pallas_call(
        functools.partial(attn_kernel, nb=nb),
        in_specs=[smem] * 4 + [anywhere] * 2,
        out_specs=[anywhere] * 2,
        scratch_shapes=[pltpu.VMEM((8, ROWS, HEADS*HD), jnp.bfloat16), pltpu.VMEM((4*MEM, HD), jnp.bfloat16),
                        pltpu.VMEM((8, ROWS, HEADS*HD), jnp.bfloat16), pltpu.VMEM((8, ROWS, 128), jnp.float32),
                        pltpu.VMEM((nrow, HD), jnp.bfloat16), pltpu.VMEM((nrow, 128), jnp.float32),
                        pltpu.VMEM((nrow, 128), jnp.float32), pltpu.VMEM((nrow, HD), jnp.float32),
                        pltpu.SMEM((40,), jnp.int32), pltpu.SemaphoreType.DMA((3, 8))],
        out_shape=[jax.ShapeDtypeStruct((8, ROWS, HEADS*HD), jnp.bfloat16),
                   jax.ShapeDtypeStruct((8, ROWS, 128), jnp.float32)],
        compiler_params=pltpu.CompilerParams(vmem_limit_bytes=56 << 20),
        name="attention",
    )(cdocs, ndocs, tiles, place, qg, kvg)


MESH = pl.DeviceIdType.MESH
WROWS = 768


def coords():
    c = lax.axis_index("ctx")
    return c // 16, (c // 4) % 4, c % 4


def ctx_of(z, x, y):
    return z * 16 + x * 4 + y


def send(src, dst, sems, i, device):
    copy = pltpu.make_async_remote_copy(
        src_ref=src, dst_ref=dst, send_sem=sems[0].at[i], recv_sem=sems[1].at[i],
        device_id=device, device_id_type=MESH)
    copy.start()
    return copy


def arrive(ref, sems, i, device):
    pltpu.make_async_remote_copy(
        src_ref=ref, dst_ref=ref, send_sem=sems[0].at[i], recv_sem=sems[1].at[i],
        device_id=device, device_id_type=MESH).wait_recv()


def greet(peers):
    barrier = pltpu.get_barrier_semaphore()
    for device in peers:
        pl.semaphore_signal(barrier, inc=1, device_id=device, device_id_type=MESH)
    pl.semaphore_wait(barrier, len(peers))


def gather_kernel(q, ck, cv, nk, nv, w, q_out, kv_out, w_out, rest_out, qg, kvg, wg, wr, ws, ssem, rsem, lsem, osem):
    z, x, y = coords()
    sems = (ssem, rsem)
    zp = 1 - z
    xr, xl, yr, yl = (x + 1) % 4, (x + 3) % 4, (y + 1) % 4, (y + 3) % 4
    x2, y2 = (x + 2) % 4, (y + 2) % 4
    dev = lambda z, x, y: {"ctx": ctx_of(z, x, y)}
    to_yr, to_yl, to_xr, to_xl, to_z = dev(z, x, yr), dev(z, x, yl), dev(z, xr, y), dev(z, xl, y), dev(zp, x, y)
    slot = lambda z, x: z * 4 + x
    me = slot(z, x)
    out = []
    pieces = [(ck, 0, CR), (nk, CR, ROWS), (cv, HALF, CR), (nv, HALF + CR, ROWS)]
    locs = [pltpu.make_async_copy(q, qg.at[me], lsem.at[0])]
    for i, (src, off, n) in enumerate(pieces):
        locs.append(pltpu.make_async_copy(src, kvg.at[y, pl.ds(off, n)], lsem.at[1 + i]))
    locs.append(pltpu.make_async_copy(w.at[pl.ds(0, WROWS)], ws, lsem.at[5]))
    locs.append(pltpu.make_async_copy(w.at[pl.ds(WROWS, 2048 - WROWS)], wr, lsem.at[6]))
    for cp in locs:
        cp.start()
    greet([to_yr, to_yl, to_xr, to_xl, to_z])
    kh, vh = pl.ds(0, HALF), pl.ds(HALF, HALF)
    saves = []

    def save(src, dst):
        saves.append(pltpu.make_async_copy(src, dst, osem.at[len(saves)]))
        saves[-1].start()

    locs[0].wait()
    out.append(send(qg.at[me], qg.at[me], sems, 0, to_z))
    out.append(send(qg.at[me], qg.at[me], sems, 9, to_xr))
    out.append(send(qg.at[me], qg.at[me], sems, 10, to_xl))
    for cp in locs[1:5]:
        cp.wait()
    out.append(send(kvg.at[y, kh], kvg.at[y, kh], sems, 1, to_yr))
    out.append(send(kvg.at[y, vh], kvg.at[y, vh], sems, 2, to_yl))
    out.append(send(kvg.at[y, vh], kvg.at[y, vh], sems, 3, to_yr))
    out.append(send(kvg.at[y, kh], kvg.at[y, kh], sems, 4, to_yl))
    locs[5].wait()
    out.append(send(ws, wg, sems, 19, to_z))
    save(qg.at[me], q_out.at[me])
    save(kvg.at[y], kv_out.at[y])
    locs[6].wait()
    save(wr, rest_out)
    other = slot(zp, x)
    arrive(qg.at[other], sems, 0, to_z)
    out.append(send(qg.at[other], qg.at[other], sems, 11, to_xr))
    out.append(send(qg.at[other], qg.at[other], sems, 12, to_xl))
    save(qg.at[other], q_out.at[other])
    lo, hi = pl.ds(0, 32), pl.ds(32, 32)
    arrive(qg.at[slot(z, xl)], sems, 9, to_xl)
    out.append(send(qg.at[slot(z, xl), lo], qg.at[slot(z, xl), lo], sems, 13, to_xr))
    save(qg.at[slot(z, xl)], q_out.at[slot(z, xl)])
    arrive(qg.at[slot(z, xr)], sems, 10, to_xr)
    out.append(send(qg.at[slot(z, xr), hi], qg.at[slot(z, xr), hi], sems, 14, to_xl))
    save(qg.at[slot(z, xr)], q_out.at[slot(z, xr)])
    arrive(kvg.at[yl, kh], sems, 1, to_yl)
    out.append(send(kvg.at[yl, kh], kvg.at[yl, kh], sems, 17, to_yr))
    arrive(kvg.at[yr, vh], sems, 2, to_yr)
    out.append(send(kvg.at[yr, vh], kvg.at[yr, vh], sems, 18, to_yl))
    arrive(qg.at[slot(zp, xl)], sems, 11, to_xl)
    out.append(send(qg.at[slot(zp, xl), lo], qg.at[slot(zp, xl), lo], sems, 15, to_xr))
    save(qg.at[slot(zp, xl)], q_out.at[slot(zp, xl)])
    arrive(qg.at[slot(zp, xr)], sems, 12, to_xr)
    out.append(send(qg.at[slot(zp, xr), hi], qg.at[slot(zp, xr), hi], sems, 16, to_xl))
    save(qg.at[slot(zp, xr)], q_out.at[slot(zp, xr)])
    arrive(kvg.at[yl, vh], sems, 3, to_yl)
    arrive(kvg.at[yr, kh], sems, 4, to_yr)
    save(kvg.at[yl], kv_out.at[yl])
    save(kvg.at[yr], kv_out.at[yr])
    arrive(qg.at[slot(z, x2), lo], sems, 13, to_xl)
    arrive(qg.at[slot(z, x2), hi], sems, 14, to_xr)
    save(qg.at[slot(z, x2)], q_out.at[slot(z, x2)])
    arrive(qg.at[slot(zp, x2), lo], sems, 15, to_xl)
    arrive(qg.at[slot(zp, x2), hi], sems, 16, to_xr)
    save(qg.at[slot(zp, x2)], q_out.at[slot(zp, x2)])
    arrive(kvg.at[y2, kh], sems, 17, to_yl)
    arrive(kvg.at[y2, vh], sems, 18, to_yr)
    save(kvg.at[y2], kv_out.at[y2])
    arrive(wg, sems, 19, to_z)
    save(wg, w_out)
    for cp in saves:
        cp.wait()
    for cp in out:
        cp.wait_send()


def gather(q, ck, cv, nk, nv, w):
    hbm, bf = pl.BlockSpec(memory_space=pl.ANY), jnp.bfloat16
    return pl.pallas_call(
        gather_kernel,
        in_specs=[hbm] * 6,
        out_specs=[hbm] * 4,
        out_shape=[jax.ShapeDtypeStruct((8, ROWS, HEADS * HD), jnp.bfloat16),
                   jax.ShapeDtypeStruct((4, MEM, HD), jnp.bfloat16),
                   jax.ShapeDtypeStruct((WROWS, 512), jnp.bfloat16),
                   jax.ShapeDtypeStruct((2048 - WROWS, 512), jnp.bfloat16)],
        scratch_shapes=[pltpu.VMEM((8, ROWS, HEADS * HD), bf), pltpu.VMEM((4, MEM, HD), bf), pltpu.VMEM((WROWS, 512), bf),
                        pltpu.VMEM((2048 - WROWS, 512), bf), pltpu.VMEM((WROWS, 512), bf), pltpu.SemaphoreType.DMA((20,)),
                        pltpu.SemaphoreType.DMA((20,)), pltpu.SemaphoreType.DMA((7,)), pltpu.SemaphoreType.DMA((14,))],
        compiler_params=pltpu.CompilerParams(collective_id=0, has_side_effects=True, vmem_limit_bytes=56 << 20),
        name="gather",
    )(q, ck, cv, nk, nv, w)


def merge(parts, stats):
    largest = functools.reduce(jnp.maximum, stats)
    e = [jnp.exp(s - largest) for s in stats]
    total = functools.reduce(jnp.add, e)
    inverse = 1.0 / total
    e = [a * inverse for a in e]
    cols = []
    for head in range(HEADS):
        a = None
        for weight, part in zip(e, parts):
            term = weight[:, head:head + 1] * part[:, head * HD:(head + 1) * HD].astype(jnp.float32)
            a = term if a is None else a + term
        cols.append(a.astype(jnp.bfloat16))
    return cols, largest + jnp.log(total)


def put(ref, cols):
    for head, a in enumerate(cols):
        ref[:, head * HD:(head + 1) * HD] = a


def project_kernel(o_hbm, st_hbm, w, wlo, whi, out, o, st, px, sx, pz, sz, mz, nz, rz, tz, mx, nx, rx, tx_s, attg, w_s, ct, cr, acc, zt, zr,
                   a_s, a_r, b_s, b_r, c_s, c_r, d_s, d_r, gs, gr, cs, crs, zs, zrs, lsem):
    z, x, y = coords()
    t = lax.axis_index("tp")
    h, k = t // 2, t % 2
    dev = lambda z, x, y: {"ctx": ctx_of(z, x, y)}
    zdev = lambda b, zh: {"ctx": ctx_of(b, x, y), "tp": zh * 2 + k}
    zp = 1 - z
    xr, xl, yr, yl = (x + 1) % 4, (x + 3) % 4, (y + 1) % 4, (y + 3) % 4
    core = {"tp": h * 2 + 1 - k}
    to_yr, to_yl, to_xr, to_xl = dev(z, x, yr), dev(z, x, yl), dev(z, xr, y), dev(z, xl, y)
    to_z = dev(zp, x, y)
    to_x = lambda d: dev(z, (x + d) % 4, y)
    ready = [pltpu.make_async_copy(o_hbm, o, lsem.at[3]), pltpu.make_async_copy(st_hbm, st, lsem.at[4])]
    for cp in ready:
        cp.start()
    greet([to_xr, to_xl, to_x(2), to_z, to_yr, to_yl, core, zdev(0, 1 - h), zdev(1, 1 - h)])
    lo, hi = pl.ds(0, 32), pl.ds(32, 32)
    outs = []

    for cp in ready:
        cp.wait()
    for d in (2, 1, 3, 0):
        xx = (x + d) % 4
        outs.append(send(st.at[zp, xx, hi], sz.at[xx], (b_s.at[1], b_r.at[1]), d, to_z))
        outs.append(send(o.at[zp, xx, hi], pz.at[xx], (b_s.at[0], b_r.at[0]), d, to_z))
    for d in (2, 1, 3):
        xx = (x + d) % 4
        outs.append(send(st.at[:, xx, lo], sx.at[x], (a_s.at[1], a_r.at[1]), d, to_x(d)))
        outs.append(send(o.at[:, xx, lo], px.at[x], (a_s.at[0], a_r.at[0]), d, to_x(d)))
    weights = [pltpu.make_async_copy(w, w_s.at[z], lsem.at[0]),
               pltpu.make_async_copy(wlo, w_s.at[zp, pl.ds(0, WROWS)], lsem.at[1]),
               pltpu.make_async_copy(whi, w_s.at[zp, pl.ds(WROWS, 2048 - WROWS)], lsem.at[2])]
    for cp in weights:
        cp.start()
    for d in (2, 1, 3, 0):
        xx = (x + d) % 4
        arrive(sz.at[xx], (b_s.at[1], b_r.at[1]), d, to_z)
        arrive(pz.at[xx], (b_s.at[0], b_r.at[0]), d, to_z)
        cols, lse = merge([o[z, xx, 32:64, :], pz[xx]], [st[z, xx, 32:64, :], sz[xx]])
        if d == 0:
            put(rx.at[x], cols)
            tx_s[x] = lse
        else:
            put(mx.at[d - 1], cols)
            nx[d - 1] = lse
            outs.append(send(nx.at[d - 1], tx_s.at[x], (d_s.at[1], d_r.at[1]), d, to_x(d)))
            outs.append(send(mx.at[d - 1], rx.at[x], (d_s.at[0], d_r.at[0]), d, to_x(d)))
    for d in (2, 1, 3):
        xx = (x + 4 - d) % 4
        arrive(sx.at[xx], (a_s.at[1], a_r.at[1]), d, to_x(4 - d))
        arrive(px.at[xx], (a_s.at[0], a_r.at[0]), d, to_x(4 - d))
    others = [(x + d) % 4 for d in (1, 2, 3)]
    cols, lse = merge([o[zp, x, 0:32, :]] + [px[xx, zp] for xx in others],
                      [st[zp, x, 0:32, :]] + [sx[xx, zp] for xx in others])
    put(mz, cols)
    nz[...] = lse
    outs.append(send(nz, tz, (c_s, c_r), 1, to_z))
    outs.append(send(mz, rz, (c_s, c_r), 0, to_z))
    own_cols, own_lse = merge([o[z, x, 0:32, :]] + [px[xx, z] for xx in others],
                              [st[z, x, 0:32, :]] + [sx[xx, z] for xx in others])
    mine = x * 4 + y
    put(attg.at[mine, lo], own_cols)
    arrive(tz, (c_s, c_r), 1, to_z)
    arrive(rz, (c_s, c_r), 0, to_z)
    cols, _ = merge([attg[mine, 0:32, :], rz[...]], [own_lse, tz[...]])
    put(attg.at[mine, lo], cols)

    slot = lambda x, y: x * 4 + y

    def block(hf, a, b, part=None):
        s = slot((x + a) % 4, (y + b) % 4) if hf == 0 else slot((x + b) % 4, (y + a) % 4)
        return attg.at[s, pl.ds(32 * hf, 32) if part is None else pl.ds(32 * hf + 16 * part, 16)]

    def ways(hf, stage):
        return (to_xr, to_xl) if (hf == 0) == (stage == 0) else (to_yr, to_yl)

    def both(hf, stage, a, i):
        right, left = ways(hf, stage)
        ref = block(hf, a, 0)
        outs.append(send(ref, ref, (gs.at[hf], gr.at[hf]), i, right))
        outs.append(send(ref, ref, (gs.at[hf], gr.at[hf]), i + 1, left))

    def at(stage, a, n):
        return (n, 0) if stage == 0 else (a, n)

    def relay(hf, stage, a, i):
        right, left = ways(hf, stage)
        arrive(block(hf, *at(stage, a, 3)), (gs.at[hf], gr.at[hf]), i, left)
        ref = block(hf, *at(stage, a, 3), part=0)
        outs.append(send(ref, ref, (gs.at[hf], gr.at[hf]), i + 2, right))
        arrive(block(hf, *at(stage, a, 1)), (gs.at[hf], gr.at[hf]), i + 1, right)
        ref = block(hf, *at(stage, a, 1), part=1)
        outs.append(send(ref, ref, (gs.at[hf], gr.at[hf]), i + 3, left))

    def last(hf, stage, a, i):
        right, left = ways(hf, stage)
        arrive(block(hf, *at(stage, a, 2), part=0), (gs.at[hf], gr.at[hf]), i + 2, left)
        arrive(block(hf, *at(stage, a, 2), part=1), (gs.at[hf], gr.at[hf]), i + 3, right)

    both(0, 0, 0, 0)
    both(0, 1, 0, 4)
    for d in (2, 1, 3):
        xx = (x + 4 - d) % 4
        arrive(tx_s.at[xx], (d_s.at[1], d_r.at[1]), d, to_x(4 - d))
        arrive(rx.at[xx], (d_s.at[0], d_r.at[0]), d, to_x(4 - d))
    cols, _ = merge([rx[i] for i in range(4)], [tx_s[i] for i in range(4)])
    put(attg.at[mine, hi], cols)
    both(1, 0, 0, 0)
    both(1, 1, 0, 4)
    for hf in (0, 1):
        relay(hf, 0, 0, 0)
        both(hf, 1, 3, 8)
        both(hf, 1, 1, 12)
    for hf in (0, 1):
        last(hf, 0, 0, 0)
        both(hf, 1, 2, 16)
    for a, i in ((0, 4), (3, 8), (1, 12), (2, 16)):
        for hf in (0, 1):
            relay(hf, 1, a, i)
    for cp in weights:
        cp.wait()

    def places(p):
        hf, late = p % 2, p // 2
        if hf == 0:
            first = [(2 * (1 - k) + i, (y + n) % 4) for i in (0, 1) for n in ((1, 3), (0, 2))[late]]
            then = [(2 * k + i, (y + n) % 4) for i in (0, 1) for n in ((1, 3), (0, 2))[late]]
        else:
            parity = (x + 1 - late) % 2
            first = [(2 * (1 - k) + parity, n) for n in range(4)]
            then = [(2 * k + parity, n) for n in range(4)]
        return hf, first, then

    mine_at = lambda b: (h == z) & (b == z)

    def multiply(p):
        hf, first, then = places(p)
        lhs = jnp.concatenate([attg[slot(*s), 32 * hf:32 * hf + 32, :] for s in first + then], axis=0)
        for b in (0, 1):
            r = jnp.dot(lhs, w_s[b], preferred_element_type=jnp.float32)
            ct[p, b] = r[:128].astype(jnp.bfloat16)
            acc[p, b] = r[128:]
        outs.append(send(ct.at[p], cr.at[p], (cs, crs), p, core))

    def exchange(p):
        arrive(cr.at[p], (cs, crs), p, core)
        for b in (0, 1):
            zt[p, b] = (acc[p, b] + cr[p, b].astype(jnp.float32)).astype(jnp.bfloat16)

            @pl.when(jnp.logical_not(mine_at(b)))
            def _():
                send(zt.at[p, b], zr.at[h, p], (zs, zrs.at[h]), p * 2 + b, zdev(b, z))

            @pl.when(mine_at(b))
            def _():
                zr[h, p] = zt[p, b]

    multiply(0)
    multiply(1)
    exchange(0)
    exchange(1)
    for a, i in ((0, 4), (3, 8), (1, 12), (2, 16)):
        for hf in (0, 1):
            last(hf, 1, a, i)
    multiply(2)
    multiply(3)
    exchange(2)
    exchange(3)
    for p in range(4):
        for s in (0, 1):
            @pl.when(jnp.logical_not((s == h) & (z == h)))
            def _():
                pltpu.make_async_remote_copy(
                    src_ref=zr.at[s, p], dst_ref=zr.at[s, p], send_sem=zs.at[0], recv_sem=zrs.at[s, p * 2 + z],
                    device_id=zdev(h, s), device_id_type=MESH).wait_recv()
        total = (zr[0, p].astype(jnp.float32) + zr[1, p].astype(jnp.float32)).astype(jnp.bfloat16)
        hf, _, then = places(p)
        for i, (xx, yy) in enumerate(then):
            off = (slot(xx, yy) - 8 * k) * 64 + 32 * hf
            out[pl.ds(pl.multiple_of(off, 32), 32), :] = total[32 * i:32 * i + 32]
    for p in range(4):
        for b in (0, 1):
            @pl.when(jnp.logical_not(mine_at(b)))
            def _():
                pltpu.make_async_remote_copy(
                    src_ref=zt.at[p, b], dst_ref=zt.at[p, b], send_sem=zs.at[p * 2 + b], recv_sem=zrs.at[0, 0],
                    device_id=zdev(b, z), device_id_type=MESH).wait_send()
    for cp in outs:
        cp.wait_send()


def project(o, st, w, wlo, whi):
    hbm, vmem = pl.BlockSpec(memory_space=pl.ANY), pl.BlockSpec(memory_space=pltpu.VMEM)
    dma = pltpu.SemaphoreType.DMA
    bf, f32 = jnp.bfloat16, jnp.float32
    wide = HEADS * HD
    return pl.pallas_call(
        project_kernel,
        in_specs=[hbm] * 5,
        out_specs=vmem,
        out_shape=jax.ShapeDtypeStruct((512, 512), bf),
        scratch_shapes=[
            pltpu.VMEM((2, 4, ROWS, wide), bf), pltpu.VMEM((2, 4, ROWS, 128), f32),
            pltpu.VMEM((4, 2, 32, wide), bf), pltpu.VMEM((4, 2, 32, 128), f32),
            pltpu.VMEM((4, 32, wide), bf), pltpu.VMEM((4, 32, 128), f32),
            pltpu.VMEM((32, wide), bf), pltpu.VMEM((32, 128), f32),
            pltpu.VMEM((32, wide), bf), pltpu.VMEM((32, 128), f32),
            pltpu.VMEM((3, 32, wide), bf), pltpu.VMEM((3, 32, 128), f32),
            pltpu.VMEM((4, 32, wide), bf), pltpu.VMEM((4, 32, 128), f32),
            pltpu.VMEM((16, ROWS, wide), bf), pltpu.VMEM((2, 2048, 512), bf),
            pltpu.VMEM((4, 2, 128, 512), bf), pltpu.VMEM((4, 2, 128, 512), bf), pltpu.VMEM((4, 2, 128, 512), f32),
            pltpu.VMEM((4, 2, 128, 512), bf), pltpu.VMEM((2, 4, 128, 512), bf),
            dma((2, 4)), dma((2, 4)), dma((2, 4)), dma((2, 4)), dma((2,)), dma((2,)), dma((2, 4)), dma((2, 4)),
            dma((2, 20)), dma((2, 20)), dma((4,)), dma((4,)), dma((8,)), dma((2, 8)), dma((5,)),
        ],
        compiler_params=pltpu.CompilerParams(collective_id=1, has_side_effects=True, vmem_limit_bytes=56 << 20),
        name="project",
    )(o, st, w, wlo, whi)


def shards(new_queries, new_keys, new_values, cache_keys, cache_values, out_weight, cache_docs, new_docs, slot_tile):
    qg, kvg, wlo, rest = gather(new_queries, cache_keys, cache_values, new_keys, new_values, out_weight)
    whi = lax.ppermute(rest, "ctx", [(i, i ^ 16) for i in range(32)])
    place = jnp.reshape(lax.axis_index("ctx"), (1,)).astype(jnp.int32)
    o, st = attention(qg, kvg.reshape(4 * MEM, HD), cache_docs, new_docs, slot_tile, place)
    return project(o.reshape(2, 4, ROWS, HEADS * HD), st.reshape(2, 4, ROWS, 128), out_weight, wlo, whi)


def solution(mesh):
    return jax.shard_map(
        shards,
        mesh=mesh,
        in_specs=(
            P("ctx", "tp"),
            P("ctx", "tp"),
            P("ctx", "tp"),
            P("ctx", "tp"),
            P("ctx", "tp"),
            P("tp", "ctx"),
            P(),
            P(),
            P(),
        ),
        out_specs=P("tp", "ctx"),
        check_vma=False,
    )
```

```python
import functools
import jax, jax.numpy as jnp
from jax import lax
from jax.experimental import pallas as pl
from jax.experimental.pallas import tpu as pltpu
from jax.sharding import PartitionSpec as P

HD=128; BLK=128; NEG=-1e30
SCALE=HD**-0.5
L2E=1.4426950408889634
ROWS=64; HEADS=16; CR=1024; HALF=CR+ROWS; MEM=2*HALF
SUB=1024

def attn_kernel(cdocs, ndocs, tiles, place, q_hbm, kv_hbm, o_hbm, st_hbm, q_ref, kv_ref, o_ref, st_ref,
                q_s, m_s, l_s, acc_s, top_s, lst, cnt, sems, *, nb):
    q_in = lambda g: pltpu.make_async_copy(q_hbm.at[g], q_ref.at[g], sems.at[0, g])
    o_out = lambda g: pltpu.make_async_copy(o_ref.at[g], o_hbm.at[g], sems.at[1, g])
    kv_in = pltpu.make_async_copy(kv_hbm, kv_ref, sems.at[2, 0])
    st_out = pltpu.make_async_copy(st_ref, st_hbm.at[pl.ds(0, 8)], sems.at[2, 1])
    kv_in.start()
    for g in range(8):
        q_in(g).start()
    c = place[0]
    y = c % 4
    for d in range(4):
        cnt[d] = 0

    def add(i, _):
        d = cdocs[(c - y) * 8 + i]
        n = cnt[d]
        lst[d * 32 + n] = (i // 8) * MEM + (i % 8) * BLK
        cnt[d] = n + 1
        return 0
    lax.fori_loop(0, 32, add, 0)
    top_s[...] = jnp.zeros_like(top_s)
    kv_in.wait()

    def run(g, careful):
        attend_run(g, c, careful, cnt, ndocs, tiles, q_ref, kv_ref, o_ref, st_ref, q_s, m_s, l_s, acc_s, top_s, lst, nb)
        o_out(g).start()

    def fast(g, _):
        q_in(g).wait()
        run(g, False)
        return 0
    lax.fori_loop(0, 8, fast, 0)

    @pl.when(jnp.logical_not(jnp.max(top_s[...]) < 1e30))
    def _():
        def again(g, _):
            o_out(g).wait()
            run(g, True)
            return 0
        lax.fori_loop(0, 8, again, 0)
    st_out.start()
    for g in range(8):
        o_out(g).wait()
    st_out.wait()


def attend_run(g, c, careful, cnt, ndocs, tiles, q_ref, kv_ref, o_ref, st_ref, q_s, m_s, l_s, acc_s, top_s, lst, nb):
    y = c % 4
    src = g * 4 + y
    members = [c - y + i for i in range(4)]
    tq = tiles[src]
    qd = ndocs[tq // 2]
    nrow = ROWS*HEADS
    for h in range(HEADS):
        part = q_ref[g, :, h*HD:(h+1)*HD]
        q_s[h*ROWS:(h+1)*ROWS, :HD] = part
        q_s[h*ROWS:(h+1)*ROWS, HD:] = part
    if careful:
        m_s[...] = jnp.full_like(m_s, NEG)
    l_s[...] = jnp.zeros_like(l_s)
    acc_s[...] = jnp.zeros_like(acc_s)
    n = cnt[qd]
    first = qd * 32

    def scores(kc, masked):
        k2 = jnp.concatenate([kc, jnp.broadcast_to(-base, kc.shape)], axis=1)
        s = lax.dot_general(q_s[...], k2, (((1,),(1,)),((),())), preferred_element_type=jnp.float32)
        tiles_of = [s[:, i*128:(i+1)*128] for i in range(s.shape[1]//128)]
        return tiles_of[:-2] + mask(tiles_of[-2:]) if masked else tiles_of

    def step(kc, vc, masked):
        s = scores(kc, masked)
        if careful:
            m_old = m_s[...]
            m = jnp.maximum(m_old, jnp.max(functools.reduce(jnp.maximum, s), axis=1, keepdims=True))
            alpha = jnp.exp2((m_old - m)*(SCALE*L2E))
            l_s[...] = l_s[...]*alpha
            acc_s[...] = acc_s[...]*alpha
            m_s[...] = m
            s = [a - m for a in s]
        p = [jnp.exp2(a*(SCALE*L2E)) for a in s]
        l_s[...] = l_s[...] + functools.reduce(jnp.add, p)
        pb = jnp.concatenate([a.astype(jnp.bfloat16) for a in p], axis=1)
        acc_s[...] = acc_s[...] + jnp.dot(pb, vc, preferred_element_type=jnp.float32)

    def at(off, rows=BLK):
        return kv_ref[pl.ds(pl.multiple_of(off, 64), rows), :]

    newlims = []
    new_k, new_v = [], []
    for mi, cm in enumerate(members):
        tk = tiles[cm]
        full_ok = (ndocs[tk // 2] == qd) & (tk < tq)
        diag = tk == tq
        newlims.append((jnp.where(full_ok, 1 << 20, jnp.where(diag, 0, -1)), jnp.where(diag, 1, 0)))
        new_k.append(kv_ref[mi*MEM + CR: mi*MEM + HALF, :])
        new_v.append(kv_ref[mi*MEM + HALF + CR: (mi+1)*MEM, :])
    any_new = functools.reduce(jnp.logical_or, [lim >= 0 for lim, _ in newlims])
    where = jnp.int32(0)
    for mi in range(4):
        where = jnp.where(newlims[mi][0] >= 0, mi*MEM + CR, where)
    where = jnp.where(n > 0, lst[first], where)
    base = at(where, 16)[0:1, :]

    def mask(pair):
        row = lax.broadcasted_iota(jnp.int32, (nrow, 128), 0) % ROWS
        lane = lax.broadcasted_iota(jnp.int32, (nrow, 128), 1)
        out = []
        for a in range(2):
            (b0, d0), (b1, d1) = newlims[2*a], newlims[2*a+1]
            ok = lane <= jnp.where(lane < ROWS, row*d0 + b0, row*d1 + b1 + ROWS)
            out.append(jnp.where(ok, pair[a], NEG))
        return out

    def chunk(base, size, with_new=False):
        offs = [lst[first + base + j] for j in range(size)]
        kc = jnp.concatenate([at(o) for o in offs] + (new_k if with_new else []), axis=0)
        vc = jnp.concatenate([at(o + HALF) for o in offs] + (new_v if with_new else []), axis=0)
        step(kc, vc, with_new)

    if careful:
        def body(i, _):
            chunk(i, 1)
            return 0
        lax.fori_loop(0, n, body, 0)

        @pl.when(any_new)
        def _():
            chunk(0, 0, True)
    else:
        def body(i, _):
            chunk(i*2*nb, 2*nb)
            return 0
        lax.fori_loop(0, n // (2*nb), body, 0)

        @pl.when((n // nb) % 2 == 1)
        def _():
            chunk(n // (2*nb) * (2*nb), nb)
        for left in range(nb):
            @pl.when(any_new & (n % nb == left))
            def _(left=left):
                chunk(n - left, left, True)

            if left:
                @pl.when(jnp.logical_not(any_new) & (n % nb == left))
                def _(left=left):
                    chunk(n - left, left)
    lane = lax.broadcasted_iota(jnp.int32, (ROWS, 128), 1)
    st = jnp.full((ROWS, 128), NEG, jnp.float32)
    top = top_s[...]
    peaks = lax.dot_general(q_s[:, :HD], jnp.broadcast_to(base, (128, HD)), (((1,),(1,)),((),())),
                            preferred_element_type=jnp.float32)
    for h in range(HEADS):
        r = pl.ds(h*ROWS, ROWS)
        l = jnp.sum(l_s[r, :], axis=1, keepdims=True)
        top = jnp.maximum(top, l)
        some = l > 0.0
        l = jnp.where(some, l, 1.0)
        o_ref[g, :, h*HD:(h+1)*HD] = (acc_s[r, :] * (1.0 / l)).astype(jnp.bfloat16)
        peak = peaks[h*ROWS:(h+1)*ROWS]
        if careful:
            peak = peak + m_s[r, :]
        st = jnp.where(lane == h, jnp.where(some, peak*SCALE + jnp.log(l), NEG), st)
    st_ref[g] = st
    top_s[...] = top


def attention(qg, kvg, cdocs, ndocs, tiles, place, nb=4):
    nrow = ROWS*HEADS
    smem, anywhere = pl.BlockSpec(memory_space=pltpu.SMEM), pl.BlockSpec(memory_space=pl.ANY)
    return pl.pallas_call(
        functools.partial(attn_kernel, nb=nb),
        in_specs=[smem] * 4 + [anywhere] * 2,
        out_specs=[anywhere] * 2,
        scratch_shapes=[pltpu.VMEM((8, ROWS, HEADS*HD), jnp.bfloat16), pltpu.VMEM((4*MEM, HD), jnp.bfloat16),
                        pltpu.VMEM((8, ROWS, HEADS*HD), jnp.bfloat16), pltpu.VMEM((8, ROWS, 128), jnp.float32),
                        pltpu.VMEM((nrow, 2*HD), jnp.bfloat16), pltpu.VMEM((nrow, 128), jnp.float32),
                        pltpu.VMEM((nrow, 128), jnp.float32), pltpu.VMEM((nrow, HD), jnp.float32),
                        pltpu.VMEM((ROWS, 128), jnp.float32),
                        pltpu.SMEM((128,), jnp.int32), pltpu.SMEM((4,), jnp.int32), pltpu.SemaphoreType.DMA((3, 8))],
        out_shape=[jax.ShapeDtypeStruct((8, ROWS, HEADS*HD), jnp.bfloat16),
                   jax.ShapeDtypeStruct((24, ROWS, 128), jnp.float32)],
        compiler_params=pltpu.CompilerParams(vmem_limit_bytes=(64 << 20) - (512 << 10)),
        name="attention",
    )(cdocs, ndocs, tiles, place, qg, kvg)


MESH = pl.DeviceIdType.MESH
WROWS = 768
WMID = 1664


def coords():
    c = lax.axis_index("ctx")
    return c // 16, (c // 4) % 4, c % 4


def ctx_of(z, x, y):
    return z * 16 + x * 4 + y


def send(src, dst, sems, i, device):
    copy = pltpu.make_async_remote_copy(
        src_ref=src, dst_ref=dst, send_sem=sems[0].at[i], recv_sem=sems[1].at[i],
        device_id=device, device_id_type=MESH)
    copy.start()
    return copy


def arrive(ref, sems, i, device):
    pltpu.make_async_remote_copy(
        src_ref=ref, dst_ref=ref, send_sem=sems[0].at[i], recv_sem=sems[1].at[i],
        device_id=device, device_id_type=MESH).wait_recv()


def greet(peers):
    barrier = pltpu.get_barrier_semaphore()
    for device in peers:
        pl.semaphore_signal(barrier, inc=1, device_id=device, device_id_type=MESH)
    pl.semaphore_wait(barrier, len(peers))


def gather_kernel(q, ck, cv, nk, nv, w, q_out, kv_out, w_out, rest_out, qg, kvg, wg, wr, ws, ssem, rsem, lsem, osem):
    z, x, y = coords()
    sems = (ssem, rsem)
    zp = 1 - z
    xr, xl, yr, yl = (x + 1) % 4, (x + 3) % 4, (y + 1) % 4, (y + 3) % 4
    x2, y2 = (x + 2) % 4, (y + 2) % 4
    dev = lambda z, x, y: {"ctx": ctx_of(z, x, y)}
    to_yr, to_yl, to_xr, to_xl, to_z = dev(z, x, yr), dev(z, x, yl), dev(z, xr, y), dev(z, xl, y), dev(zp, x, y)
    slot = lambda z, x: z * 4 + x
    me = slot(z, x)
    out = []
    pieces = [(ck, 0, CR), (nk, CR, ROWS), (cv, HALF, CR), (nv, HALF + CR, ROWS)]
    locs = [pltpu.make_async_copy(q, qg.at[me], lsem.at[0])]
    for i, (src, off, n) in enumerate(pieces):
        locs.append(pltpu.make_async_copy(src, kvg.at[y, pl.ds(off, n)], lsem.at[1 + i]))
    locs.append(pltpu.make_async_copy(w.at[pl.ds(0, WROWS)], ws, lsem.at[5]))
    locs.append(pltpu.make_async_copy(w.at[pl.ds(WROWS, WMID - WROWS)], wr, lsem.at[6]))
    for cp in locs:
        cp.start()
    greet([to_yr, to_yl, to_xr, to_xl, to_z])
    kh, vh = pl.ds(0, HALF), pl.ds(HALF, HALF)
    saves = []

    def save(src, dst):
        saves.append(pltpu.make_async_copy(src, dst, osem.at[len(saves)]))
        saves[-1].start()

    locs[0].wait()
    out.append(send(qg.at[me], qg.at[me], sems, 0, to_z))
    out.append(send(qg.at[me], qg.at[me], sems, 9, to_xr))
    out.append(send(qg.at[me], qg.at[me], sems, 10, to_xl))
    for cp in locs[1:5]:
        cp.wait()
    out.append(send(kvg.at[y, kh], kvg.at[y, kh], sems, 1, to_yr))
    out.append(send(kvg.at[y, vh], kvg.at[y, vh], sems, 2, to_yl))
    out.append(send(kvg.at[y, vh], kvg.at[y, vh], sems, 3, to_yr))
    out.append(send(kvg.at[y, kh], kvg.at[y, kh], sems, 4, to_yl))
    locs[5].wait()
    out.append(send(ws, wg, sems, 19, to_z))
    save(qg.at[me], q_out.at[me])
    save(kvg.at[y], kv_out.at[y])
    locs[6].wait()
    save(wr, rest_out)
    other = slot(zp, x)
    arrive(qg.at[other], sems, 0, to_z)
    out.append(send(qg.at[other], qg.at[other], sems, 11, to_xr))
    out.append(send(qg.at[other], qg.at[other], sems, 12, to_xl))
    save(qg.at[other], q_out.at[other])
    lo, hi = pl.ds(0, 32), pl.ds(32, 32)
    arrive(qg.at[slot(z, xl)], sems, 9, to_xl)
    out.append(send(qg.at[slot(z, xl), lo], qg.at[slot(z, xl), lo], sems, 13, to_xr))
    save(qg.at[slot(z, xl)], q_out.at[slot(z, xl)])
    arrive(qg.at[slot(z, xr)], sems, 10, to_xr)
    out.append(send(qg.at[slot(z, xr), hi], qg.at[slot(z, xr), hi], sems, 14, to_xl))
    save(qg.at[slot(z, xr)], q_out.at[slot(z, xr)])
    arrive(kvg.at[yl, kh], sems, 1, to_yl)
    out.append(send(kvg.at[yl, kh], kvg.at[yl, kh], sems, 17, to_yr))
    arrive(kvg.at[yr, vh], sems, 2, to_yr)
    out.append(send(kvg.at[yr, vh], kvg.at[yr, vh], sems, 18, to_yl))
    arrive(qg.at[slot(zp, xl)], sems, 11, to_xl)
    out.append(send(qg.at[slot(zp, xl), lo], qg.at[slot(zp, xl), lo], sems, 15, to_xr))
    save(qg.at[slot(zp, xl)], q_out.at[slot(zp, xl)])
    arrive(qg.at[slot(zp, xr)], sems, 12, to_xr)
    out.append(send(qg.at[slot(zp, xr), hi], qg.at[slot(zp, xr), hi], sems, 16, to_xl))
    save(qg.at[slot(zp, xr)], q_out.at[slot(zp, xr)])
    arrive(kvg.at[yl, vh], sems, 3, to_yl)
    arrive(kvg.at[yr, kh], sems, 4, to_yr)
    save(kvg.at[yl], kv_out.at[yl])
    save(kvg.at[yr], kv_out.at[yr])
    arrive(qg.at[slot(z, x2), lo], sems, 13, to_xl)
    arrive(qg.at[slot(z, x2), hi], sems, 14, to_xr)
    save(qg.at[slot(z, x2)], q_out.at[slot(z, x2)])
    arrive(qg.at[slot(zp, x2), lo], sems, 15, to_xl)
    arrive(qg.at[slot(zp, x2), hi], sems, 16, to_xr)
    save(qg.at[slot(zp, x2)], q_out.at[slot(zp, x2)])
    arrive(kvg.at[y2, kh], sems, 17, to_yl)
    arrive(kvg.at[y2, vh], sems, 18, to_yr)
    save(kvg.at[y2], kv_out.at[y2])
    arrive(wg, sems, 19, to_z)
    save(wg, w_out)
    for cp in saves:
        cp.wait()
    for cp in out:
        cp.wait_send()


def gather(q, ck, cv, nk, nv, w):
    hbm, bf = pl.BlockSpec(memory_space=pl.ANY), jnp.bfloat16
    return pl.pallas_call(
        gather_kernel,
        in_specs=[hbm] * 6,
        out_specs=[hbm] * 4,
        out_shape=[jax.ShapeDtypeStruct((8, ROWS, HEADS * HD), jnp.bfloat16),
                   jax.ShapeDtypeStruct((4, MEM, HD), jnp.bfloat16),
                   jax.ShapeDtypeStruct((WROWS, 512), jnp.bfloat16),
                   jax.ShapeDtypeStruct((WMID - WROWS, 512), jnp.bfloat16)],
        scratch_shapes=[pltpu.VMEM((8, ROWS, HEADS * HD), bf), pltpu.VMEM((4, MEM, HD), bf), pltpu.VMEM((WROWS, 512), bf),
                        pltpu.VMEM((WMID - WROWS, 512), bf), pltpu.VMEM((WROWS, 512), bf), pltpu.SemaphoreType.DMA((20,)),
                        pltpu.SemaphoreType.DMA((20,)), pltpu.SemaphoreType.DMA((7,)), pltpu.SemaphoreType.DMA((14,))],
        compiler_params=pltpu.CompilerParams(collective_id=0, has_side_effects=True, vmem_limit_bytes=56 << 20),
        name="gather",
    )(q, ck, cv, nk, nv, w)


def merge(parts, stats):
    largest = functools.reduce(jnp.maximum, stats)
    e = [jnp.exp(s - largest) for s in stats]
    total = functools.reduce(jnp.add, e)
    inverse = 1.0 / total
    e = [a * inverse for a in e]
    cols = []
    for head in range(HEADS):
        a = None
        for weight, part in zip(e, parts):
            term = weight[:, head:head + 1] * part[:, head * HD:(head + 1) * HD].astype(jnp.float32)
            a = term if a is None else a + term
        cols.append(a.astype(jnp.bfloat16))
    return cols, largest + jnp.log(total)


def put(ref, cols):
    for head, a in enumerate(cols):
        ref[:, head * HD:(head + 1) * HD] = a


def project_kernel(o_hbm, st_hbm, w, wlo, whi, out, o, st, px, sx, pz, sz, mz, nz, rz, tz, mx, nx, rx, tx_s, attg, w_s, ct, cr, acc, zt, zr,
                   a_s, a_r, b_s, b_r, c_s, c_r, d_s, d_r, gs, gr, cs, crs, zs, zrs, lsem):
    z, x, y = coords()
    t = lax.axis_index("tp")
    h, k = t // 2, t % 2
    dev = lambda z, x, y: {"ctx": ctx_of(z, x, y)}
    zdev = lambda b, zh: {"ctx": ctx_of(b, x, y), "tp": zh * 2 + k}
    zp = 1 - z
    xr, xl, yr, yl = (x + 1) % 4, (x + 3) % 4, (y + 1) % 4, (y + 3) % 4
    core = {"tp": h * 2 + 1 - k}
    to_yr, to_yl, to_xr, to_xl = dev(z, x, yr), dev(z, x, yl), dev(z, xr, y), dev(z, xl, y)
    to_z = dev(zp, x, y)
    to_x = lambda d: dev(z, (x + d) % 4, y)
    ready = [pltpu.make_async_copy(o_hbm, o, lsem.at[3]), pltpu.make_async_copy(st_hbm.at[pl.ds(0, 2)], st, lsem.at[4])]
    for cp in ready:
        cp.start()
    greet([to_xr, to_xl, to_x(2), to_z, to_yr, to_yl, core, zdev(0, 1 - h), zdev(1, 1 - h)])
    lo, hi = pl.ds(0, 32), pl.ds(32, 32)
    outs = []

    for cp in ready:
        cp.wait()
    for d in (2, 1, 3, 0):
        xx = (x + d) % 4
        outs.append(send(st.at[zp, xx, hi], sz.at[xx], (b_s.at[1], b_r.at[1]), d, to_z))
        outs.append(send(o.at[zp, xx, hi], pz.at[xx], (b_s.at[0], b_r.at[0]), d, to_z))
    for d in (2, 1, 3):
        xx = (x + d) % 4
        outs.append(send(st.at[:, xx, lo], sx.at[x], (a_s.at[1], a_r.at[1]), d, to_x(d)))
        outs.append(send(o.at[:, xx, lo], px.at[x], (a_s.at[0], a_r.at[0]), d, to_x(d)))
    weights = [pltpu.make_async_copy(w, w_s.at[z], lsem.at[0]),
               pltpu.make_async_copy(wlo, w_s.at[zp, pl.ds(0, WROWS)], lsem.at[1]),
               pltpu.make_async_copy(whi, w_s.at[zp, pl.ds(WROWS, WMID - WROWS)], lsem.at[2])]
    for cp in weights:
        cp.start()
    for d in (2, 1, 3, 0):
        xx = (x + d) % 4
        arrive(sz.at[xx], (b_s.at[1], b_r.at[1]), d, to_z)
        arrive(pz.at[xx], (b_s.at[0], b_r.at[0]), d, to_z)
        cols, lse = merge([o[z, xx, 32:64, :], pz[xx]], [st[z, xx, 32:64, :], sz[xx]])
        if d == 0:
            put(rx.at[x], cols)
            tx_s[x] = lse
        else:
            put(mx.at[d - 1], cols)
            nx[d - 1] = lse
            outs.append(send(nx.at[d - 1], tx_s.at[x], (d_s.at[1], d_r.at[1]), d, to_x(d)))
            outs.append(send(mx.at[d - 1], rx.at[x], (d_s.at[0], d_r.at[0]), d, to_x(d)))
    for d in (2, 1, 3):
        xx = (x + 4 - d) % 4
        arrive(sx.at[xx], (a_s.at[1], a_r.at[1]), d, to_x(4 - d))
        arrive(px.at[xx], (a_s.at[0], a_r.at[0]), d, to_x(4 - d))
    others = [(x + d) % 4 for d in (1, 2, 3)]
    cols, lse = merge([o[zp, x, 0:32, :]] + [px[xx, zp] for xx in others],
                      [st[zp, x, 0:32, :]] + [sx[xx, zp] for xx in others])
    put(mz, cols)
    nz[...] = lse
    outs.append(send(nz, tz, (c_s, c_r), 1, to_z))
    outs.append(send(mz, rz, (c_s, c_r), 0, to_z))
    weights[0].wait()
    far = pl.ds(WMID, 2048 - WMID)
    outs.append(send(w_s.at[z, far], w_s.at[z, far], (c_s, c_r), 2, to_z))
    own_cols, own_lse = merge([o[z, x, 0:32, :]] + [px[xx, z] for xx in others],
                              [st[z, x, 0:32, :]] + [sx[xx, z] for xx in others])
    mine = x * 4 + y
    put(attg.at[mine, lo], own_cols)
    arrive(tz, (c_s, c_r), 1, to_z)
    arrive(rz, (c_s, c_r), 0, to_z)
    cols, _ = merge([attg[mine, 0:32, :], rz[...]], [own_lse, tz[...]])
    put(attg.at[mine, lo], cols)

    slot = lambda x, y: x * 4 + y

    def block(hf, a, b, part=None):
        s = slot((x + a) % 4, (y + b) % 4) if hf == 0 else slot((x + b) % 4, (y + a) % 4)
        return attg.at[s, pl.ds(32 * hf, 32) if part is None else pl.ds(32 * hf + 16 * part, 16)]

    def ways(hf, stage):
        return (to_xr, to_xl) if (hf == 0) == (stage == 0) else (to_yr, to_yl)

    def both(hf, stage, a, i):
        right, left = ways(hf, stage)
        ref = block(hf, a, 0)
        outs.append(send(ref, ref, (gs.at[hf], gr.at[hf]), i, right))
        outs.append(send(ref, ref, (gs.at[hf], gr.at[hf]), i + 1, left))

    def at(stage, a, n):
        return (n, 0) if stage == 0 else (a, n)

    def relay(hf, stage, a, i):
        right, left = ways(hf, stage)
        arrive(block(hf, *at(stage, a, 3)), (gs.at[hf], gr.at[hf]), i, left)
        ref = block(hf, *at(stage, a, 3), part=0)
        outs.append(send(ref, ref, (gs.at[hf], gr.at[hf]), i + 2, right))
        arrive(block(hf, *at(stage, a, 1)), (gs.at[hf], gr.at[hf]), i + 1, right)
        ref = block(hf, *at(stage, a, 1), part=1)
        outs.append(send(ref, ref, (gs.at[hf], gr.at[hf]), i + 3, left))

    def last(hf, stage, a, i):
        right, left = ways(hf, stage)
        arrive(block(hf, *at(stage, a, 2), part=0), (gs.at[hf], gr.at[hf]), i + 2, left)
        arrive(block(hf, *at(stage, a, 2), part=1), (gs.at[hf], gr.at[hf]), i + 3, right)

    both(0, 0, 0, 0)
    both(0, 1, 0, 4)
    for d in (2, 1, 3):
        xx = (x + 4 - d) % 4
        arrive(tx_s.at[xx], (d_s.at[1], d_r.at[1]), d, to_x(4 - d))
        arrive(rx.at[xx], (d_s.at[0], d_r.at[0]), d, to_x(4 - d))
    cols, _ = merge([rx[i] for i in range(4)], [tx_s[i] for i in range(4)])
    put(attg.at[mine, hi], cols)
    both(1, 0, 0, 0)
    both(1, 1, 0, 4)
    for hf in (0, 1):
        relay(hf, 0, 0, 0)
        both(hf, 1, 3, 8)
        both(hf, 1, 1, 12)
    for hf in (0, 1):
        last(hf, 0, 0, 0)
        both(hf, 1, 2, 16)

    near, sides, beyond = (0,), (1, 3), (2,)
    pieces = [(0, near), (0, sides), (1, 1), (1, 0), (0, beyond)]
    counts = [64, 128, 128, 128, 64]

    def places(p, kk):
        hf, what = pieces[p]
        if hf == 0:
            return [(2 * kk + i, (y + n) % 4) for i in (0, 1) for n in what]
        return [(2 * kk + (x + what) % 2, n) for n in range(4)]

    def rows_of(hf, blocks):
        return [attg[slot(*s), 32 * hf:32 * hf + 32, :] for s in blocks]

    def product(lhs, b):
        return jnp.dot(jnp.concatenate(lhs, axis=0), w_s[b], preferred_element_type=jnp.float32)

    mine_at = lambda b: (h == z) & (b == z)
    part_of = lambda p: pl.ds(0, counts[p])

    def to_core(p):
        outs.append(send(ct.at[p, :, part_of(p)], cr.at[p, :, part_of(p)], (cs, crs), p, core))

    def multiply(p):
        n = counts[p]
        lhs = rows_of(pieces[p][0], places(p, 1 - k) + places(p, k))
        for b in (0, 1):
            r = product(lhs, b)
            ct[p, b, :n] = r[:n].astype(jnp.bfloat16)
            acc[p, b, :n] = r[n:]
        to_core(p)

    def exchange(p):
        n = counts[p]
        arrive(cr.at[p, :, part_of(p)], (cs, crs), p, core)
        for b in (0, 1):
            zt[p, b, :n] = (acc[p, b, :n] + cr[p, b, :n].astype(jnp.float32)).astype(jnp.bfloat16)

            @pl.when(jnp.logical_not(mine_at(b)))
            def _():
                send(zt.at[p, b, part_of(p)], zr.at[h, p, part_of(p)], (zs, zrs.at[h]), p * 2 + b, zdev(b, z))

            @pl.when(mine_at(b))
            def _():
                zr[h, p, :n] = zt[p, b, :n]

    for hf in (0, 1):
        relay(hf, 1, 0, 4)
    for cp in weights[1:]:
        cp.wait()
    arrive(w_s.at[zp, far], (c_s, c_r), 2, to_z)
    lhs = rows_of(0, places(0, 1 - k) + places(0, k)) + rows_of(1, [(x, n) for n in range(4)])
    for b in (0, 1):
        r = product(lhs, b)
        ct[0, b, :64] = r[:64].astype(jnp.bfloat16)
        acc[0, b, :64] = r[64:128]
        acc[3, b] = r[128:]
    to_core(0)
    for hf in (0, 1):
        relay(hf, 1, 3, 8)
    for hf in (0, 1):
        relay(hf, 1, 1, 12)
    exchange(0)
    for hf in (0, 1):
        relay(hf, 1, 2, 16)
    multiply(1)
    multiply(2)
    exchange(1)
    exchange(2)
    for hf in (0, 1):
        for a, i in ((0, 4), (3, 8), (1, 12), (2, 16)):
            last(hf, 1, a, i)
    here = (x // 2) == k
    lhs = rows_of(0, places(4, 1 - k) + places(4, k)) + rows_of(1, [((x + 2) % 4, n) for n in range(4)])
    for b in (0, 1):
        r = product(lhs, b)
        ct[4, b, :64] = r[:64].astype(jnp.bfloat16)
        acc[4, b, :64] = r[64:128]
        early, late = acc[3, b], r[128:]
        ct[3, b] = jnp.where(here, late, early).astype(jnp.bfloat16)
        acc[3, b] = jnp.where(here, early, late)
    to_core(3)
    to_core(4)
    exchange(3)
    exchange(4)
    for p in range(5):
        n = counts[p]
        for s in (0, 1):
            @pl.when(jnp.logical_not((s == h) & (z == h)))
            def _():
                pltpu.make_async_remote_copy(
                    src_ref=zr.at[s, p, part_of(p)], dst_ref=zr.at[s, p, part_of(p)], send_sem=zs.at[0],
                    recv_sem=zrs.at[s, p * 2 + z], device_id=zdev(h, s), device_id_type=MESH).wait_recv()
        total = (zr[0, p, :n].astype(jnp.float32) + zr[1, p, :n].astype(jnp.float32)).astype(jnp.bfloat16)
        for i, (xx, yy) in enumerate(places(p, k)):
            off = (slot(xx, yy) - 8 * k) * 64 + 32 * pieces[p][0]
            out[pl.ds(pl.multiple_of(off, 32), 32), :] = total[32 * i:32 * i + 32]
    for p in range(5):
        for b in (0, 1):
            @pl.when(jnp.logical_not(mine_at(b)))
            def _():
                pltpu.make_async_remote_copy(
                    src_ref=zt.at[p, b, part_of(p)], dst_ref=zt.at[p, b, part_of(p)], send_sem=zs.at[p * 2 + b],
                    recv_sem=zrs.at[0, 0], device_id=zdev(b, z), device_id_type=MESH).wait_send()
    for cp in outs:
        cp.wait_send()


def project(o, st, w, wlo, whi):
    hbm, vmem = pl.BlockSpec(memory_space=pl.ANY), pl.BlockSpec(memory_space=pltpu.VMEM)
    dma = pltpu.SemaphoreType.DMA
    bf, f32 = jnp.bfloat16, jnp.float32
    wide = HEADS * HD
    return pl.pallas_call(
        project_kernel,
        in_specs=[hbm] * 5,
        out_specs=vmem,
        out_shape=jax.ShapeDtypeStruct((512, 512), bf),
        scratch_shapes=[
            pltpu.VMEM((2, 4, ROWS, wide), bf), pltpu.VMEM((2, 4, ROWS, 128), f32),
            pltpu.VMEM((4, 2, 32, wide), bf), pltpu.VMEM((4, 2, 32, 128), f32),
            pltpu.VMEM((4, 32, wide), bf), pltpu.VMEM((4, 32, 128), f32),
            pltpu.VMEM((32, wide), bf), pltpu.VMEM((32, 128), f32),
            pltpu.VMEM((32, wide), bf), pltpu.VMEM((32, 128), f32),
            pltpu.VMEM((3, 32, wide), bf), pltpu.VMEM((3, 32, 128), f32),
            pltpu.VMEM((4, 32, wide), bf), pltpu.VMEM((4, 32, 128), f32),
            pltpu.VMEM((16, ROWS, wide), bf), pltpu.VMEM((2, 2048, 512), bf),
            pltpu.VMEM((5, 2, 128, 512), bf), pltpu.VMEM((5, 2, 128, 512), bf), pltpu.VMEM((5, 2, 128, 512), f32),
            pltpu.VMEM((5, 2, 128, 512), bf), pltpu.VMEM((2, 5, 128, 512), bf),
            dma((2, 4)), dma((2, 4)), dma((2, 4)), dma((2, 4)), dma((3,)), dma((3,)), dma((2, 4)), dma((2, 4)),
            dma((2, 20)), dma((2, 20)), dma((5,)), dma((5,)), dma((10,)), dma((2, 10)), dma((5,)),
        ],
        compiler_params=pltpu.CompilerParams(collective_id=1, has_side_effects=True, vmem_limit_bytes=53 << 20),
        name="project",
    )(o, st, w, wlo, whi)


def shards(new_queries, new_keys, new_values, cache_keys, cache_values, out_weight, cache_docs, new_docs, slot_tile):
    qg, kvg, wlo, rest = gather(new_queries, cache_keys, cache_values, new_keys, new_values, out_weight)
    whi = lax.ppermute(rest, "ctx", [(i, i ^ 16) for i in range(32)])
    place = jnp.reshape(lax.axis_index("ctx"), (1,)).astype(jnp.int32)
    o, st = attention(qg, kvg.reshape(4 * MEM, HD), cache_docs, new_docs, slot_tile, place)
    return project(o.reshape(2, 4, ROWS, HEADS * HD), st.reshape(6, 4, ROWS, 128), out_weight, wlo, whi)


def solution(mesh):
    return jax.shard_map(
        shards,
        mesh=mesh,
        in_specs=(
            P("ctx", "tp"),
            P("ctx", "tp"),
            P("ctx", "tp"),
            P("ctx", "tp"),
            P("ctx", "tp"),
            P("tp", "ctx"),
            P(),
            P(),
            P(),
        ),
        out_specs=P("tp", "ctx"),
        check_vma=False,
    )
```

```python
import functools
import jax, jax.numpy as jnp
from jax import lax
from jax.experimental import pallas as pl
from jax.experimental.pallas import tpu as pltpu
from jax.sharding import PartitionSpec as P

HD=128; BLK=128; NEG=-1e30
SCALE=HD**-0.5
L2E=1.4426950408889634
ROWS=64; HEADS=16; CR=1024; HALF=CR+ROWS; MEM=2*HALF
SUB=1024

def attn_kernel(cdocs, ndocs, tiles, place, q_hbm, kv_hbm, o_hbm, st_hbm, q_ref, kv_ref, o_ref, st_ref,
                q_s, m_s, l_s, acc_s, top_s, lst, cnt, sems, *, nb):
    q_in = lambda g: pltpu.make_async_copy(q_hbm.at[g], q_ref.at[g], sems.at[0, g])
    o_out = lambda g: pltpu.make_async_copy(o_ref.at[g], o_hbm.at[g], sems.at[1, g])
    kv_in = pltpu.make_async_copy(kv_hbm, kv_ref, sems.at[2, 0])
    st_out = pltpu.make_async_copy(st_ref, st_hbm.at[pl.ds(0, 8)], sems.at[2, 1])
    kv_in.start()
    for g in range(8):
        q_in(g).start()
    c = place[0]
    y = c % 4
    for d in range(4):
        cnt[d] = 0

    def add(i, _):
        d = cdocs[(c - y) * 8 + i]
        n = cnt[d]
        lst[d * 32 + n] = (i // 8) * MEM + (i % 8) * BLK
        cnt[d] = n + 1
        return 0
    lax.fori_loop(0, 32, add, 0)
    top_s[...] = jnp.zeros_like(top_s)
    kv_in.wait()

    def run(g, careful):
        attend_run(g, c, careful, cnt, ndocs, tiles, q_ref, kv_ref, o_ref, st_ref, q_s, m_s, l_s, acc_s, top_s, lst, nb)
        o_out(g).start()

    def fast(g, _):
        q_in(g).wait()
        run(g, False)
        return 0
    lax.fori_loop(0, 8, fast, 0)

    @pl.when(jnp.logical_not(jnp.max(top_s[...]) < 1e30))
    def _():
        def again(g, _):
            o_out(g).wait()
            run(g, True)
            return 0
        lax.fori_loop(0, 8, again, 0)
    st_out.start()
    for g in range(8):
        o_out(g).wait()
    st_out.wait()


def attend_run(g, c, careful, cnt, ndocs, tiles, q_ref, kv_ref, o_ref, st_ref, q_s, m_s, l_s, acc_s, top_s, lst, nb):
    y = c % 4
    src = g * 4 + y
    members = [c - y + i for i in range(4)]
    tq = tiles[src]
    qd = ndocs[tq // 2]
    nrow = ROWS*HEADS
    for h in range(HEADS):
        part = q_ref[g, :, h*HD:(h+1)*HD]
        q_s[h*ROWS:(h+1)*ROWS, :HD] = part
        q_s[h*ROWS:(h+1)*ROWS, HD:] = part
    if careful:
        m_s[...] = jnp.full_like(m_s, NEG)
    l_s[...] = jnp.zeros_like(l_s)
    acc_s[...] = jnp.zeros_like(acc_s)
    n = cnt[qd]
    first = qd * 32

    def scores(kc, masked):
        k2 = jnp.concatenate([kc, jnp.broadcast_to(-base, kc.shape)], axis=1)
        s = lax.dot_general(q_s[...], k2, (((1,),(1,)),((),())), preferred_element_type=jnp.float32)
        tiles_of = [s[:, i*128:(i+1)*128] for i in range(s.shape[1]//128)]
        return tiles_of[:-2] + mask(tiles_of[-2:]) if masked else tiles_of

    def step(kc, vc, masked):
        s = scores(kc, masked)
        if careful:
            m_old = m_s[...]
            m = jnp.maximum(m_old, jnp.max(functools.reduce(jnp.maximum, s), axis=1, keepdims=True))
            alpha = jnp.exp2((m_old - m)*(SCALE*L2E))
            l_s[...] = l_s[...]*alpha
            acc_s[...] = acc_s[...]*alpha
            m_s[...] = m
            s = [a - m for a in s]
        p = [jnp.exp2(a*(SCALE*L2E)) for a in s]
        l_s[...] = l_s[...] + functools.reduce(jnp.add, p)
        pb = jnp.concatenate([a.astype(jnp.bfloat16) for a in p], axis=1)
        acc_s[...] = acc_s[...] + jnp.dot(pb, vc, preferred_element_type=jnp.float32)

    def at(off, rows=BLK):
        return kv_ref[pl.ds(pl.multiple_of(off, 64), rows), :]

    newlims = []
    new_k, new_v = [], []
    for mi, cm in enumerate(members):
        tk = tiles[cm]
        full_ok = (ndocs[tk // 2] == qd) & (tk < tq)
        diag = tk == tq
        newlims.append((jnp.where(full_ok, 1 << 20, jnp.where(diag, 0, -1)), jnp.where(diag, 1, 0)))
        new_k.append(kv_ref[mi*MEM + CR: mi*MEM + HALF, :])
        new_v.append(kv_ref[mi*MEM + HALF + CR: (mi+1)*MEM, :])
    any_new = functools.reduce(jnp.logical_or, [lim >= 0 for lim, _ in newlims])
    where = jnp.int32(0)
    for mi in range(4):
        where = jnp.where(newlims[mi][0] >= 0, mi*MEM + CR, where)
    where = jnp.where(n > 0, lst[first], where)
    base = at(where, 16)[0:1, :]

    def mask(pair):
        row = lax.broadcasted_iota(jnp.int32, (ROWS, 128), 0)
        lane = lax.broadcasted_iota(jnp.int32, (ROWS, 128), 1)
        out = []
        for a in range(2):
            (b0, d0), (b1, d1) = newlims[2*a], newlims[2*a+1]
            ok = lane <= jnp.where(lane < ROWS, row*d0 + b0, row*d1 + b1 + ROWS)
            bias = jnp.where(ok, 0.0, NEG)
            out.append((pair[a].reshape(HEADS, ROWS, 128) + bias[None]).reshape(nrow, 128))
        return out

    def chunk(base, size, with_new=False):
        offs = [lst[first + base + j] for j in range(size)]
        kc = jnp.concatenate([at(o) for o in offs] + (new_k if with_new else []), axis=0)
        vc = jnp.concatenate([at(o + HALF) for o in offs] + (new_v if with_new else []), axis=0)
        step(kc, vc, with_new)

    if careful:
        def body(i, _):
            chunk(i, 1)
            return 0
        lax.fori_loop(0, n, body, 0)

        @pl.when(any_new)
        def _():
            chunk(0, 0, True)
    else:
        def body(i, _):
            chunk(i*2*nb, 2*nb)
            return 0
        lax.fori_loop(0, n // (2*nb), body, 0)

        @pl.when((n // nb) % 2 == 1)
        def _():
            chunk(n // (2*nb) * (2*nb), nb)
        for left in range(nb):
            @pl.when(any_new & (n % nb == left))
            def _(left=left):
                chunk(n - left, left, True)

            if left:
                @pl.when(jnp.logical_not(any_new) & (n % nb == left))
                def _(left=left):
                    chunk(n - left, left)
    lane = lax.broadcasted_iota(jnp.int32, (ROWS, 128), 1)
    st = jnp.full((ROWS, 128), NEG, jnp.float32)
    top = top_s[...]
    peaks = lax.dot_general(q_s[:, :HD], jnp.broadcast_to(base, (128, HD)), (((1,),(1,)),((),())),
                            preferred_element_type=jnp.float32)
    for h in range(HEADS):
        r = pl.ds(h*ROWS, ROWS)
        l = jnp.sum(l_s[r, :], axis=1, keepdims=True)
        top = jnp.maximum(top, l)
        some = l > 0.0
        l = jnp.where(some, l, 1.0)
        o_ref[g, :, h*HD:(h+1)*HD] = (acc_s[r, :] * (1.0 / l)).astype(jnp.bfloat16)
        peak = peaks[h*ROWS:(h+1)*ROWS]
        if careful:
            peak = peak + m_s[r, :]
        st = jnp.where(lane == h, jnp.where(some, peak*SCALE + jnp.log(l), NEG), st)
    st_ref[g] = st
    top_s[...] = top


def attention(qg, kvg, cdocs, ndocs, tiles, place, nb=4):
    nrow = ROWS*HEADS
    smem, anywhere = pl.BlockSpec(memory_space=pltpu.SMEM), pl.BlockSpec(memory_space=pl.ANY)
    return pl.pallas_call(
        functools.partial(attn_kernel, nb=nb),
        in_specs=[smem] * 4 + [anywhere] * 2,
        out_specs=[anywhere] * 2,
        scratch_shapes=[pltpu.VMEM((8, ROWS, HEADS*HD), jnp.bfloat16), pltpu.VMEM((4*MEM, HD), jnp.bfloat16),
                        pltpu.VMEM((8, ROWS, HEADS*HD), jnp.bfloat16), pltpu.VMEM((8, ROWS, 128), jnp.float32),
                        pltpu.VMEM((nrow, 2*HD), jnp.bfloat16), pltpu.VMEM((nrow, 128), jnp.float32),
                        pltpu.VMEM((nrow, 128), jnp.float32), pltpu.VMEM((nrow, HD), jnp.float32),
                        pltpu.VMEM((ROWS, 128), jnp.float32),
                        pltpu.SMEM((128,), jnp.int32), pltpu.SMEM((4,), jnp.int32), pltpu.SemaphoreType.DMA((3, 8))],
        out_shape=[jax.ShapeDtypeStruct((8, ROWS, HEADS*HD), jnp.bfloat16),
                   jax.ShapeDtypeStruct((24, ROWS, 128), jnp.float32)],
        compiler_params=pltpu.CompilerParams(vmem_limit_bytes=(64 << 20) - (512 << 10)),
        name="attention",
    )(cdocs, ndocs, tiles, place, qg, kvg)


MESH = pl.DeviceIdType.MESH
WROWS = 512
WMID = 1600


def coords():
    c = lax.axis_index("ctx")
    return c // 16, (c // 4) % 4, c % 4


def ctx_of(z, x, y):
    return z * 16 + x * 4 + y


def send(src, dst, sems, i, device):
    copy = pltpu.make_async_remote_copy(
        src_ref=src, dst_ref=dst, send_sem=sems[0].at[i], recv_sem=sems[1].at[i],
        device_id=device, device_id_type=MESH)
    copy.start()
    return copy


def arrive(ref, sems, i, device):
    pltpu.make_async_remote_copy(
        src_ref=ref, dst_ref=ref, send_sem=sems[0].at[i], recv_sem=sems[1].at[i],
        device_id=device, device_id_type=MESH).wait_recv()


def greet(peers):
    barrier = pltpu.get_barrier_semaphore()
    for device in peers:
        pl.semaphore_signal(barrier, inc=1, device_id=device, device_id_type=MESH)
    pl.semaphore_wait(barrier, len(peers))


def gather_kernel(q, ck, cv, nk, nv, w, q_out, kv_out, w_out, rest_out, qg, kvg, wg, wr, ws, ssem, rsem, lsem, osem):
    z, x, y = coords()
    sems = (ssem, rsem)
    zp = 1 - z
    xr, xl, yr, yl = (x + 1) % 4, (x + 3) % 4, (y + 1) % 4, (y + 3) % 4
    x2, y2 = (x + 2) % 4, (y + 2) % 4
    dev = lambda z, x, y: {"ctx": ctx_of(z, x, y)}
    to_yr, to_yl, to_xr, to_xl, to_z = dev(z, x, yr), dev(z, x, yl), dev(z, xr, y), dev(z, xl, y), dev(zp, x, y)
    slot = lambda z, x: z * 4 + x
    me = slot(z, x)
    out = []
    pieces = [(ck, 0, CR), (nk, CR, ROWS), (cv, HALF, CR), (nv, HALF + CR, ROWS)]
    locs = [pltpu.make_async_copy(q, qg.at[me], lsem.at[0])]
    for i, (src, off, n) in enumerate(pieces):
        locs.append(pltpu.make_async_copy(src, kvg.at[y, pl.ds(off, n)], lsem.at[1 + i]))
    locs.append(pltpu.make_async_copy(w.at[pl.ds(0, WROWS)], ws, lsem.at[5]))
    locs.append(pltpu.make_async_copy(w.at[pl.ds(WROWS, WMID - WROWS)], wr, lsem.at[6]))
    for cp in locs:
        cp.start()
    greet([to_yr, to_yl, to_xr, to_xl, to_z])
    kh, vh = pl.ds(0, HALF), pl.ds(HALF, HALF)
    saves = []

    def save(src, dst):
        saves.append(pltpu.make_async_copy(src, dst, osem.at[len(saves)]))
        saves[-1].start()

    locs[0].wait()
    out.append(send(qg.at[me], qg.at[me], sems, 0, to_z))
    out.append(send(qg.at[me], qg.at[me], sems, 9, to_xr))
    out.append(send(qg.at[me], qg.at[me], sems, 10, to_xl))
    for cp in locs[1:5]:
        cp.wait()
    out.append(send(kvg.at[y, kh], kvg.at[y, kh], sems, 1, to_yr))
    out.append(send(kvg.at[y, vh], kvg.at[y, vh], sems, 2, to_yl))
    out.append(send(kvg.at[y, vh], kvg.at[y, vh], sems, 3, to_yr))
    out.append(send(kvg.at[y, kh], kvg.at[y, kh], sems, 4, to_yl))
    locs[5].wait()
    out.append(send(ws, wg, sems, 19, to_z))
    save(qg.at[me], q_out.at[me])
    save(kvg.at[y], kv_out.at[y])
    locs[6].wait()
    save(wr, rest_out)
    other = slot(zp, x)
    arrive(qg.at[other], sems, 0, to_z)
    out.append(send(qg.at[other], qg.at[other], sems, 11, to_xr))
    out.append(send(qg.at[other], qg.at[other], sems, 12, to_xl))
    save(qg.at[other], q_out.at[other])
    lo, hi = pl.ds(0, 32), pl.ds(32, 32)
    arrive(qg.at[slot(z, xl)], sems, 9, to_xl)
    out.append(send(qg.at[slot(z, xl), lo], qg.at[slot(z, xl), lo], sems, 13, to_xr))
    save(qg.at[slot(z, xl)], q_out.at[slot(z, xl)])
    arrive(qg.at[slot(z, xr)], sems, 10, to_xr)
    out.append(send(qg.at[slot(z, xr), hi], qg.at[slot(z, xr), hi], sems, 14, to_xl))
    save(qg.at[slot(z, xr)], q_out.at[slot(z, xr)])
    arrive(kvg.at[yl, kh], sems, 1, to_yl)
    out.append(send(kvg.at[yl, kh], kvg.at[yl, kh], sems, 17, to_yr))
    arrive(kvg.at[yr, vh], sems, 2, to_yr)
    out.append(send(kvg.at[yr, vh], kvg.at[yr, vh], sems, 18, to_yl))
    arrive(qg.at[slot(zp, xl)], sems, 11, to_xl)
    out.append(send(qg.at[slot(zp, xl), lo], qg.at[slot(zp, xl), lo], sems, 15, to_xr))
    save(qg.at[slot(zp, xl)], q_out.at[slot(zp, xl)])
    arrive(qg.at[slot(zp, xr)], sems, 12, to_xr)
    out.append(send(qg.at[slot(zp, xr), hi], qg.at[slot(zp, xr), hi], sems, 16, to_xl))
    save(qg.at[slot(zp, xr)], q_out.at[slot(zp, xr)])
    arrive(kvg.at[yl, vh], sems, 3, to_yl)
    arrive(kvg.at[yr, kh], sems, 4, to_yr)
    save(kvg.at[yl], kv_out.at[yl])
    save(kvg.at[yr], kv_out.at[yr])
    arrive(qg.at[slot(z, x2), lo], sems, 13, to_xl)
    arrive(qg.at[slot(z, x2), hi], sems, 14, to_xr)
    save(qg.at[slot(z, x2)], q_out.at[slot(z, x2)])
    arrive(qg.at[slot(zp, x2), lo], sems, 15, to_xl)
    arrive(qg.at[slot(zp, x2), hi], sems, 16, to_xr)
    save(qg.at[slot(zp, x2)], q_out.at[slot(zp, x2)])
    arrive(kvg.at[y2, kh], sems, 17, to_yl)
    arrive(kvg.at[y2, vh], sems, 18, to_yr)
    save(kvg.at[y2], kv_out.at[y2])
    arrive(wg, sems, 19, to_z)
    save(wg, w_out)
    for cp in saves:
        cp.wait()
    for cp in out:
        cp.wait_send()


def gather(q, ck, cv, nk, nv, w):
    hbm, bf = pl.BlockSpec(memory_space=pl.ANY), jnp.bfloat16
    return pl.pallas_call(
        gather_kernel,
        in_specs=[hbm] * 6,
        out_specs=[hbm] * 4,
        out_shape=[jax.ShapeDtypeStruct((8, ROWS, HEADS * HD), jnp.bfloat16),
                   jax.ShapeDtypeStruct((4, MEM, HD), jnp.bfloat16),
                   jax.ShapeDtypeStruct((WROWS, 512), jnp.bfloat16),
                   jax.ShapeDtypeStruct((WMID - WROWS, 512), jnp.bfloat16)],
        scratch_shapes=[pltpu.VMEM((8, ROWS, HEADS * HD), bf), pltpu.VMEM((4, MEM, HD), bf), pltpu.VMEM((WROWS, 512), bf),
                        pltpu.VMEM((WMID - WROWS, 512), bf), pltpu.VMEM((WROWS, 512), bf), pltpu.SemaphoreType.DMA((20,)),
                        pltpu.SemaphoreType.DMA((20,)), pltpu.SemaphoreType.DMA((7,)), pltpu.SemaphoreType.DMA((14,))],
        compiler_params=pltpu.CompilerParams(collective_id=0, has_side_effects=True, vmem_limit_bytes=56 << 20),
        name="gather",
    )(q, ck, cv, nk, nv, w)


def merge(parts, stats):
    largest = functools.reduce(jnp.maximum, stats)
    e = [jnp.exp(s - largest) for s in stats]
    total = functools.reduce(jnp.add, e)
    inverse = 1.0 / total
    e = [a * inverse for a in e]
    cols = []
    for head in range(HEADS):
        a = None
        for weight, part in zip(e, parts):
            term = weight[:, head:head + 1] * part[:, head * HD:(head + 1) * HD].astype(jnp.float32)
            a = term if a is None else a + term
        cols.append(a.astype(jnp.bfloat16))
    return cols, largest + jnp.log(total)


def put(ref, cols):
    for head, a in enumerate(cols):
        ref[:, head * HD:(head + 1) * HD] = a


def project_kernel(o_hbm, st_hbm, w, wlo, whi, out, o, st, px, sx, pz, sz, mz, nz, rz, tz, mx, nx, rx, tx_s, attg, w_s, ct, cr, acc, zt, zr,
                   a_s, a_r, b_s, b_r, c_s, c_r, d_s, d_r, gs, gr, cs, crs, zs, zrs, lsem):
    z, x, y = coords()
    t = lax.axis_index("tp")
    h, k = t // 2, t % 2
    dev = lambda z, x, y: {"ctx": ctx_of(z, x, y)}
    zdev = lambda b, zh: {"ctx": ctx_of(b, x, y), "tp": zh * 2 + k}
    zp = 1 - z
    xr, xl, yr, yl = (x + 1) % 4, (x + 3) % 4, (y + 1) % 4, (y + 3) % 4
    core = {"tp": h * 2 + 1 - k}
    to_yr, to_yl, to_xr, to_xl = dev(z, x, yr), dev(z, x, yl), dev(z, xr, y), dev(z, xl, y)
    to_z = dev(zp, x, y)
    to_x = lambda d: dev(z, (x + d) % 4, y)
    ready = [pltpu.make_async_copy(o_hbm, o, lsem.at[3]), pltpu.make_async_copy(st_hbm.at[pl.ds(0, 2)], st, lsem.at[4])]
    for cp in ready:
        cp.start()
    greet([to_xr, to_xl, to_x(2), to_z, to_yr, to_yl, core, zdev(0, 1 - h), zdev(1, 1 - h)])
    lo, hi = pl.ds(0, 32), pl.ds(32, 32)
    outs = []

    for cp in ready:
        cp.wait()
    for d in (2, 1, 3, 0):
        xx = (x + d) % 4
        outs.append(send(st.at[zp, xx, hi], sz.at[xx], (b_s.at[1], b_r.at[1]), d, to_z))
        outs.append(send(o.at[zp, xx, hi], pz.at[xx], (b_s.at[0], b_r.at[0]), d, to_z))
    for d in (2, 1, 3):
        xx = (x + d) % 4
        outs.append(send(st.at[:, xx, lo], sx.at[x], (a_s.at[1], a_r.at[1]), d, to_x(d)))
        outs.append(send(o.at[:, xx, lo], px.at[x], (a_s.at[0], a_r.at[0]), d, to_x(d)))
    weights = [pltpu.make_async_copy(w, w_s.at[z], lsem.at[0]),
               pltpu.make_async_copy(wlo, w_s.at[zp, pl.ds(0, WROWS)], lsem.at[1]),
               pltpu.make_async_copy(whi, w_s.at[zp, pl.ds(WROWS, WMID - WROWS)], lsem.at[2])]
    for cp in weights:
        cp.start()
    for d in (2, 1, 3, 0):
        xx = (x + d) % 4
        arrive(sz.at[xx], (b_s.at[1], b_r.at[1]), d, to_z)
        arrive(pz.at[xx], (b_s.at[0], b_r.at[0]), d, to_z)
        cols, lse = merge([o[z, xx, 32:64, :], pz[xx]], [st[z, xx, 32:64, :], sz[xx]])
        if d == 0:
            put(rx.at[x], cols)
            tx_s[x] = lse
        else:
            put(mx.at[d - 1], cols)
            nx[d - 1] = lse
            outs.append(send(nx.at[d - 1], tx_s.at[x], (d_s.at[1], d_r.at[1]), d, to_x(d)))
            outs.append(send(mx.at[d - 1], rx.at[x], (d_s.at[0], d_r.at[0]), d, to_x(d)))
    for d in (2, 1, 3):
        xx = (x + 4 - d) % 4
        arrive(sx.at[xx], (a_s.at[1], a_r.at[1]), d, to_x(4 - d))
        arrive(px.at[xx], (a_s.at[0], a_r.at[0]), d, to_x(4 - d))
    others = [(x + d) % 4 for d in (1, 2, 3)]
    cols, lse = merge([o[zp, x, 0:32, :]] + [px[xx, zp] for xx in others],
                      [st[zp, x, 0:32, :]] + [sx[xx, zp] for xx in others])
    put(mz, cols)
    nz[...] = lse
    outs.append(send(nz, tz, (c_s, c_r), 1, to_z))
    outs.append(send(mz, rz, (c_s, c_r), 0, to_z))
    weights[0].wait()
    far = pl.ds(WMID, 2048 - WMID)
    outs.append(send(w_s.at[z, far], w_s.at[z, far], (c_s, c_r), 2, to_z))
    own_cols, own_lse = merge([o[z, x, 0:32, :]] + [px[xx, z] for xx in others],
                              [st[z, x, 0:32, :]] + [sx[xx, z] for xx in others])
    mine = x * 4 + y
    put(attg.at[mine, lo], own_cols)
    arrive(tz, (c_s, c_r), 1, to_z)
    arrive(rz, (c_s, c_r), 0, to_z)
    cols, _ = merge([attg[mine, 0:32, :], rz[...]], [own_lse, tz[...]])
    put(attg.at[mine, lo], cols)

    slot = lambda x, y: x * 4 + y

    def block(hf, a, b, part=None):
        s = slot((x + a) % 4, (y + b) % 4) if hf == 0 else slot((x + b) % 4, (y + a) % 4)
        return attg.at[s, pl.ds(32 * hf, 32) if part is None else pl.ds(32 * hf + 16 * part, 16)]

    def ways(hf, stage):
        return (to_xr, to_xl) if (hf == 0) == (stage == 0) else (to_yr, to_yl)

    def both(hf, stage, a, i):
        right, left = ways(hf, stage)
        ref = block(hf, a, 0)
        outs.append(send(ref, ref, (gs.at[hf], gr.at[hf]), i, right))
        outs.append(send(ref, ref, (gs.at[hf], gr.at[hf]), i + 1, left))

    def at(stage, a, n):
        return (n, 0) if stage == 0 else (a, n)

    def relay(hf, stage, a, i):
        right, left = ways(hf, stage)
        arrive(block(hf, *at(stage, a, 3)), (gs.at[hf], gr.at[hf]), i, left)
        ref = block(hf, *at(stage, a, 3), part=0)
        outs.append(send(ref, ref, (gs.at[hf], gr.at[hf]), i + 2, right))
        arrive(block(hf, *at(stage, a, 1)), (gs.at[hf], gr.at[hf]), i + 1, right)
        ref = block(hf, *at(stage, a, 1), part=1)
        outs.append(send(ref, ref, (gs.at[hf], gr.at[hf]), i + 3, left))

    def last(hf, stage, a, i):
        right, left = ways(hf, stage)
        arrive(block(hf, *at(stage, a, 2), part=0), (gs.at[hf], gr.at[hf]), i + 2, left)
        arrive(block(hf, *at(stage, a, 2), part=1), (gs.at[hf], gr.at[hf]), i + 3, right)

    both(0, 0, 0, 0)
    both(0, 1, 0, 4)
    for d in (2, 1, 3):
        xx = (x + 4 - d) % 4
        arrive(tx_s.at[xx], (d_s.at[1], d_r.at[1]), d, to_x(4 - d))
        arrive(rx.at[xx], (d_s.at[0], d_r.at[0]), d, to_x(4 - d))
    cols, _ = merge([rx[i] for i in range(4)], [tx_s[i] for i in range(4)])
    put(attg.at[mine, hi], cols)
    both(1, 0, 0, 0)
    both(1, 1, 0, 4)
    for hf in (0, 1):
        relay(hf, 0, 0, 0)
        both(hf, 1, 3, 8)
        both(hf, 1, 1, 12)
    for hf in (0, 1):
        last(hf, 0, 0, 0)
        both(hf, 1, 2, 16)

    near, sides, beyond = (0,), (1, 3), (2,)
    pieces = [(0, near), (0, sides), (1, 1), (1, 0), (0, beyond)]
    counts = [64, 128, 128, 128, 64]

    def places(p, kk):
        hf, what = pieces[p]
        if hf == 0:
            return [(2 * kk + i, (y + n) % 4) for i in (0, 1) for n in what]
        return [(2 * kk + (x + what) % 2, n) for n in range(4)]

    def rows_of(hf, blocks):
        return [attg[slot(*s), 32 * hf:32 * hf + 32, :] for s in blocks]

    def product(lhs, b):
        return jnp.dot(jnp.concatenate(lhs, axis=0), w_s[b], preferred_element_type=jnp.float32)

    mine_at = lambda b: (h == z) & (b == z)
    part_of = lambda p: pl.ds(0, counts[p])

    def to_core(p):
        outs.append(send(ct.at[p, :, part_of(p)], cr.at[p, :, part_of(p)], (cs, crs), p, core))

    def multiply(p):
        n = counts[p]
        lhs = rows_of(pieces[p][0], places(p, 1 - k) + places(p, k))
        for b in (0, 1):
            r = product(lhs, b)
            ct[p, b, :n] = r[:n].astype(jnp.bfloat16)
            acc[p, b, :n] = r[n:]
        to_core(p)

    def exchange(p):
        n = counts[p]
        arrive(cr.at[p, :, part_of(p)], (cs, crs), p, core)
        for b in (0, 1):
            zt[p, b, :n] = (acc[p, b, :n] + cr[p, b, :n].astype(jnp.float32)).astype(jnp.bfloat16)

            @pl.when(jnp.logical_not(mine_at(b)))
            def _():
                send(zt.at[p, b, part_of(p)], zr.at[h, p, part_of(p)], (zs, zrs.at[h]), p * 2 + b, zdev(b, z))

            @pl.when(mine_at(b))
            def _():
                zr[h, p, :n] = zt[p, b, :n]

    for hf in (0, 1):
        relay(hf, 1, 0, 4)
    for cp in weights[1:]:
        cp.wait()
    arrive(w_s.at[zp, far], (c_s, c_r), 2, to_z)
    lhs = rows_of(0, places(0, 1 - k) + places(0, k)) + rows_of(1, [(x, n) for n in range(4)])
    for b in (0, 1):
        r = product(lhs, b)
        ct[0, b, :64] = r[:64].astype(jnp.bfloat16)
        acc[0, b, :64] = r[64:128]
        acc[3, b] = r[128:]
    to_core(0)
    for hf in (0, 1):
        relay(hf, 1, 3, 8)
    for hf in (0, 1):
        relay(hf, 1, 1, 12)
    exchange(0)
    for hf in (0, 1):
        relay(hf, 1, 2, 16)
    multiply(1)
    multiply(2)
    exchange(1)
    exchange(2)
    for hf in (0, 1):
        for a, i in ((0, 4), (3, 8), (1, 12), (2, 16)):
            last(hf, 1, a, i)
    here = (x // 2) == k
    lhs = rows_of(0, places(4, 1 - k) + places(4, k)) + rows_of(1, [((x + 2) % 4, n) for n in range(4)])
    for b in (0, 1):
        r = product(lhs, b)
        ct[4, b, :64] = r[:64].astype(jnp.bfloat16)
        acc[4, b, :64] = r[64:128]
        early, late = acc[3, b], r[128:]
        ct[3, b] = jnp.where(here, late, early).astype(jnp.bfloat16)
        acc[3, b] = jnp.where(here, early, late)
    to_core(3)
    to_core(4)
    exchange(3)
    exchange(4)
    for p in range(5):
        n = counts[p]
        for s in (0, 1):
            @pl.when(jnp.logical_not((s == h) & (z == h)))
            def _():
                pltpu.make_async_remote_copy(
                    src_ref=zr.at[s, p, part_of(p)], dst_ref=zr.at[s, p, part_of(p)], send_sem=zs.at[0],
                    recv_sem=zrs.at[s, p * 2 + z], device_id=zdev(h, s), device_id_type=MESH).wait_recv()
        total = (zr[0, p, :n].astype(jnp.float32) + zr[1, p, :n].astype(jnp.float32)).astype(jnp.bfloat16)
        for i, (xx, yy) in enumerate(places(p, k)):
            off = (slot(xx, yy) - 8 * k) * 64 + 32 * pieces[p][0]
            out[pl.ds(pl.multiple_of(off, 32), 32), :] = total[32 * i:32 * i + 32]
    for p in range(5):
        for b in (0, 1):
            @pl.when(jnp.logical_not(mine_at(b)))
            def _():
                pltpu.make_async_remote_copy(
                    src_ref=zt.at[p, b, part_of(p)], dst_ref=zt.at[p, b, part_of(p)], send_sem=zs.at[p * 2 + b],
                    recv_sem=zrs.at[0, 0], device_id=zdev(b, z), device_id_type=MESH).wait_send()
    for cp in outs:
        cp.wait_send()


def project(o, st, w, wlo, whi):
    hbm, vmem = pl.BlockSpec(memory_space=pl.ANY), pl.BlockSpec(memory_space=pltpu.VMEM)
    dma = pltpu.SemaphoreType.DMA
    bf, f32 = jnp.bfloat16, jnp.float32
    wide = HEADS * HD
    return pl.pallas_call(
        project_kernel,
        in_specs=[hbm] * 5,
        out_specs=vmem,
        out_shape=jax.ShapeDtypeStruct((512, 512), bf),
        scratch_shapes=[
            pltpu.VMEM((2, 4, ROWS, wide), bf), pltpu.VMEM((2, 4, ROWS, 128), f32),
            pltpu.VMEM((4, 2, 32, wide), bf), pltpu.VMEM((4, 2, 32, 128), f32),
            pltpu.VMEM((4, 32, wide), bf), pltpu.VMEM((4, 32, 128), f32),
            pltpu.VMEM((32, wide), bf), pltpu.VMEM((32, 128), f32),
            pltpu.VMEM((32, wide), bf), pltpu.VMEM((32, 128), f32),
            pltpu.VMEM((3, 32, wide), bf), pltpu.VMEM((3, 32, 128), f32),
            pltpu.VMEM((4, 32, wide), bf), pltpu.VMEM((4, 32, 128), f32),
            pltpu.VMEM((16, ROWS, wide), bf), pltpu.VMEM((2, 2048, 512), bf),
            pltpu.VMEM((5, 2, 128, 512), bf), pltpu.VMEM((5, 2, 128, 512), bf), pltpu.VMEM((5, 2, 128, 512), f32),
            pltpu.VMEM((5, 2, 128, 512), bf), pltpu.VMEM((2, 5, 128, 512), bf),
            dma((2, 4)), dma((2, 4)), dma((2, 4)), dma((2, 4)), dma((3,)), dma((3,)), dma((2, 4)), dma((2, 4)),
            dma((2, 20)), dma((2, 20)), dma((5,)), dma((5,)), dma((10,)), dma((2, 10)), dma((5,)),
        ],
        compiler_params=pltpu.CompilerParams(collective_id=1, has_side_effects=True, vmem_limit_bytes=53 << 20),
        name="project",
    )(o, st, w, wlo, whi)


def shards(new_queries, new_keys, new_values, cache_keys, cache_values, out_weight, cache_docs, new_docs, slot_tile):
    qg, kvg, wlo, rest = gather(new_queries, cache_keys, cache_values, new_keys, new_values, out_weight)
    whi = lax.ppermute(rest, "ctx", [(i, i ^ 16) for i in range(32)])
    place = jnp.reshape(lax.axis_index("ctx"), (1,)).astype(jnp.int32)
    o, st = attention(qg, kvg.reshape(4 * MEM, HD), cache_docs, new_docs, slot_tile, place)
    return project(o.reshape(2, 4, ROWS, HEADS * HD), st.reshape(6, 4, ROWS, 128), out_weight, wlo, whi)


def solution(mesh):
    return jax.shard_map(
        shards,
        mesh=mesh,
        in_specs=(
            P("ctx", "tp"),
            P("ctx", "tp"),
            P("ctx", "tp"),
            P("ctx", "tp"),
            P("ctx", "tp"),
            P("tp", "ctx"),
            P(),
            P(),
            P(),
        ),
        out_specs=P("tp", "ctx"),
        check_vma=False,
    )
```

```python
import functools
import jax, jax.numpy as jnp
from jax import lax
from jax.experimental import pallas as pl
from jax.experimental.pallas import tpu as pltpu
from jax.sharding import PartitionSpec as P

HD=128; BLK=128; NEG=-1e30
SCALE=HD**-0.5
L2E=1.4426950408889634
ROWS=64; HEADS=16; CR=1024; HALF=CR+ROWS; MEM=2*HALF
SUB=1024

def attn_kernel(cdocs, ndocs, tiles, place, q_hbm, kv_hbm, o_hbm, st_hbm, q_ref, kv_ref, o_ref, st_ref,
                q_s, m_s, l_s, acc_s, top_s, lst, cnt, sems, *, nb):
    q_in = lambda g: pltpu.make_async_copy(q_hbm.at[g], q_ref.at[g], sems.at[0, g])
    o_out = lambda g: pltpu.make_async_copy(o_ref.at[g], o_hbm.at[g], sems.at[1, g])
    kv_in = pltpu.make_async_copy(kv_hbm, kv_ref, sems.at[2, 0])
    st_out = pltpu.make_async_copy(st_ref, st_hbm.at[pl.ds(0, 8)], sems.at[2, 1])
    kv_in.start()
    for g in range(8):
        q_in(g).start()
    c = place[0]
    y = c % 4
    for d in range(4):
        cnt[d] = 0

    def add(i, _):
        d = cdocs[(c - y) * 8 + i]
        n = cnt[d]
        lst[d * 32 + n] = (i // 8) * MEM + (i % 8) * BLK
        cnt[d] = n + 1
        return 0
    lax.fori_loop(0, 32, add, 0)
    top_s[...] = jnp.zeros_like(top_s)
    kv_in.wait()

    def run(g, careful):
        attend_run(g, c, careful, cnt, ndocs, tiles, q_ref, kv_ref, o_ref, st_ref, q_s, m_s, l_s, acc_s, top_s, lst, nb)
        o_out(g).start()

    def fast(g, _):
        q_in(g).wait()
        run(g, False)
        return 0
    lax.fori_loop(0, 8, fast, 0)

    @pl.when(jnp.logical_not(jnp.max(top_s[...]) < 1e30))
    def _():
        def again(g, _):
            o_out(g).wait()
            run(g, True)
            return 0
        lax.fori_loop(0, 8, again, 0)
    st_out.start()
    for g in range(8):
        o_out(g).wait()
    st_out.wait()


def attend_run(g, c, careful, cnt, ndocs, tiles, q_ref, kv_ref, o_ref, st_ref, q_s, m_s, l_s, acc_s, top_s, lst, nb):
    y = c % 4
    src = g * 4 + y
    members = [c - y + i for i in range(4)]
    tq = tiles[src]
    qd = ndocs[tq // 2]
    nrow = ROWS*HEADS
    for h in range(HEADS):
        part = q_ref[g, :, h*HD:(h+1)*HD]
        q_s[h*ROWS:(h+1)*ROWS, :HD] = part
        q_s[h*ROWS:(h+1)*ROWS, HD:] = part
    if careful:
        m_s[...] = jnp.full_like(m_s, NEG)
    l_s[...] = jnp.zeros_like(l_s)
    acc_s[...] = jnp.zeros_like(acc_s)
    n = cnt[qd]
    first = qd * 32

    def scores(kc, masked):
        k2 = jnp.concatenate([kc, jnp.broadcast_to(-base, kc.shape)], axis=1)
        s = lax.dot_general(q_s[...], k2, (((1,),(1,)),((),())), preferred_element_type=jnp.float32)
        tiles_of = [s[:, i*128:(i+1)*128] for i in range(s.shape[1]//128)]
        return tiles_of[:-2] + mask(tiles_of[-2:]) if masked else tiles_of

    def step(kc, vc, masked):
        s = scores(kc, masked)
        if careful:
            m_old = m_s[...]
            m = jnp.maximum(m_old, jnp.max(functools.reduce(jnp.maximum, s), axis=1, keepdims=True))
            alpha = jnp.exp2((m_old - m)*(SCALE*L2E))
            l_s[...] = l_s[...]*alpha
            acc_s[...] = acc_s[...]*alpha
            m_s[...] = m
            s = [a - m for a in s]
        p = [jnp.exp2(a*(SCALE*L2E)) for a in s]
        l_s[...] = l_s[...] + functools.reduce(jnp.add, p)
        pb = jnp.concatenate([a.astype(jnp.bfloat16) for a in p], axis=1)
        acc_s[...] = acc_s[...] + jnp.dot(pb, vc, preferred_element_type=jnp.float32)

    def at(off, rows=BLK):
        return kv_ref[pl.ds(pl.multiple_of(off, 64), rows), :]

    newlims = []
    new_k, new_v = [], []
    for mi, cm in enumerate(members):
        tk = tiles[cm]
        full_ok = (ndocs[tk // 2] == qd) & (tk < tq)
        diag = tk == tq
        newlims.append((jnp.where(full_ok, 1 << 20, jnp.where(diag, 0, -1)), jnp.where(diag, 1, 0)))
        new_k.append(kv_ref[mi*MEM + CR: mi*MEM + HALF, :])
        new_v.append(kv_ref[mi*MEM + HALF + CR: (mi+1)*MEM, :])
    any_new = functools.reduce(jnp.logical_or, [lim >= 0 for lim, _ in newlims])
    where = jnp.int32(0)
    for mi in range(4):
        where = jnp.where(newlims[mi][0] >= 0, mi*MEM + CR, where)
    where = jnp.where(n > 0, lst[first], where)
    base = at(where, 16)[0:1, :]

    def mask(pair):
        row = lax.broadcasted_iota(jnp.int32, (ROWS, 128), 0)
        lane = lax.broadcasted_iota(jnp.int32, (ROWS, 128), 1)
        out = []
        for a in range(2):
            (b0, d0), (b1, d1) = newlims[2*a], newlims[2*a+1]
            ok = lane <= jnp.where(lane < ROWS, row*d0 + b0, row*d1 + b1 + ROWS)
            bias = jnp.where(ok, 0.0, NEG)
            out.append((pair[a].reshape(HEADS, ROWS, 128) + bias[None]).reshape(nrow, 128))
        return out

    def chunk(base, size, with_new=False):
        offs = [lst[first + base + j] for j in range(size)]
        kc = jnp.concatenate([at(o) for o in offs] + (new_k if with_new else []), axis=0)
        vc = jnp.concatenate([at(o + HALF) for o in offs] + (new_v if with_new else []), axis=0)
        step(kc, vc, with_new)

    if careful:
        def body(i, _):
            chunk(i, 1)
            return 0
        lax.fori_loop(0, n, body, 0)

        @pl.when(any_new)
        def _():
            chunk(0, 0, True)
    else:
        def body(i, _):
            chunk(i*2*nb, 2*nb)
            return 0
        lax.fori_loop(0, n // (2*nb), body, 0)

        @pl.when((n // nb) % 2 == 1)
        def _():
            chunk(n // (2*nb) * (2*nb), nb)
        for left in range(nb):
            @pl.when(any_new & (n % nb == left))
            def _(left=left):
                chunk(n - left, left, True)

            if left:
                @pl.when(jnp.logical_not(any_new) & (n % nb == left))
                def _(left=left):
                    chunk(n - left, left)
    lane = lax.broadcasted_iota(jnp.int32, (ROWS, 128), 1)
    st = jnp.full((ROWS, 128), NEG, jnp.float32)
    top = top_s[...]
    peaks = lax.dot_general(q_s[:, :HD], jnp.broadcast_to(base, (128, HD)), (((1,),(1,)),((),())),
                            preferred_element_type=jnp.float32)
    for h in range(HEADS):
        r = pl.ds(h*ROWS, ROWS)
        l = jnp.sum(l_s[r, :], axis=1, keepdims=True)
        top = jnp.maximum(top, l)
        some = l > 0.0
        l = jnp.where(some, l, 1.0)
        o_ref[g, :, h*HD:(h+1)*HD] = (acc_s[r, :] * (1.0 / l)).astype(jnp.bfloat16)
        peak = peaks[h*ROWS:(h+1)*ROWS]
        if careful:
            peak = peak + m_s[r, :]
        st = jnp.where(lane == h, jnp.where(some, peak*SCALE + jnp.log(l), NEG), st)
    st_ref[g] = st
    top_s[...] = top


def attention(qg, kvg, cdocs, ndocs, tiles, place, nb=4):
    nrow = ROWS*HEADS
    smem, anywhere = pl.BlockSpec(memory_space=pltpu.SMEM), pl.BlockSpec(memory_space=pl.ANY)
    return pl.pallas_call(
        functools.partial(attn_kernel, nb=nb),
        in_specs=[smem] * 4 + [anywhere] * 2,
        out_specs=[anywhere] * 2,
        scratch_shapes=[pltpu.VMEM((8, ROWS, HEADS*HD), jnp.bfloat16), pltpu.VMEM((4*MEM, HD), jnp.bfloat16),
                        pltpu.VMEM((8, ROWS, HEADS*HD), jnp.bfloat16), pltpu.VMEM((8, ROWS, 128), jnp.float32),
                        pltpu.VMEM((nrow, 2*HD), jnp.bfloat16), pltpu.VMEM((nrow, 128), jnp.float32),
                        pltpu.VMEM((nrow, 128), jnp.float32), pltpu.VMEM((nrow, HD), jnp.float32),
                        pltpu.VMEM((ROWS, 128), jnp.float32),
                        pltpu.SMEM((128,), jnp.int32), pltpu.SMEM((4,), jnp.int32), pltpu.SemaphoreType.DMA((3, 8))],
        out_shape=[jax.ShapeDtypeStruct((8, ROWS, HEADS*HD), jnp.bfloat16),
                   jax.ShapeDtypeStruct((24, ROWS, 128), jnp.float32)],
        compiler_params=pltpu.CompilerParams(vmem_limit_bytes=(64 << 20) - (512 << 10)),
        name="attention",
    )(cdocs, ndocs, tiles, place, qg, kvg)


MESH = pl.DeviceIdType.MESH
WROWS = 512
WMID = 1600


def coords():
    c = lax.axis_index("ctx")
    return c // 16, (c // 4) % 4, c % 4


def ctx_of(z, x, y):
    return z * 16 + x * 4 + y


def send(src, dst, sems, i, device):
    copy = pltpu.make_async_remote_copy(
        src_ref=src, dst_ref=dst, send_sem=sems[0].at[i], recv_sem=sems[1].at[i],
        device_id=device, device_id_type=MESH)
    copy.start()
    return copy


def arrive(ref, sems, i, device):
    pltpu.make_async_remote_copy(
        src_ref=ref, dst_ref=ref, send_sem=sems[0].at[i], recv_sem=sems[1].at[i],
        device_id=device, device_id_type=MESH).wait_recv()


def greet(peers):
    barrier = pltpu.get_barrier_semaphore()
    for device in peers:
        pl.semaphore_signal(barrier, inc=1, device_id=device, device_id_type=MESH)
    pl.semaphore_wait(barrier, len(peers))


def gather_kernel(q, ck, cv, nk, nv, w, q_out, kv_out, w_out, rest_out, qg, kvg, wg, wr, ws, ssem, rsem, lsem, osem):
    z, x, y = coords()
    sems = (ssem, rsem)
    zp = 1 - z
    xr, xl, yr, yl = (x + 1) % 4, (x + 3) % 4, (y + 1) % 4, (y + 3) % 4
    x2, y2 = (x + 2) % 4, (y + 2) % 4
    dev = lambda z, x, y: {"ctx": ctx_of(z, x, y)}
    to_yr, to_yl, to_xr, to_xl, to_z = dev(z, x, yr), dev(z, x, yl), dev(z, xr, y), dev(z, xl, y), dev(zp, x, y)
    slot = lambda z, x: z * 4 + x
    me = slot(z, x)
    out = []
    pieces = [(ck, 0, CR), (nk, CR, ROWS), (cv, HALF, CR), (nv, HALF + CR, ROWS)]
    locs = [pltpu.make_async_copy(q, qg.at[me], lsem.at[0])]
    for i, (src, off, n) in enumerate(pieces):
        locs.append(pltpu.make_async_copy(src, kvg.at[y, pl.ds(off, n)], lsem.at[1 + i]))
    locs.append(pltpu.make_async_copy(w.at[pl.ds(0, WROWS)], ws, lsem.at[5]))
    locs.append(pltpu.make_async_copy(w.at[pl.ds(WROWS, WMID - WROWS)], wr, lsem.at[6]))
    for cp in locs:
        cp.start()
    greet([to_yr, to_yl, to_xr, to_xl, to_z])
    kh, vh = pl.ds(0, HALF), pl.ds(HALF, HALF)
    saves = []

    def save(src, dst):
        saves.append(pltpu.make_async_copy(src, dst, osem.at[len(saves)]))
        saves[-1].start()

    locs[0].wait()
    out.append(send(qg.at[me], qg.at[me], sems, 0, to_z))
    out.append(send(qg.at[me], qg.at[me], sems, 9, to_xr))
    out.append(send(qg.at[me], qg.at[me], sems, 10, to_xl))
    for cp in locs[1:5]:
        cp.wait()
    out.append(send(kvg.at[y, kh], kvg.at[y, kh], sems, 1, to_yr))
    out.append(send(kvg.at[y, vh], kvg.at[y, vh], sems, 2, to_yl))
    out.append(send(kvg.at[y, vh], kvg.at[y, vh], sems, 3, to_yr))
    out.append(send(kvg.at[y, kh], kvg.at[y, kh], sems, 4, to_yl))
    locs[5].wait()
    out.append(send(ws, wg, sems, 19, to_z))
    save(qg.at[me], q_out.at[me])
    save(kvg.at[y], kv_out.at[y])
    locs[6].wait()
    save(wr, rest_out)
    other = slot(zp, x)
    arrive(qg.at[other], sems, 0, to_z)
    out.append(send(qg.at[other], qg.at[other], sems, 11, to_xr))
    out.append(send(qg.at[other], qg.at[other], sems, 12, to_xl))
    save(qg.at[other], q_out.at[other])
    lo, hi = pl.ds(0, 32), pl.ds(32, 32)
    arrive(qg.at[slot(z, xl)], sems, 9, to_xl)
    out.append(send(qg.at[slot(z, xl), lo], qg.at[slot(z, xl), lo], sems, 13, to_xr))
    save(qg.at[slot(z, xl)], q_out.at[slot(z, xl)])
    arrive(qg.at[slot(z, xr)], sems, 10, to_xr)
    out.append(send(qg.at[slot(z, xr), hi], qg.at[slot(z, xr), hi], sems, 14, to_xl))
    save(qg.at[slot(z, xr)], q_out.at[slot(z, xr)])
    arrive(kvg.at[yl, kh], sems, 1, to_yl)
    out.append(send(kvg.at[yl, kh], kvg.at[yl, kh], sems, 17, to_yr))
    arrive(kvg.at[yr, vh], sems, 2, to_yr)
    out.append(send(kvg.at[yr, vh], kvg.at[yr, vh], sems, 18, to_yl))
    arrive(qg.at[slot(zp, xl)], sems, 11, to_xl)
    out.append(send(qg.at[slot(zp, xl), lo], qg.at[slot(zp, xl), lo], sems, 15, to_xr))
    save(qg.at[slot(zp, xl)], q_out.at[slot(zp, xl)])
    arrive(qg.at[slot(zp, xr)], sems, 12, to_xr)
    out.append(send(qg.at[slot(zp, xr), hi], qg.at[slot(zp, xr), hi], sems, 16, to_xl))
    save(qg.at[slot(zp, xr)], q_out.at[slot(zp, xr)])
    arrive(kvg.at[yl, vh], sems, 3, to_yl)
    arrive(kvg.at[yr, kh], sems, 4, to_yr)
    save(kvg.at[yl], kv_out.at[yl])
    save(kvg.at[yr], kv_out.at[yr])
    arrive(qg.at[slot(z, x2), lo], sems, 13, to_xl)
    arrive(qg.at[slot(z, x2), hi], sems, 14, to_xr)
    save(qg.at[slot(z, x2)], q_out.at[slot(z, x2)])
    arrive(qg.at[slot(zp, x2), lo], sems, 15, to_xl)
    arrive(qg.at[slot(zp, x2), hi], sems, 16, to_xr)
    save(qg.at[slot(zp, x2)], q_out.at[slot(zp, x2)])
    arrive(kvg.at[y2, kh], sems, 17, to_yl)
    arrive(kvg.at[y2, vh], sems, 18, to_yr)
    save(kvg.at[y2], kv_out.at[y2])
    arrive(wg, sems, 19, to_z)
    save(wg, w_out)
    for cp in saves:
        cp.wait()
    for cp in out:
        cp.wait_send()


def gather(q, ck, cv, nk, nv, w):
    hbm, bf = pl.BlockSpec(memory_space=pl.ANY), jnp.bfloat16
    return pl.pallas_call(
        gather_kernel,
        in_specs=[hbm] * 6,
        out_specs=[hbm] * 4,
        out_shape=[jax.ShapeDtypeStruct((8, ROWS, HEADS * HD), jnp.bfloat16),
                   jax.ShapeDtypeStruct((4, MEM, HD), jnp.bfloat16),
                   jax.ShapeDtypeStruct((WROWS, 512), jnp.bfloat16),
                   jax.ShapeDtypeStruct((WMID - WROWS, 512), jnp.bfloat16)],
        scratch_shapes=[pltpu.VMEM((8, ROWS, HEADS * HD), bf), pltpu.VMEM((4, MEM, HD), bf), pltpu.VMEM((WROWS, 512), bf),
                        pltpu.VMEM((WMID - WROWS, 512), bf), pltpu.VMEM((WROWS, 512), bf), pltpu.SemaphoreType.DMA((20,)),
                        pltpu.SemaphoreType.DMA((20,)), pltpu.SemaphoreType.DMA((7,)), pltpu.SemaphoreType.DMA((14,))],
        compiler_params=pltpu.CompilerParams(collective_id=0, has_side_effects=True, vmem_limit_bytes=56 << 20),
        name="gather",
    )(q, ck, cv, nk, nv, w)


def merge(parts, stats):
    largest = functools.reduce(jnp.maximum, stats)
    e = [jnp.exp(s - largest) for s in stats]
    total = functools.reduce(jnp.add, e)
    inverse = 1.0 / total
    e = [a * inverse for a in e]
    cols = []
    for head in range(HEADS):
        a = None
        for weight, part in zip(e, parts):
            term = weight[:, head:head + 1] * part[:, head * HD:(head + 1) * HD].astype(jnp.float32)
            a = term if a is None else a + term
        cols.append(a.astype(jnp.bfloat16))
    return cols, largest + jnp.log(total)


def pack(stats):
    lane = lax.broadcasted_iota(jnp.int32, (8, 128), 1)
    out = None
    for i in range(4 * len(stats)):
        a = stats[i // 4][8 * (i % 4):8 * (i % 4) + 8]
        out = a if i == 0 else jnp.where(lane >= 16 * i, pltpu.roll(a, 16 * i, 1), out)
    return out


def unpack(packed, i=0):
    return jnp.concatenate([packed if i + g == 0 else pltpu.roll(packed, 128 - 64 * i - 16 * g, 1) for g in range(4)], axis=0)


def put(ref, cols):
    for head, a in enumerate(cols):
        ref[:, head * HD:(head + 1) * HD] = a


def project_kernel(o_hbm, st_hbm, w, wlo, whi, out, o, st, px, sx, pz, sz, mz, nz, rz, tz, mx, nx, rx, tx_s, attg, w_s, ct, cr, acc, zt, zr,
                   a_s, a_r, b_s, b_r, c_s, c_r, d_s, d_r, gs, gr, cs, crs, zs, zrs, lsem, sp):
    z, x, y = coords()
    t = lax.axis_index("tp")
    h, k = t // 2, t % 2
    dev = lambda z, x, y: {"ctx": ctx_of(z, x, y)}
    zdev = lambda b, zh: {"ctx": ctx_of(b, x, y), "tp": zh * 2 + k}
    zp = 1 - z
    xr, xl, yr, yl = (x + 1) % 4, (x + 3) % 4, (y + 1) % 4, (y + 3) % 4
    core = {"tp": h * 2 + 1 - k}
    to_yr, to_yl, to_xr, to_xl = dev(z, x, yr), dev(z, x, yl), dev(z, xr, y), dev(z, xl, y)
    to_z = dev(zp, x, y)
    to_x = lambda d: dev(z, (x + d) % 4, y)
    ready = [pltpu.make_async_copy(o_hbm, o, lsem.at[3]), pltpu.make_async_copy(st_hbm.at[pl.ds(0, 2)], st, lsem.at[4])]
    for cp in ready:
        cp.start()
    greet([to_xr, to_xl, to_x(2), to_z, to_yr, to_yl, core, zdev(0, 1 - h), zdev(1, 1 - h)])
    lo, hi = pl.ds(0, 32), pl.ds(32, 32)
    outs = []

    for cp in ready:
        cp.wait()
    for d in (2, 1, 3, 0):
        xx = (x + d) % 4
        outs.append(send(o.at[zp, xx, hi], pz.at[xx], (b_s.at[0], b_r.at[0]), d, to_z))
    for d in (2, 1, 3):
        xx = (x + d) % 4
        outs.append(send(o.at[:, xx, lo], px.at[x], (a_s.at[0], a_r.at[0]), d, to_x(d)))
    for d in (2, 1, 3, 0):
        xx = (x + d) % 4
        sp[0, d] = pack([st[zp, xx, 32:64, :]])
        outs.append(send(sp.at[0, d], sz.at[xx], (b_s.at[1], b_r.at[1]), d, to_z))
    for d in (2, 1, 3):
        xx = (x + d) % 4
        sp[1, d] = pack([st[0, xx, 0:32, :], st[1, xx, 0:32, :]])
        outs.append(send(sp.at[1, d], sx.at[x], (a_s.at[1], a_r.at[1]), d, to_x(d)))
    weights = [pltpu.make_async_copy(w, w_s.at[z], lsem.at[0]),
               pltpu.make_async_copy(wlo, w_s.at[zp, pl.ds(0, WROWS)], lsem.at[1]),
               pltpu.make_async_copy(whi, w_s.at[zp, pl.ds(WROWS, WMID - WROWS)], lsem.at[2])]
    for cp in weights:
        cp.start()
    for d in (2, 1, 3, 0):
        xx = (x + d) % 4
        arrive(sz.at[xx], (b_s.at[1], b_r.at[1]), d, to_z)
        arrive(pz.at[xx], (b_s.at[0], b_r.at[0]), d, to_z)
        cols, lse = merge([o[z, xx, 32:64, :], pz[xx]], [st[z, xx, 32:64, :], unpack(sz[xx])])
        if d == 0:
            put(rx.at[x], cols)
            tx_s[x] = pack([lse])
        else:
            put(mx.at[d - 1], cols)
            nx[d - 1] = pack([lse])
            outs.append(send(nx.at[d - 1], tx_s.at[x], (d_s.at[1], d_r.at[1]), d, to_x(d)))
            outs.append(send(mx.at[d - 1], rx.at[x], (d_s.at[0], d_r.at[0]), d, to_x(d)))
    for d in (2, 1, 3):
        xx = (x + 4 - d) % 4
        arrive(sx.at[xx], (a_s.at[1], a_r.at[1]), d, to_x(4 - d))
        arrive(px.at[xx], (a_s.at[0], a_r.at[0]), d, to_x(4 - d))
    others = [(x + d) % 4 for d in (1, 2, 3)]
    both_runs = [(unpack(sx[xx], 0), unpack(sx[xx], 1)) for xx in others]
    first = z == 0
    cols, lse = merge([o[zp, x, 0:32, :]] + [px[xx, zp] for xx in others],
                      [st[zp, x, 0:32, :]] + [jnp.where(first, b, a) for a, b in both_runs])
    put(mz, cols)
    nz[...] = pack([lse])
    outs.append(send(nz, tz, (c_s, c_r), 1, to_z))
    outs.append(send(mz, rz, (c_s, c_r), 0, to_z))
    weights[0].wait()
    far = pl.ds(WMID, 2048 - WMID)
    outs.append(send(w_s.at[z, far], w_s.at[z, far], (c_s, c_r), 2, to_z))
    own_cols, own_lse = merge([o[z, x, 0:32, :]] + [px[xx, z] for xx in others],
                              [st[z, x, 0:32, :]] + [jnp.where(first, a, b) for a, b in both_runs])
    mine = x * 4 + y
    put(attg.at[mine, lo], own_cols)
    arrive(tz, (c_s, c_r), 1, to_z)
    arrive(rz, (c_s, c_r), 0, to_z)
    cols, _ = merge([attg[mine, 0:32, :], rz[...]], [own_lse, unpack(tz[...])])
    put(attg.at[mine, lo], cols)

    slot = lambda x, y: x * 4 + y

    def block(hf, a, b, part=None):
        s = slot((x + a) % 4, (y + b) % 4) if hf == 0 else slot((x + b) % 4, (y + a) % 4)
        return attg.at[s, pl.ds(32 * hf, 32) if part is None else pl.ds(32 * hf + 16 * part, 16)]

    def ways(hf, stage):
        return (to_xr, to_xl) if (hf == 0) == (stage == 0) else (to_yr, to_yl)

    def both(hf, stage, a, i):
        right, left = ways(hf, stage)
        ref = block(hf, a, 0)
        outs.append(send(ref, ref, (gs.at[hf], gr.at[hf]), i, right))
        outs.append(send(ref, ref, (gs.at[hf], gr.at[hf]), i + 1, left))

    def at(stage, a, n):
        return (n, 0) if stage == 0 else (a, n)

    def relay(hf, stage, a, i):
        right, left = ways(hf, stage)
        arrive(block(hf, *at(stage, a, 3)), (gs.at[hf], gr.at[hf]), i, left)
        ref = block(hf, *at(stage, a, 3), part=0)
        outs.append(send(ref, ref, (gs.at[hf], gr.at[hf]), i + 2, right))
        arrive(block(hf, *at(stage, a, 1)), (gs.at[hf], gr.at[hf]), i + 1, right)
        ref = block(hf, *at(stage, a, 1), part=1)
        outs.append(send(ref, ref, (gs.at[hf], gr.at[hf]), i + 3, left))

    def last(hf, stage, a, i):
        right, left = ways(hf, stage)
        arrive(block(hf, *at(stage, a, 2), part=0), (gs.at[hf], gr.at[hf]), i + 2, left)
        arrive(block(hf, *at(stage, a, 2), part=1), (gs.at[hf], gr.at[hf]), i + 3, right)

    both(0, 0, 0, 0)
    both(0, 1, 0, 4)
    for d in (2, 1, 3):
        xx = (x + 4 - d) % 4
        arrive(tx_s.at[xx], (d_s.at[1], d_r.at[1]), d, to_x(4 - d))
        arrive(rx.at[xx], (d_s.at[0], d_r.at[0]), d, to_x(4 - d))
    cols, _ = merge([rx[i] for i in range(4)], [unpack(tx_s[i]) for i in range(4)])
    put(attg.at[mine, hi], cols)
    both(1, 0, 0, 0)
    both(1, 1, 0, 4)
    for hf in (0, 1):
        relay(hf, 0, 0, 0)
        both(hf, 1, 3, 8)
        both(hf, 1, 1, 12)
    for hf in (0, 1):
        last(hf, 0, 0, 0)
        both(hf, 1, 2, 16)

    near, sides, beyond = (0,), (1, 3), (2,)
    pieces = [(0, near), (0, sides), (1, 1), (1, 0), (0, beyond)]
    counts = [64, 128, 128, 128, 64]

    def places(p, kk):
        hf, what = pieces[p]
        if hf == 0:
            return [(2 * kk + i, (y + n) % 4) for i in (0, 1) for n in what]
        return [(2 * kk + (x + what) % 2, n) for n in range(4)]

    def rows_of(hf, blocks):
        return [attg[slot(*s), 32 * hf:32 * hf + 32, :] for s in blocks]

    def product(lhs, b):
        return jnp.dot(jnp.concatenate(lhs, axis=0), w_s[b], preferred_element_type=jnp.float32)

    mine_at = lambda b: (h == z) & (b == z)
    part_of = lambda p: pl.ds(0, counts[p])

    def to_core(p):
        outs.append(send(ct.at[p, :, part_of(p)], cr.at[p, :, part_of(p)], (cs, crs), p, core))

    def multiply(p):
        n = counts[p]
        lhs = rows_of(pieces[p][0], places(p, 1 - k) + places(p, k))
        for b in (0, 1):
            r = product(lhs, b)
            ct[p, b, :n] = r[:n].astype(jnp.bfloat16)
            acc[p, b, :n] = r[n:]
        to_core(p)

    def exchange(p):
        n = counts[p]
        arrive(cr.at[p, :, part_of(p)], (cs, crs), p, core)
        for b in (0, 1):
            zt[p, b, :n] = (acc[p, b, :n] + cr[p, b, :n].astype(jnp.float32)).astype(jnp.bfloat16)

            @pl.when(jnp.logical_not(mine_at(b)))
            def _():
                send(zt.at[p, b, part_of(p)], zr.at[h, p, part_of(p)], (zs, zrs.at[h]), p * 2 + b, zdev(b, z))

            @pl.when(mine_at(b))
            def _():
                zr[h, p, :n] = zt[p, b, :n]

    for hf in (0, 1):
        relay(hf, 1, 0, 4)
    for cp in weights[1:]:
        cp.wait()
    arrive(w_s.at[zp, far], (c_s, c_r), 2, to_z)
    lhs = rows_of(0, places(0, 1 - k) + places(0, k)) + rows_of(1, [(x, n) for n in range(4)])
    for b in (0, 1):
        r = product(lhs, b)
        ct[0, b, :64] = r[:64].astype(jnp.bfloat16)
        acc[0, b, :64] = r[64:128]
        acc[3, b] = r[128:]
    to_core(0)
    for hf in (0, 1):
        relay(hf, 1, 3, 8)
    for hf in (0, 1):
        relay(hf, 1, 1, 12)
    exchange(0)
    for hf in (0, 1):
        relay(hf, 1, 2, 16)
    multiply(1)
    multiply(2)
    exchange(1)
    exchange(2)
    for hf in (0, 1):
        for a, i in ((0, 4), (3, 8), (1, 12), (2, 16)):
            last(hf, 1, a, i)
    here = (x // 2) == k
    lhs = rows_of(0, places(4, 1 - k) + places(4, k)) + rows_of(1, [((x + 2) % 4, n) for n in range(4)])
    for b in (0, 1):
        r = product(lhs, b)
        ct[4, b, :64] = r[:64].astype(jnp.bfloat16)
        acc[4, b, :64] = r[64:128]
        early, late = acc[3, b], r[128:]
        ct[3, b] = jnp.where(here, late, early).astype(jnp.bfloat16)
        acc[3, b] = jnp.where(here, early, late)
    to_core(3)
    to_core(4)
    exchange(3)
    exchange(4)
    for p in range(5):
        n = counts[p]
        for s in (0, 1):
            @pl.when(jnp.logical_not((s == h) & (z == h)))
            def _():
                pltpu.make_async_remote_copy(
                    src_ref=zr.at[s, p, part_of(p)], dst_ref=zr.at[s, p, part_of(p)], send_sem=zs.at[0],
                    recv_sem=zrs.at[s, p * 2 + z], device_id=zdev(h, s), device_id_type=MESH).wait_recv()
        total = (zr[0, p, :n].astype(jnp.float32) + zr[1, p, :n].astype(jnp.float32)).astype(jnp.bfloat16)
        for i, (xx, yy) in enumerate(places(p, k)):
            off = (slot(xx, yy) - 8 * k) * 64 + 32 * pieces[p][0]
            out[pl.ds(pl.multiple_of(off, 32), 32), :] = total[32 * i:32 * i + 32]
    for p in range(5):
        for b in (0, 1):
            @pl.when(jnp.logical_not(mine_at(b)))
            def _():
                pltpu.make_async_remote_copy(
                    src_ref=zt.at[p, b, part_of(p)], dst_ref=zt.at[p, b, part_of(p)], send_sem=zs.at[p * 2 + b],
                    recv_sem=zrs.at[0, 0], device_id=zdev(b, z), device_id_type=MESH).wait_send()
    for cp in outs:
        cp.wait_send()


def project(o, st, w, wlo, whi):
    hbm, vmem = pl.BlockSpec(memory_space=pl.ANY), pl.BlockSpec(memory_space=pltpu.VMEM)
    dma = pltpu.SemaphoreType.DMA
    bf, f32 = jnp.bfloat16, jnp.float32
    wide = HEADS * HD
    return pl.pallas_call(
        project_kernel,
        in_specs=[hbm] * 5,
        out_specs=vmem,
        out_shape=jax.ShapeDtypeStruct((512, 512), bf),
        scratch_shapes=[
            pltpu.VMEM((2, 4, ROWS, wide), bf), pltpu.VMEM((2, 4, ROWS, 128), f32),
            pltpu.VMEM((4, 2, 32, wide), bf), pltpu.VMEM((4, 8, 128), f32),
            pltpu.VMEM((4, 32, wide), bf), pltpu.VMEM((4, 8, 128), f32),
            pltpu.VMEM((32, wide), bf), pltpu.VMEM((8, 128), f32),
            pltpu.VMEM((32, wide), bf), pltpu.VMEM((8, 128), f32),
            pltpu.VMEM((3, 32, wide), bf), pltpu.VMEM((3, 8, 128), f32),
            pltpu.VMEM((4, 32, wide), bf), pltpu.VMEM((4, 8, 128), f32),
            pltpu.VMEM((16, ROWS, wide), bf), pltpu.VMEM((2, 2048, 512), bf),
            pltpu.VMEM((5, 2, 128, 512), bf), pltpu.VMEM((5, 2, 128, 512), bf), pltpu.VMEM((5, 2, 128, 512), f32),
            pltpu.VMEM((5, 2, 128, 512), bf), pltpu.VMEM((2, 5, 128, 512), bf),
            dma((2, 4)), dma((2, 4)), dma((2, 4)), dma((2, 4)), dma((3,)), dma((3,)), dma((2, 4)), dma((2, 4)),
            dma((2, 20)), dma((2, 20)), dma((5,)), dma((5,)), dma((10,)), dma((2, 10)), dma((5,)),
            pltpu.VMEM((2, 4, 8, 128), f32),
        ],
        compiler_params=pltpu.CompilerParams(collective_id=1, has_side_effects=True, vmem_limit_bytes=53 << 20),
        name="project",
    )(o, st, w, wlo, whi)


def shards(new_queries, new_keys, new_values, cache_keys, cache_values, out_weight, cache_docs, new_docs, slot_tile):
    qg, kvg, wlo, rest = gather(new_queries, cache_keys, cache_values, new_keys, new_values, out_weight)
    whi = lax.ppermute(rest, "ctx", [(i, i ^ 16) for i in range(32)])
    place = jnp.reshape(lax.axis_index("ctx"), (1,)).astype(jnp.int32)
    o, st = attention(qg, kvg.reshape(4 * MEM, HD), cache_docs, new_docs, slot_tile, place)
    return project(o.reshape(2, 4, ROWS, HEADS * HD), st.reshape(6, 4, ROWS, 128), out_weight, wlo, whi)


def solution(mesh):
    return jax.shard_map(
        shards,
        mesh=mesh,
        in_specs=(
            P("ctx", "tp"),
            P("ctx", "tp"),
            P("ctx", "tp"),
            P("ctx", "tp"),
            P("ctx", "tp"),
            P("tp", "ctx"),
            P(),
            P(),
            P(),
        ),
        out_specs=P("tp", "ctx"),
        check_vma=False,
    )
```

```python
import functools
import jax, jax.numpy as jnp
from jax import lax
from jax.experimental import pallas as pl
from jax.experimental.pallas import tpu as pltpu
from jax.sharding import PartitionSpec as P

HD=128; BLK=128; NEG=-1e30
SCALE=HD**-0.5
L2E=1.4426950408889634
ROWS=64; HEADS=16; CR=1024; HALF=CR+ROWS; MEM=2*HALF
SUB=1024

def attn_kernel(cdocs, ndocs, tiles, place, q_hbm, kv_hbm, o_hbm, st_hbm, q_ref, kv_ref, o_ref, st_ref,
                q_s, m_s, l_s, acc_s, top_s, lst, cnt, sems, *, nb):
    q_in = lambda g: pltpu.make_async_copy(q_hbm.at[g], q_ref.at[g], sems.at[0, g])
    o_out = lambda g: pltpu.make_async_copy(o_ref.at[g], o_hbm.at[g], sems.at[1, g])
    kv_in = pltpu.make_async_copy(kv_hbm, kv_ref, sems.at[2, 0])
    st_out = pltpu.make_async_copy(st_ref, st_hbm.at[pl.ds(0, 8)], sems.at[2, 1])
    kv_in.start()
    for g in range(8):
        q_in(g).start()
    c = place[0]
    y = c % 4
    for d in range(4):
        cnt[d] = 0

    def add(i, _):
        d = cdocs[(c - y) * 8 + i]
        n = cnt[d]
        lst[d * 32 + n] = (i // 8) * MEM + (i % 8) * BLK
        cnt[d] = n + 1
        return 0
    lax.fori_loop(0, 32, add, 0)
    top_s[...] = jnp.zeros_like(top_s)
    kv_in.wait()

    def run(g, careful):
        attend_run(g, c, careful, cnt, ndocs, tiles, q_ref, kv_ref, o_ref, st_ref, q_s, m_s, l_s, acc_s, top_s, lst, nb)
        o_out(g).start()

    def fast(g, _):
        q_in(g).wait()
        run(g, False)
        return 0
    lax.fori_loop(0, 8, fast, 0)

    @pl.when(jnp.logical_not(jnp.max(top_s[...]) < 1e30))
    def _():
        def again(g, _):
            o_out(g).wait()
            run(g, True)
            return 0
        lax.fori_loop(0, 8, again, 0)
    st_out.start()
    for g in range(8):
        o_out(g).wait()
    st_out.wait()


def attend_run(g, c, careful, cnt, ndocs, tiles, q_ref, kv_ref, o_ref, st_ref, q_s, m_s, l_s, acc_s, top_s, lst, nb):
    y = c % 4
    src = g * 4 + y
    members = [c - y + i for i in range(4)]
    tq = tiles[src]
    qd = ndocs[tq // 2]
    nrow = ROWS*HEADS
    for h in range(HEADS):
        part = q_ref[g, :, h*HD:(h+1)*HD]
        q_s[h*ROWS:(h+1)*ROWS, :HD] = part
        q_s[h*ROWS:(h+1)*ROWS, HD:] = part
    if careful:
        m_s[...] = jnp.full_like(m_s, NEG)
    l_s[...] = jnp.zeros_like(l_s)
    acc_s[...] = jnp.zeros_like(acc_s)
    n = cnt[qd]
    first = qd * 32

    def scores(kc, masked):
        k2 = jnp.concatenate([kc, jnp.broadcast_to(-base, kc.shape)], axis=1)
        s = lax.dot_general(q_s[...], k2, (((1,),(1,)),((),())), preferred_element_type=jnp.float32)
        tiles_of = [s[:, i*128:(i+1)*128] for i in range(s.shape[1]//128)]
        return tiles_of[:-2] + mask(tiles_of[-2:]) if masked else tiles_of

    def step(kc, vc, masked):
        s = scores(kc, masked)
        if careful:
            m_old = m_s[...]
            m = jnp.maximum(m_old, jnp.max(functools.reduce(jnp.maximum, s), axis=1, keepdims=True))
            alpha = jnp.exp2((m_old - m)*(SCALE*L2E))
            l_s[...] = l_s[...]*alpha
            acc_s[...] = acc_s[...]*alpha
            m_s[...] = m
            s = [a - m for a in s]
        p = [jnp.exp2(a*(SCALE*L2E)) for a in s]
        l_s[...] = l_s[...] + functools.reduce(jnp.add, p)
        pb = jnp.concatenate([a.astype(jnp.bfloat16) for a in p], axis=1)
        acc_s[...] = acc_s[...] + jnp.dot(pb, vc, preferred_element_type=jnp.float32)

    def at(off, rows=BLK):
        return kv_ref[pl.ds(pl.multiple_of(off, 64), rows), :]

    newlims = []
    new_k, new_v = [], []
    for mi, cm in enumerate(members):
        tk = tiles[cm]
        full_ok = (ndocs[tk // 2] == qd) & (tk < tq)
        diag = tk == tq
        newlims.append((jnp.where(full_ok, 1 << 20, jnp.where(diag, 0, -1)), jnp.where(diag, 1, 0)))
        new_k.append(kv_ref[mi*MEM + CR: mi*MEM + HALF, :])
        new_v.append(kv_ref[mi*MEM + HALF + CR: (mi+1)*MEM, :])
    any_new = functools.reduce(jnp.logical_or, [lim >= 0 for lim, _ in newlims])
    where = jnp.int32(0)
    for mi in range(4):
        where = jnp.where(newlims[mi][0] >= 0, mi*MEM + CR, where)
    where = jnp.where(n > 0, lst[first], where)
    base = at(where, 16)[0:1, :]

    def mask(pair):
        row = lax.broadcasted_iota(jnp.int32, (ROWS, 128), 0)
        lane = lax.broadcasted_iota(jnp.int32, (ROWS, 128), 1)
        out = []
        for a in range(2):
            (b0, d0), (b1, d1) = newlims[2*a], newlims[2*a+1]
            ok = lane <= jnp.where(lane < ROWS, row*d0 + b0, row*d1 + b1 + ROWS)
            bias = jnp.where(ok, 0.0, NEG)
            out.append((pair[a].reshape(HEADS, ROWS, 128) + bias[None]).reshape(nrow, 128))
        return out

    def chunk(base, size, with_new=False):
        offs = [lst[first + base + j] for j in range(size)]
        kc = jnp.concatenate([at(o) for o in offs] + (new_k if with_new else []), axis=0)
        vc = jnp.concatenate([at(o + HALF) for o in offs] + (new_v if with_new else []), axis=0)
        step(kc, vc, with_new)

    if careful:
        def body(i, _):
            chunk(i, 1)
            return 0
        lax.fori_loop(0, n, body, 0)

        @pl.when(any_new)
        def _():
            chunk(0, 0, True)
    else:
        def body(i, _):
            chunk(i*2*nb, 2*nb)
            return 0
        lax.fori_loop(0, n // (2*nb), body, 0)

        @pl.when((n // nb) % 2 == 1)
        def _():
            chunk(n // (2*nb) * (2*nb), nb)
        for left in range(nb):
            @pl.when(any_new & (n % nb == left))
            def _(left=left):
                chunk(n - left, left, True)

            if left:
                @pl.when(jnp.logical_not(any_new) & (n % nb == left))
                def _(left=left):
                    chunk(n - left, left)
    lane = lax.broadcasted_iota(jnp.int32, (ROWS, 128), 1)
    st = jnp.full((ROWS, 128), NEG, jnp.float32)
    top = top_s[...]
    peaks = lax.dot_general(q_s[:, :HD], jnp.broadcast_to(base, (128, HD)), (((1,),(1,)),((),())),
                            preferred_element_type=jnp.float32)
    for h in range(HEADS):
        r = pl.ds(h*ROWS, ROWS)
        l = jnp.sum(l_s[r, :], axis=1, keepdims=True)
        top = jnp.maximum(top, l)
        some = l > 0.0
        l = jnp.where(some, l, 1.0)
        o_ref[g, :, h*HD:(h+1)*HD] = (acc_s[r, :] * (1.0 / l)).astype(jnp.bfloat16)
        peak = peaks[h*ROWS:(h+1)*ROWS]
        if careful:
            peak = peak + m_s[r, :]
        st = jnp.where(lane == h, jnp.where(some, peak*SCALE + jnp.log(l), NEG), st)
    st_ref[g] = st
    top_s[...] = top


def attention(qg, kvg, cdocs, ndocs, tiles, place, nb=4):
    nrow = ROWS*HEADS
    smem, anywhere = pl.BlockSpec(memory_space=pltpu.SMEM), pl.BlockSpec(memory_space=pl.ANY)
    return pl.pallas_call(
        functools.partial(attn_kernel, nb=nb),
        in_specs=[smem] * 4 + [anywhere] * 2,
        out_specs=[anywhere] * 2,
        scratch_shapes=[pltpu.VMEM((8, ROWS, HEADS*HD), jnp.bfloat16), pltpu.VMEM((4*MEM, HD), jnp.bfloat16),
                        pltpu.VMEM((8, ROWS, HEADS*HD), jnp.bfloat16), pltpu.VMEM((8, ROWS, 128), jnp.float32),
                        pltpu.VMEM((nrow, 2*HD), jnp.bfloat16), pltpu.VMEM((nrow, 128), jnp.float32),
                        pltpu.VMEM((nrow, 128), jnp.float32), pltpu.VMEM((nrow, HD), jnp.float32),
                        pltpu.VMEM((ROWS, 128), jnp.float32),
                        pltpu.SMEM((128,), jnp.int32), pltpu.SMEM((4,), jnp.int32), pltpu.SemaphoreType.DMA((3, 8))],
        out_shape=[jax.ShapeDtypeStruct((8, ROWS, HEADS*HD), jnp.bfloat16),
                   jax.ShapeDtypeStruct((24, ROWS, 128), jnp.float32)],
        compiler_params=pltpu.CompilerParams(vmem_limit_bytes=(64 << 20) - (512 << 10)),
        name="attention",
    )(cdocs, ndocs, tiles, place, qg, kvg)


MESH = pl.DeviceIdType.MESH
WROWS = 512
WMID = 1600


def coords():
    c = lax.axis_index("ctx")
    return c // 16, (c // 4) % 4, c % 4


def ctx_of(z, x, y):
    return z * 16 + x * 4 + y


def send(src, dst, sems, i, device):
    copy = pltpu.make_async_remote_copy(
        src_ref=src, dst_ref=dst, send_sem=sems[0].at[i], recv_sem=sems[1].at[i],
        device_id=device, device_id_type=MESH)
    copy.start()
    return copy


def arrive(ref, sems, i, device):
    pltpu.make_async_remote_copy(
        src_ref=ref, dst_ref=ref, send_sem=sems[0].at[i], recv_sem=sems[1].at[i],
        device_id=device, device_id_type=MESH).wait_recv()


def greet(peers):
    barrier = pltpu.get_barrier_semaphore()
    for device in peers:
        pl.semaphore_signal(barrier, inc=1, device_id=device, device_id_type=MESH)
    pl.semaphore_wait(barrier, len(peers))


def gather_kernel(q, ck, cv, nk, nv, w, q_out, kv_out, w_out, rest_out, qg, kvg, wg, wr, ws, ssem, rsem, lsem, osem):
    z, x, y = coords()
    sems = (ssem, rsem)
    zp = 1 - z
    xr, xl, yr, yl = (x + 1) % 4, (x + 3) % 4, (y + 1) % 4, (y + 3) % 4
    x2, y2 = (x + 2) % 4, (y + 2) % 4
    dev = lambda z, x, y: {"ctx": ctx_of(z, x, y)}
    to_yr, to_yl, to_xr, to_xl, to_z = dev(z, x, yr), dev(z, x, yl), dev(z, xr, y), dev(z, xl, y), dev(zp, x, y)
    slot = lambda z, x: z * 4 + x
    me = slot(z, x)
    out = []
    pieces = [(ck, 0, CR), (nk, CR, ROWS), (cv, HALF, CR), (nv, HALF + CR, ROWS)]
    locs = [pltpu.make_async_copy(q, qg.at[me], lsem.at[0])]
    for i, (src, off, n) in enumerate(pieces):
        locs.append(pltpu.make_async_copy(src, kvg.at[y, pl.ds(off, n)], lsem.at[1 + i]))
    locs.append(pltpu.make_async_copy(w.at[pl.ds(0, WROWS)], ws, lsem.at[5]))
    locs.append(pltpu.make_async_copy(w.at[pl.ds(WROWS, WMID - WROWS)], wr, lsem.at[6]))
    for cp in locs:
        cp.start()
    greet([to_yr, to_yl, to_xr, to_xl, to_z])
    kh, vh = pl.ds(0, HALF), pl.ds(HALF, HALF)
    saves = []

    def save(src, dst):
        saves.append(pltpu.make_async_copy(src, dst, osem.at[len(saves)]))
        saves[-1].start()

    locs[0].wait()
    out.append(send(qg.at[me], qg.at[me], sems, 0, to_z))
    out.append(send(qg.at[me], qg.at[me], sems, 9, to_xr))
    out.append(send(qg.at[me], qg.at[me], sems, 10, to_xl))
    for cp in locs[1:5]:
        cp.wait()
    out.append(send(kvg.at[y, kh], kvg.at[y, kh], sems, 1, to_yr))
    out.append(send(kvg.at[y, vh], kvg.at[y, vh], sems, 2, to_yl))
    out.append(send(kvg.at[y, vh], kvg.at[y, vh], sems, 3, to_yr))
    out.append(send(kvg.at[y, kh], kvg.at[y, kh], sems, 4, to_yl))
    locs[5].wait()
    out.append(send(ws, wg, sems, 19, to_z))
    save(qg.at[me], q_out.at[me])
    save(kvg.at[y], kv_out.at[y])
    locs[6].wait()
    save(wr, rest_out)
    other = slot(zp, x)
    arrive(qg.at[other], sems, 0, to_z)
    out.append(send(qg.at[other], qg.at[other], sems, 11, to_xr))
    out.append(send(qg.at[other], qg.at[other], sems, 12, to_xl))
    save(qg.at[other], q_out.at[other])
    lo, hi = pl.ds(0, 32), pl.ds(32, 32)
    arrive(qg.at[slot(z, xl)], sems, 9, to_xl)
    out.append(send(qg.at[slot(z, xl), lo], qg.at[slot(z, xl), lo], sems, 13, to_xr))
    save(qg.at[slot(z, xl)], q_out.at[slot(z, xl)])
    arrive(qg.at[slot(z, xr)], sems, 10, to_xr)
    out.append(send(qg.at[slot(z, xr), hi], qg.at[slot(z, xr), hi], sems, 14, to_xl))
    save(qg.at[slot(z, xr)], q_out.at[slot(z, xr)])
    arrive(kvg.at[yl, kh], sems, 1, to_yl)
    out.append(send(kvg.at[yl, kh], kvg.at[yl, kh], sems, 17, to_yr))
    arrive(kvg.at[yr, vh], sems, 2, to_yr)
    out.append(send(kvg.at[yr, vh], kvg.at[yr, vh], sems, 18, to_yl))
    arrive(qg.at[slot(zp, xl)], sems, 11, to_xl)
    out.append(send(qg.at[slot(zp, xl), lo], qg.at[slot(zp, xl), lo], sems, 15, to_xr))
    save(qg.at[slot(zp, xl)], q_out.at[slot(zp, xl)])
    arrive(qg.at[slot(zp, xr)], sems, 12, to_xr)
    out.append(send(qg.at[slot(zp, xr), hi], qg.at[slot(zp, xr), hi], sems, 16, to_xl))
    save(qg.at[slot(zp, xr)], q_out.at[slot(zp, xr)])
    arrive(kvg.at[yl, vh], sems, 3, to_yl)
    arrive(kvg.at[yr, kh], sems, 4, to_yr)
    save(kvg.at[yl], kv_out.at[yl])
    save(kvg.at[yr], kv_out.at[yr])
    arrive(qg.at[slot(z, x2), lo], sems, 13, to_xl)
    arrive(qg.at[slot(z, x2), hi], sems, 14, to_xr)
    save(qg.at[slot(z, x2)], q_out.at[slot(z, x2)])
    arrive(qg.at[slot(zp, x2), lo], sems, 15, to_xl)
    arrive(qg.at[slot(zp, x2), hi], sems, 16, to_xr)
    save(qg.at[slot(zp, x2)], q_out.at[slot(zp, x2)])
    arrive(kvg.at[y2, kh], sems, 17, to_yl)
    arrive(kvg.at[y2, vh], sems, 18, to_yr)
    save(kvg.at[y2], kv_out.at[y2])
    arrive(wg, sems, 19, to_z)
    save(wg, w_out)
    for cp in saves:
        cp.wait()
    for cp in out:
        cp.wait_send()


def gather(q, ck, cv, nk, nv, w):
    hbm, bf = pl.BlockSpec(memory_space=pl.ANY), jnp.bfloat16
    return pl.pallas_call(
        gather_kernel,
        in_specs=[hbm] * 6,
        out_specs=[hbm] * 4,
        out_shape=[jax.ShapeDtypeStruct((8, ROWS, HEADS * HD), jnp.bfloat16),
                   jax.ShapeDtypeStruct((4, MEM, HD), jnp.bfloat16),
                   jax.ShapeDtypeStruct((WROWS, 512), jnp.bfloat16),
                   jax.ShapeDtypeStruct((WMID - WROWS, 512), jnp.bfloat16)],
        scratch_shapes=[pltpu.VMEM((8, ROWS, HEADS * HD), bf), pltpu.VMEM((4, MEM, HD), bf), pltpu.VMEM((WROWS, 512), bf),
                        pltpu.VMEM((WMID - WROWS, 512), bf), pltpu.VMEM((WROWS, 512), bf), pltpu.SemaphoreType.DMA((20,)),
                        pltpu.SemaphoreType.DMA((20,)), pltpu.SemaphoreType.DMA((7,)), pltpu.SemaphoreType.DMA((14,))],
        compiler_params=pltpu.CompilerParams(collective_id=0, has_side_effects=True, vmem_limit_bytes=56 << 20),
        name="gather",
    )(q, ck, cv, nk, nv, w)


def merge(parts, stats):
    largest = functools.reduce(jnp.maximum, stats)
    e = [jnp.exp(s - largest) for s in stats]
    total = functools.reduce(jnp.add, e)
    inverse = 1.0 / total
    e = [a * inverse for a in e]
    cols = []
    for head in range(HEADS):
        a = None
        for weight, part in zip(e, parts):
            term = weight[:, head:head + 1] * part[:, head * HD:(head + 1) * HD].astype(jnp.float32)
            a = term if a is None else a + term
        cols.append(a.astype(jnp.bfloat16))
    return cols, largest + jnp.log(total)


def pack(stats):
    lane = lax.broadcasted_iota(jnp.int32, (8, 128), 1)
    out = None
    for i in range(4 * len(stats)):
        a = stats[i // 4][8 * (i % 4):8 * (i % 4) + 8]
        out = a if i == 0 else jnp.where(lane >= 16 * i, pltpu.roll(a, 16 * i, 1), out)
    return out


def unpack(packed, i=0):
    return jnp.concatenate([packed if i + g == 0 else pltpu.roll(packed, 128 - 64 * i - 16 * g, 1) for g in range(4)], axis=0)


def put(ref, cols):
    for head, a in enumerate(cols):
        ref[:, head * HD:(head + 1) * HD] = a


def project_kernel(o_hbm, st_hbm, w, wlo, whi, out, o, st, px, sx, pz, sz, mz, nz, rz, tz, mx, nx, rx, tx_s, attg, w_s, ct, cr, acc, zt, zr,
                   a_s, a_r, b_s, b_r, c_s, c_r, d_s, d_r, gs, gr, cs, crs, zs, zrs, lsem, sp):
    z, x, y = coords()
    t = lax.axis_index("tp")
    h, k = t // 2, t % 2
    dev = lambda z, x, y: {"ctx": ctx_of(z, x, y)}
    zdev = lambda b, zh: {"ctx": ctx_of(b, x, y), "tp": zh * 2 + k}
    zp = 1 - z
    xr, xl, yr, yl = (x + 1) % 4, (x + 3) % 4, (y + 1) % 4, (y + 3) % 4
    core = {"tp": h * 2 + 1 - k}
    to_yr, to_yl, to_xr, to_xl = dev(z, x, yr), dev(z, x, yl), dev(z, xr, y), dev(z, xl, y)
    to_z = dev(zp, x, y)
    to_x = lambda d: dev(z, (x + d) % 4, y)
    ready = [pltpu.make_async_copy(o_hbm, o, lsem.at[3]), pltpu.make_async_copy(st_hbm.at[pl.ds(0, 2)], st, lsem.at[4])]
    for cp in ready:
        cp.start()
    greet([to_xr, to_xl, to_x(2), to_z, to_yr, to_yl, core, zdev(0, 1 - h), zdev(1, 1 - h)])
    lo, hi = pl.ds(0, 32), pl.ds(32, 32)
    outs = []

    for cp in ready:
        cp.wait()
    for d in (2, 1, 3, 0):
        xx = (x + d) % 4
        outs.append(send(o.at[zp, xx, hi], pz.at[xx], (b_s.at[0], b_r.at[0]), d, to_z))
    for d in (2, 1, 3):
        xx = (x + d) % 4
        outs.append(send(o.at[:, xx, lo], px.at[x], (a_s.at[0], a_r.at[0]), d, to_x(d)))
    for d in (2, 1, 3, 0):
        xx = (x + d) % 4
        sp[0, d] = pack([st[zp, xx, 32:64, :]])
        outs.append(send(sp.at[0, d], sz.at[xx], (b_s.at[1], b_r.at[1]), d, to_z))
    for d in (2, 1, 3):
        xx = (x + d) % 4
        sp[1, d] = pack([st[0, xx, 0:32, :], st[1, xx, 0:32, :]])
        outs.append(send(sp.at[1, d], sx.at[x], (a_s.at[1], a_r.at[1]), d, to_x(d)))
    weights = [pltpu.make_async_copy(w, w_s.at[z], lsem.at[0]),
               pltpu.make_async_copy(wlo, w_s.at[zp, pl.ds(0, WROWS)], lsem.at[1]),
               pltpu.make_async_copy(whi, w_s.at[zp, pl.ds(WROWS, WMID - WROWS)], lsem.at[2])]
    for cp in weights:
        cp.start()
    for d in (2, 1, 3, 0):
        xx = (x + d) % 4
        arrive(sz.at[xx], (b_s.at[1], b_r.at[1]), d, to_z)
        arrive(pz.at[xx], (b_s.at[0], b_r.at[0]), d, to_z)
        cols, lse = merge([o[z, xx, 32:64, :], pz[xx]], [st[z, xx, 32:64, :], unpack(sz[xx])])
        if d == 0:
            put(rx.at[x], cols)
            tx_s[x] = pack([lse])
        else:
            put(mx.at[d - 1], cols)
            nx[d - 1] = pack([lse])
            outs.append(send(nx.at[d - 1], tx_s.at[x], (d_s.at[1], d_r.at[1]), d, to_x(d)))
            outs.append(send(mx.at[d - 1], rx.at[x], (d_s.at[0], d_r.at[0]), d, to_x(d)))
    for d in (2, 1, 3):
        xx = (x + 4 - d) % 4
        arrive(sx.at[xx], (a_s.at[1], a_r.at[1]), d, to_x(4 - d))
        arrive(px.at[xx], (a_s.at[0], a_r.at[0]), d, to_x(4 - d))
    others = [(x + d) % 4 for d in (1, 2, 3)]
    both_runs = [(unpack(sx[xx], 0), unpack(sx[xx], 1)) for xx in others]
    first = z == 0
    cols, lse = merge([o[zp, x, 0:32, :]] + [px[xx, zp] for xx in others],
                      [st[zp, x, 0:32, :]] + [jnp.where(first, b, a) for a, b in both_runs])
    put(mz, cols)
    nz[...] = pack([lse])
    outs.append(send(nz, tz, (c_s, c_r), 1, to_z))
    outs.append(send(mz, rz, (c_s, c_r), 0, to_z))
    weights[0].wait()
    far = pl.ds(WMID, 2048 - WMID)
    outs.append(send(w_s.at[z, far], w_s.at[z, far], (c_s, c_r), 2, to_z))
    own_cols, own_lse = merge([o[z, x, 0:32, :]] + [px[xx, z] for xx in others],
                              [st[z, x, 0:32, :]] + [jnp.where(first, a, b) for a, b in both_runs])
    mine = x * 4 + y
    put(attg.at[mine, lo], own_cols)
    arrive(tz, (c_s, c_r), 1, to_z)
    arrive(rz, (c_s, c_r), 0, to_z)
    cols, _ = merge([attg[mine, 0:32, :], rz[...]], [own_lse, unpack(tz[...])])
    put(attg.at[mine, lo], cols)

    slot = lambda x, y: x * 4 + y

    def block(hf, a, b, part=None):
        s = slot((x + a) % 4, (y + b) % 4) if hf == 0 else slot((x + b) % 4, (y + a) % 4)
        return attg.at[s, pl.ds(32 * hf, 32) if part is None else pl.ds(32 * hf + 16 * part, 16)]

    def ways(hf, stage):
        return (to_xr, to_xl) if (hf == 0) == (stage == 0) else (to_yr, to_yl)

    def both(hf, stage, a, i):
        right, left = ways(hf, stage)
        ref = block(hf, a, 0)
        outs.append(send(ref, ref, (gs.at[hf], gr.at[hf]), i, right))
        outs.append(send(ref, ref, (gs.at[hf], gr.at[hf]), i + 1, left))

    def at(stage, a, n):
        return (n, 0) if stage == 0 else (a, n)

    def relay(hf, stage, a, i):
        right, left = ways(hf, stage)
        arrive(block(hf, *at(stage, a, 3)), (gs.at[hf], gr.at[hf]), i, left)
        ref = block(hf, *at(stage, a, 3), part=0)
        outs.append(send(ref, ref, (gs.at[hf], gr.at[hf]), i + 2, right))
        arrive(block(hf, *at(stage, a, 1)), (gs.at[hf], gr.at[hf]), i + 1, right)
        ref = block(hf, *at(stage, a, 1), part=1)
        outs.append(send(ref, ref, (gs.at[hf], gr.at[hf]), i + 3, left))

    def last(hf, stage, a, i):
        right, left = ways(hf, stage)
        arrive(block(hf, *at(stage, a, 2), part=0), (gs.at[hf], gr.at[hf]), i + 2, left)
        arrive(block(hf, *at(stage, a, 2), part=1), (gs.at[hf], gr.at[hf]), i + 3, right)

    both(0, 0, 0, 0)
    both(0, 1, 0, 4)
    for d in (2, 1, 3):
        xx = (x + 4 - d) % 4
        arrive(tx_s.at[xx], (d_s.at[1], d_r.at[1]), d, to_x(4 - d))
        arrive(rx.at[xx], (d_s.at[0], d_r.at[0]), d, to_x(4 - d))
    cols, _ = merge([rx[i] for i in range(4)], [unpack(tx_s[i]) for i in range(4)])
    put(attg.at[mine, hi], cols)
    both(1, 0, 0, 0)
    both(1, 1, 0, 4)
    for hf in (0, 1):
        relay(hf, 0, 0, 0)
        both(hf, 1, 3, 8)
        both(hf, 1, 1, 12)
    for hf in (0, 1):
        last(hf, 0, 0, 0)
        both(hf, 1, 2, 16)

    near, sides, beyond = (0,), (1, 3), (2,)
    pieces = [(0, near), (0, sides), (1, 1), (1, 0), (0, beyond)]
    counts = [64, 128, 128, 128, 64]

    def places(p, kk):
        hf, what = pieces[p]
        if hf == 0:
            return [(2 * kk + i, (y + n) % 4) for i in (0, 1) for n in what]
        return [(2 * kk + (x + what) % 2, n) for n in range(4)]

    def rows_of(hf, blocks):
        return [attg[slot(*s), 32 * hf:32 * hf + 32, :] for s in blocks]

    def product(lhs, b):
        return jnp.dot(jnp.concatenate(lhs, axis=0), w_s[b], preferred_element_type=jnp.float32)

    mine_at = lambda b: (h == z) & (b == z)
    part_of = lambda p: pl.ds(0, counts[p])

    def to_core(p, b):
        outs.append(send(ct.at[p, b, part_of(p)], cr.at[p, b, part_of(p)], (cs.at[p], crs.at[p]), b, core))

    def multiply(p):
        n = counts[p]
        lhs = rows_of(pieces[p][0], places(p, 1 - k) + places(p, k))
        for b in (0, 1):
            r = product(lhs, b)
            ct[p, b, :n] = r[:n].astype(jnp.bfloat16)
            acc[p, b, :n] = r[n:]
            to_core(p, b)

    def exchange(p, blocks=(0, 1)):
        n = counts[p]
        for b in blocks:
            arrive(cr.at[p, b, part_of(p)], (cs.at[p], crs.at[p]), b, core)
            zt[p, b, :n] = (acc[p, b, :n] + cr[p, b, :n].astype(jnp.float32)).astype(jnp.bfloat16)

            @pl.when(jnp.logical_not(mine_at(b)))
            def _():
                send(zt.at[p, b, part_of(p)], zr.at[h, p, part_of(p)], (zs, zrs.at[h]), p * 2 + b, zdev(b, z))

            @pl.when(mine_at(b))
            def _():
                zr[h, p, :n] = zt[p, b, :n]

    for hf in (0, 1):
        relay(hf, 1, 0, 4)
    for cp in weights[1:]:
        cp.wait()
    arrive(w_s.at[zp, far], (c_s, c_r), 2, to_z)
    lhs = rows_of(0, places(0, 1 - k) + places(0, k)) + rows_of(1, [(x, n) for n in range(4)])
    for b in (0, 1):
        r = product(lhs, b)
        ct[0, b, :64] = r[:64].astype(jnp.bfloat16)
        acc[0, b, :64] = r[64:128]
        acc[3, b] = r[128:]
        to_core(0, b)
    for hf in (0, 1):
        relay(hf, 1, 3, 8)
    for hf in (0, 1):
        relay(hf, 1, 1, 12)
    exchange(0)
    for hf in (0, 1):
        relay(hf, 1, 2, 16)
    multiply(1)
    multiply(2)
    exchange(1)
    exchange(2)
    for hf in (0, 1):
        for a, i in ((0, 4), (3, 8), (1, 12), (2, 16)):
            last(hf, 1, a, i)
    here = (x // 2) == k
    lhs = rows_of(0, places(4, 1 - k) + places(4, k)) + rows_of(1, [((x + 2) % 4, n) for n in range(4)])
    for b in (0, 1):
        r = product(lhs, b)
        ct[4, b, :64] = r[:64].astype(jnp.bfloat16)
        acc[4, b, :64] = r[64:128]
        early, late = acc[3, b], r[128:]
        ct[3, b] = jnp.where(here, late, early).astype(jnp.bfloat16)
        acc[3, b] = jnp.where(here, early, late)
        to_core(3, b)
        to_core(4, b)
    for b in (0, 1):
        exchange(3, (b,))
        exchange(4, (b,))
    for p in range(5):
        n = counts[p]
        for s in (0, 1):
            @pl.when(jnp.logical_not((s == h) & (z == h)))
            def _():
                pltpu.make_async_remote_copy(
                    src_ref=zr.at[s, p, part_of(p)], dst_ref=zr.at[s, p, part_of(p)], send_sem=zs.at[0],
                    recv_sem=zrs.at[s, p * 2 + z], device_id=zdev(h, s), device_id_type=MESH).wait_recv()
        total = (zr[0, p, :n].astype(jnp.float32) + zr[1, p, :n].astype(jnp.float32)).astype(jnp.bfloat16)
        for i, (xx, yy) in enumerate(places(p, k)):
            off = (slot(xx, yy) - 8 * k) * 64 + 32 * pieces[p][0]
            out[pl.ds(pl.multiple_of(off, 32), 32), :] = total[32 * i:32 * i + 32]
    for p in range(5):
        for b in (0, 1):
            @pl.when(jnp.logical_not(mine_at(b)))
            def _():
                pltpu.make_async_remote_copy(
                    src_ref=zt.at[p, b, part_of(p)], dst_ref=zt.at[p, b, part_of(p)], send_sem=zs.at[p * 2 + b],
                    recv_sem=zrs.at[0, 0], device_id=zdev(b, z), device_id_type=MESH).wait_send()
    for cp in outs:
        cp.wait_send()


def project(o, st, w, wlo, whi):
    hbm, vmem = pl.BlockSpec(memory_space=pl.ANY), pl.BlockSpec(memory_space=pltpu.VMEM)
    dma = pltpu.SemaphoreType.DMA
    bf, f32 = jnp.bfloat16, jnp.float32
    wide = HEADS * HD
    return pl.pallas_call(
        project_kernel,
        in_specs=[hbm] * 5,
        out_specs=vmem,
        out_shape=jax.ShapeDtypeStruct((512, 512), bf),
        scratch_shapes=[
            pltpu.VMEM((2, 4, ROWS, wide), bf), pltpu.VMEM((2, 4, ROWS, 128), f32),
            pltpu.VMEM((4, 2, 32, wide), bf), pltpu.VMEM((4, 8, 128), f32),
            pltpu.VMEM((4, 32, wide), bf), pltpu.VMEM((4, 8, 128), f32),
            pltpu.VMEM((32, wide), bf), pltpu.VMEM((8, 128), f32),
            pltpu.VMEM((32, wide), bf), pltpu.VMEM((8, 128), f32),
            pltpu.VMEM((3, 32, wide), bf), pltpu.VMEM((3, 8, 128), f32),
            pltpu.VMEM((4, 32, wide), bf), pltpu.VMEM((4, 8, 128), f32),
            pltpu.VMEM((16, ROWS, wide), bf), pltpu.VMEM((2, 2048, 512), bf),
            pltpu.VMEM((5, 2, 128, 512), bf), pltpu.VMEM((5, 2, 128, 512), bf), pltpu.VMEM((5, 2, 128, 512), f32),
            pltpu.VMEM((5, 2, 128, 512), bf), pltpu.VMEM((2, 5, 128, 512), bf),
            dma((2, 4)), dma((2, 4)), dma((2, 4)), dma((2, 4)), dma((3,)), dma((3,)), dma((2, 4)), dma((2, 4)),
            dma((2, 20)), dma((2, 20)), dma((5, 2)), dma((5, 2)), dma((10,)), dma((2, 10)), dma((5,)),
            pltpu.VMEM((2, 4, 8, 128), f32),
        ],
        compiler_params=pltpu.CompilerParams(collective_id=1, has_side_effects=True, vmem_limit_bytes=53 << 20),
        name="project",
    )(o, st, w, wlo, whi)


def shards(new_queries, new_keys, new_values, cache_keys, cache_values, out_weight, cache_docs, new_docs, slot_tile):
    qg, kvg, wlo, rest = gather(new_queries, cache_keys, cache_values, new_keys, new_values, out_weight)
    whi = lax.ppermute(rest, "ctx", [(i, i ^ 16) for i in range(32)])
    place = jnp.reshape(lax.axis_index("ctx"), (1,)).astype(jnp.int32)
    o, st = attention(qg, kvg.reshape(4 * MEM, HD), cache_docs, new_docs, slot_tile, place)
    return project(o.reshape(2, 4, ROWS, HEADS * HD), st.reshape(6, 4, ROWS, 128), out_weight, wlo, whi)


def solution(mesh):
    return jax.shard_map(
        shards,
        mesh=mesh,
        in_specs=(
            P("ctx", "tp"),
            P("ctx", "tp"),
            P("ctx", "tp"),
            P("ctx", "tp"),
            P("ctx", "tp"),
            P("tp", "ctx"),
            P(),
            P(),
            P(),
        ),
        out_specs=P("tp", "ctx"),
        check_vma=False,
    )
```
